32 devices in a mesh: seg: 4 (over z), lines: 8 (over y, x, core).
Axes of the slice: x: 2, y: 2, z: 4, core: 2. Of those that a mesh axis runs over, the one named last changes fastest.
Arguments:
- left_features: bfloat16 [32, 4096, 128], P('lines', 'seg'), may hold values from -400 to 400
- right_features: bfloat16 [32, 4096, 128], P('lines', 'seg'), may hold values from -6 to 6
- conv_weight: bfloat16 [3, 3, 3, 128, 128], replicated, may hold values from -0.1875 to 0.1875
- conv_bias: float32 [3, 128], replicated, may hold values from -3 to 3
Outputs:
- refined: bfloat16 [32, 4096, 128], P('lines', 'seg')
- disparity: float32 [32, 4096], P('lines', 'seg')
The draws below stay inside these ranges and needn't reach their ends.
All inputs are finite; a program needn't handle non-finite values.
Results may differ from the reference program's by a relative error of at most 0.006.
Values may be sent and summed in bfloat16 or wider, within the bound.
No kernel may reach another device: no remote copies, remote signals or barrier semaphores. Data moves between devices by JAX's collectives and lax.ppermute only.
A program may use at most 128 MiB of HBM per device.

```python
import math
import jax
import jax.numpy as jnp
from jax import lax

C = 128
DISP = 1024
SWEEPS = 2
LAYERS = 3
SEG = 1024
LINES = 32
PIXELS = 4096


def stereo_pair(key):
    base = jax.random.fold_in(key, 7103)
    right_key, left_key = jax.random.split(base, 2)
    shape = (LINES, PIXELS, C)
    right = jnp.clip(jax.random.normal(right_key, shape, jnp.float32), -6.0, 6.0)
    left = jnp.clip(jax.random.normal(left_key, shape, jnp.float32), -6.0, 6.0)
    return (jnp.clip(left, -400.0, 400.0), right)


def draw_left_features(key, part):
    return stereo_pair(key)[0].astype(jnp.bfloat16)


def draw_right_features(key, part):
    return stereo_pair(key)[1].astype(jnp.bfloat16)


def centred(own_key, dims, scale, reach, held_as=jnp.bfloat16):
    entries = scale * jax.random.normal(own_key, dims, jnp.float32)
    return jnp.clip(entries, min=-reach, max=reach).astype(held_as)


def setup_inputs(seed: int = 0) -> dict:
    streams_of = jax.random.split(jax.random.key(seed), 5)
    return {
        "left_features": draw_left_features(jax.random.fold_in(streams_of[4], 71), 0),
        "right_features": draw_right_features(jax.random.fold_in(streams_of[4], 71), 0),
        "conv_weight": centred(streams_of[2], (LAYERS, 3, 3, C, C), (9 * C) ** -0.5, 0.1875),
        "conv_bias": centred(streams_of[3], (LAYERS, C), 0.5, 3.0, jnp.float32),
    }


NEG = -1e+30

def merge_parts(first_part, second_part):
    maxima = jnp.maximum(first_part[0], second_part[0])
    totals = first_part[1] * jnp.exp(first_part[0] - maxima) + second_part[1] * jnp.exp(second_part[0] - maxima)
    return (maxima, totals)

def potentials(maxima, totals):
    live = totals > 0
    return jnp.where(live, -(maxima + jnp.log(jnp.where(live, totals, 1.0))), 0.0)

def band_scores(left_blk, right_win, offset, band_reach, valid_from):
    scores = jnp.einsum('lrc,lkc->lrk', left_blk.astype(jnp.float32), right_win.astype(jnp.float32), precision=lax.Precision.HIGHEST)
    scores = scores * (1.0 / math.sqrt(left_blk.shape[2]))
    row_ids = lax.broadcasted_iota(jnp.int32, scores.shape, 1)
    col_ids = lax.broadcasted_iota(jnp.int32, scores.shape, 2)
    inside = (col_ids > row_ids) & (col_ids <= row_ids + band_reach) & (col_ids + offset >= valid_from)
    return (scores, inside, row_ids, col_ids)

def column_partials(left_side, right_ext, row_pot, band_reach, valid_from, block_rows):
    lines_here, seg_len = (left_side.shape[0], left_side.shape[1])
    window = block_rows + band_reach
    maxima = jnp.full((lines_here, seg_len + band_reach), NEG, jnp.float32)
    totals = jnp.zeros((lines_here, seg_len + band_reach), jnp.float32)
    for offset in range(0, seg_len, block_rows):
        scores, inside, row_ids, col_ids = band_scores(left_side[:, offset:offset + block_rows], right_ext[:, offset:offset + window], offset, band_reach, valid_from)
        shifted = jnp.where(inside, scores + row_pot[:, offset:offset + block_rows, None], NEG)
        block_max = lax.optimization_barrier(jnp.max(shifted, axis=1))
        block_sum = lax.optimization_barrier(jnp.sum(jnp.where(inside, jnp.exp(shifted - block_max[:, None, :]), 0.0), axis=1))
        merged = merge_parts((maxima[:, offset:offset + window], totals[:, offset:offset + window]), (block_max, block_sum))
        maxima = maxima.at[:, offset:offset + window].set(merged[0])
        totals = totals.at[:, offset:offset + window].set(merged[1])
    return (maxima, totals)

def row_potentials(left_side, right_ext, col_pot, band_reach, valid_from, block_rows):
    seg_len = left_side.shape[1]
    window = block_rows + band_reach
    pieces = []
    for offset in range(0, seg_len, block_rows):
        scores, inside, row_ids, col_ids = band_scores(left_side[:, offset:offset + block_rows], right_ext[:, offset:offset + window], offset, band_reach, valid_from)
        shifted = jnp.where(inside, scores + col_pot[:, None, offset:offset + window], NEG)
        row_max = lax.optimization_barrier(jnp.max(shifted, axis=2))
        row_sum = lax.optimization_barrier(jnp.sum(jnp.where(inside, jnp.exp(shifted - row_max[:, :, None]), 0.0), axis=2))
        pieces.append(-(row_max + jnp.log(row_sum)))
    return jnp.concatenate(pieces, axis=1)

def transport(left_side, right_ext, row_pot, col_pot, band_reach, valid_from, block_rows):
    seg_len = left_side.shape[1]
    window = block_rows + band_reach
    matched_parts = []
    disparity_parts = []
    for offset in range(0, seg_len, block_rows):
        right_win = right_ext[:, offset:offset + window]
        scores, inside, row_ids, col_ids = band_scores(left_side[:, offset:offset + block_rows], right_win, offset, band_reach, valid_from)
        weights = jnp.where(inside, jnp.exp(scores + row_pot[:, offset:offset + block_rows, None] + col_pot[:, None, offset:offset + window]), 0.0)
        distance = (row_ids - col_ids + band_reach).astype(jnp.float32)
        disparity_parts.append(lax.optimization_barrier(jnp.sum(weights * distance, axis=2)))
        weights_low = weights.astype(jnp.bfloat16)
        matched_parts.append(jnp.einsum('lrk,lkc->lrc', weights_low.astype(jnp.float32), right_win.astype(jnp.float32), precision=lax.Precision.HIGHEST))
    return (jnp.concatenate(matched_parts, axis=1), jnp.concatenate(disparity_parts, axis=1))

def conv_layer(state, padded, kernel, bias):
    height, width, channels = state.shape
    total = jnp.zeros((height * width, channels), jnp.float32)
    for row_tap in range(3):
        for col_tap in range(3):
            shifted = padded[row_tap:row_tap + height, col_tap:col_tap + width].reshape(height * width, channels)
            total = total + jnp.dot(shifted, kernel[row_tap, col_tap], preferred_element_type=jnp.float32)
    updated = state.astype(jnp.float32) + jax.nn.relu(total.reshape(state.shape) + bias)
    return updated.astype(jnp.bfloat16)

def one_line(line_pair):
    left_side = line_pair[0][None]
    right_side = line_pair[1][None]
    channels = left_side.shape[2]
    block_rows = min(512, SEG)
    right_ext = jnp.concatenate([jnp.zeros((1, DISP, channels), jnp.bfloat16), right_side], axis=1)
    row_pot = jnp.zeros((1, PIXELS), jnp.float32)
    col_pot = jnp.zeros((1, PIXELS + DISP), jnp.float32)
    for sweep_index in range(SWEEPS):
        maxima, totals = column_partials(left_side, right_ext, row_pot, DISP, DISP, block_rows)
        col_pot = potentials(maxima, totals)
        row_pot = row_potentials(left_side, right_ext, col_pot, DISP, DISP, block_rows)
    matched, disparity = transport(left_side, right_ext, row_pot, col_pot, DISP, DISP, block_rows)
    residual = (matched - left_side.astype(jnp.float32)).astype(jnp.bfloat16)
    return (residual[0], disparity[0])

def reference(left_features, right_features, conv_weight, conv_bias):
    residual, disparity = lax.map(one_line, (left_features, right_features))
    state = residual
    for layer in range(LAYERS):
        padded = jnp.pad(state, ((1, 1), (1, 1), (0, 0)))
        state = conv_layer(state, padded, conv_weight[layer], conv_bias[layer])
    return (state, disparity)
```

```python
import functools
import math

import jax
import jax.numpy as jnp
from jax import lax
from jax.experimental import pallas as pl
from jax.experimental.pallas import tpu as pltpu
from jax.sharding import PartitionSpec as P

DISP = 1024
NEG = -1e30
EDGE = 16
VMEM_BYTES = 56 * 1024 * 1024


def shifted(block, axis, step):
    count = lax.axis_size(axis)
    route = [(i, i + step) for i in range(count) if 0 <= i + step < count]
    return lax.ppermute(block, axis, route)


def whole(shape):
    return pl.BlockSpec(shape, lambda l: (0,) * len(shape))


def per_line(shape):
    return pl.BlockSpec((1,) + shape, lambda l: (l,) + (0,) * len(shape))


def params():
    return pltpu.CompilerParams(vmem_limit_bytes=VMEM_BYTES)


def scores_of(left, right):
    return lax.dot_general(
        left, right, (((1,), (1,)), ((), ())), preferred_element_type=jnp.float32
    )


def log2_scale(channels):
    return math.log2(math.e) / math.sqrt(channels)


def column_kernel(own, block, left_ref, right_ref, out_ref):
    line = pl.program_id(0)
    lines_here = out_ref.shape[0] // 2
    seg_len, channels = left_ref.shape[1:]
    scale = log2_scale(channels)
    row_ids = lax.broadcasted_iota(jnp.int32, (block, block), 0)
    col_ids = lax.broadcasted_iota(jnp.int32, (block, block), 1)
    for first in range(0, seg_len, block):
        cols = slice(first, first + block)
        rows = slice(first, seg_len) if own else slice(0, first + block)
        raw = scores_of(left_ref[0, rows], right_ref[0, cols])
        if own:
            edge = jnp.where(col_ids <= row_ids, raw[:block], NEG)
            rest = raw[block:]
        else:
            edge = jnp.where(col_ids > row_ids, raw[first:], NEG)
            rest = raw[:first]
        peak = jnp.max(edge, axis=0, keepdims=True)
        if rest.shape[0]:
            peak = jnp.maximum(peak, jnp.max(rest, axis=0, keepdims=True))
        total = jnp.sum(jnp.exp2((edge - peak) * scale), axis=0, keepdims=True)
        if rest.shape[0]:
            total += jnp.sum(jnp.exp2((rest - peak) * scale), axis=0, keepdims=True)
        out_ref[pl.ds(line, 1), cols] = peak * scale
        out_ref[pl.ds(lines_here + line, 1), cols] = total


def column_partials(own, left, right):
    lines_here, seg_len, channels = left.shape
    block = min(256, seg_len)
    return pl.pallas_call(
        functools.partial(column_kernel, own, block),
        grid=(lines_here,),
        in_specs=[per_line((seg_len, channels))] * 2,
        out_specs=whole((2 * lines_here, seg_len)),
        out_shape=jax.ShapeDtypeStruct((2 * lines_here, seg_len), jnp.float32),
        compiler_params=params(),
        cost_estimate=pl.CostEstimate(
            flops=lines_here * seg_len * seg_len * channels,
            bytes_accessed=4 * lines_here * seg_len * channels,
            transcendentals=lines_here * seg_len * seg_len // 2,
        ),
        name="column_own" if own else "column_prev",
    )(left, right)


def merged_potential(first, second, lines_here):
    first_max = jnp.where(first[lines_here:] > 0, first[:lines_here], NEG)
    second_max = jnp.where(second[lines_here:] > 0, second[:lines_here], NEG)
    peak = jnp.maximum(first_max, second_max)
    total = first[lines_here:] * jnp.exp2(first_max - peak) + second[
        lines_here:
    ] * jnp.exp2(second_max - peak)
    return -(peak + jnp.log2(total))


def row_kernel(
    block,
    left_ref,
    right_ref,
    prev_ref,
    own_ref,
    next_ref,
    before_ref,
    back_ref,
    plan_ref,
    own_out,
    prev_out,
    ext,
    pot,
    sums,
):
    line = pl.program_id(0)
    lines_here = own_out.shape[0]
    seg_len, channels = left_ref.shape[1:]
    scale = log2_scale(channels)

    @pl.when(line == 0)
    def _():
        pot[:, seg_len:] = merged_potential(own_ref[...], next_ref[...], lines_here)
        before = before_ref[...]
        pot[:, :seg_len] = jnp.where(
            before[lines_here:] > 0,
            merged_potential(before, back_ref[...], lines_here),
            NEG,
        )

    ext[:seg_len] = prev_ref[0]
    ext[seg_len:] = right_ref[0]
    sums[...] = jnp.zeros_like(sums)
    row_ids = lax.broadcasted_iota(jnp.int32, (block, block), 0)
    col_ids = lax.broadcasted_iota(jnp.int32, (block, block), 1)
    window = seg_len + block
    col_pot = pot[pl.ds(line, 1), :]
    for index in range(seg_len // block):
        first = index * block
        raw = scores_of(left_ref[0, first : first + block], ext[first : first + window])
        logits = raw * scale + col_pot[:, first : first + window]
        logits = jnp.concatenate(
            [
                jnp.where(col_ids > row_ids, logits[:, :block], NEG),
                logits[:, block:seg_len],
                jnp.where(col_ids <= row_ids, logits[:, seg_len:], NEG),
            ],
            axis=1,
        )
        peak = jnp.max(logits, axis=1, keepdims=True)
        terms = jnp.exp2(logits - peak)
        plan_ref[0, index] = terms.astype(plan_ref.dtype)
        plan = terms * (1.0 / jnp.sum(terms, axis=1, keepdims=True))
        sums[:, first : first + window] += jnp.sum(
            plan.reshape(block // 8, 8, window), axis=0
        )
    totals = jnp.sum(sums[...], axis=0, keepdims=True)
    prev_out[pl.ds(line, 1), :] = totals[:, :seg_len]
    own_out[pl.ds(line, 1), :] = totals[:, seg_len:]


def row_pass(left, right, prev, own, following, before, back, block):
    lines_here, seg_len, channels = left.shape
    window = seg_len + block
    part = (2 * lines_here, seg_len)
    marginal = jax.ShapeDtypeStruct((lines_here, seg_len), jnp.float32)
    return pl.pallas_call(
        functools.partial(row_kernel, block),
        grid=(lines_here,),
        in_specs=[per_line((seg_len, channels))] * 3 + [whole(part)] * 4,
        out_specs=[
            per_line((seg_len // block, block, window)),
            whole((lines_here, seg_len)),
            whole((lines_here, seg_len)),
        ],
        out_shape=[
            jax.ShapeDtypeStruct(
                (lines_here, seg_len // block, block, window), jnp.bfloat16
            ),
            marginal,
            marginal,
        ],
        scratch_shapes=[
            pltpu.VMEM((2 * seg_len, channels), jnp.bfloat16),
            pltpu.VMEM((lines_here, 2 * seg_len), jnp.float32),
            pltpu.VMEM((8, 2 * seg_len), jnp.float32),
        ],
        compiler_params=params(),
        name="row_pass",
    )(left, right, prev, own, following, before, back)


def transport_kernel(
    block,
    plan_ref,
    left_ref,
    right_ref,
    prev_ref,
    own_ref,
    next_ref,
    before_ref,
    back_ref,
    state_ref,
    disp_ref,
    ext,
    gain,
    marks,
):
    line = pl.program_id(0)
    seg_len, channels = left_ref.shape[1:]
    window = seg_len + block

    @pl.when(line == 0)
    def _():
        gain[:, seg_len:] = 1.0 / (own_ref[...] + next_ref[...])
        total = before_ref[...] + back_ref[...]
        gain[:, :seg_len] = jnp.where(
            total > 0, 1.0 / jnp.where(total > 0, total, 1.0), 0.0
        )
        lane = lax.broadcasted_iota(jnp.int32, (window, channels), 1)
        distance = seg_len - lax.broadcasted_iota(jnp.int32, (window, channels), 0)
        low = jnp.bitwise_and(distance, 15)
        values = jnp.where(
            lane == 0,
            1,
            jnp.where(lane == 1, distance - low, jnp.where(lane == 2, low, 0)),
        )
        marks[...] = values.astype(jnp.float32).astype(jnp.bfloat16)

    ext[:seg_len] = prev_ref[0]
    ext[seg_len:] = right_ref[0]
    line_gain = gain[pl.ds(line, 1), :]
    offsets = lax.broadcasted_iota(jnp.int32, (1, block), 1).astype(jnp.float32)
    disparity = []
    for index in range(seg_len // block):
        first = index * block
        rows = slice(first, first + block)
        weights = (
            plan_ref[0, index].astype(jnp.float32)
            * line_gain[:, first : first + window]
        ).astype(jnp.bfloat16)
        table = jnp.concatenate([ext[first : first + window], marks[...]], axis=1)
        result = jnp.dot(weights, table, preferred_element_type=jnp.float32)
        total = result[:, channels : channels + 1]
        matched = result[:, :channels] * (1.0 / total)
        state_ref[0, rows] = (matched - left_ref[0, rows].astype(jnp.float32)).astype(
            state_ref.dtype
        )
        moments = result[:, channels:].T
        disparity.append(offsets + (moments[1:2] + moments[2:3]) / moments[0:1])
    disp_ref[pl.ds(line, 1), :] = jnp.concatenate(disparity, axis=1)


def transport(plan, left, right, prev, own, following, before, back, block):
    lines_here, seg_len, channels = left.shape
    window = seg_len + block
    return pl.pallas_call(
        functools.partial(transport_kernel, block),
        grid=(lines_here,),
        in_specs=[per_line((seg_len // block, block, window))]
        + [per_line((seg_len, channels))] * 3
        + [whole((lines_here, seg_len))] * 4,
        out_specs=[per_line((seg_len, channels)), whole((lines_here, seg_len))],
        out_shape=[
            jax.ShapeDtypeStruct(left.shape, jnp.bfloat16),
            jax.ShapeDtypeStruct((lines_here, seg_len), jnp.float32),
        ],
        scratch_shapes=[
            pltpu.VMEM((2 * seg_len, channels), jnp.bfloat16),
            pltpu.VMEM((lines_here, 2 * seg_len), jnp.float32),
            pltpu.VMEM((window, channels), jnp.bfloat16),
        ],
        compiler_params=params(),
        name="transport",
    )(plan, left, right, prev, own, following, before, back)


def conv_layers(state, top, bottom, left_px, right_px, corners_top, corners_bottom, weight, bias):
    layers = weight.shape[0]
    lines_here, seg_len, channels = state.shape
    middle = jnp.concatenate([top, state, bottom], axis=0)
    before = jnp.concatenate(
        [corners_top[:, EDGE - layers : EDGE], left_px[:, EDGE - layers :], corners_bottom[:, EDGE - layers : EDGE]], axis=0
    )
    after = jnp.concatenate(
        [corners_top[:, EDGE : EDGE + layers], right_px[:, :layers], corners_bottom[:, EDGE : EDGE + layers]], axis=0
    )
    image = jnp.concatenate([before, middle, after], axis=1)
    line0 = lax.axis_index("lines") * lines_here
    px0 = lax.axis_index("seg") * seg_len
    all_lines = lax.axis_size("lines") * lines_here
    all_px = lax.axis_size("seg") * seg_len
    for layer in range(layers):
        reach = layers - 1 - layer
        total = lax.conv_general_dilated(
            image[None],
            weight[layer],
            (1, 1),
            "VALID",
            dimension_numbers=("NHWC", "HWIO", "NHWC"),
            preferred_element_type=jnp.float32,
        )[0]
        updated = image[1:-1, 1:-1].astype(jnp.float32) + jax.nn.relu(total + bias[layer])
        if reach:
            line_ids = line0 - reach + lax.broadcasted_iota(jnp.int32, updated.shape, 0)
            px_ids = px0 - reach + lax.broadcasted_iota(jnp.int32, updated.shape, 1)
            inside = (line_ids >= 0) & (line_ids < all_lines) & (px_ids >= 0) & (px_ids < all_px)
            updated = jnp.where(inside, updated, 0.0)
        image = updated.astype(jnp.bfloat16)
    return image


def shards(left_features, right_features, conv_weight, conv_bias):
    seg_len = left_features.shape[1]
    block = min(128, seg_len)
    layers = conv_weight.shape[0]
    prev = shifted(right_features, "seg", 1)
    own = column_partials(True, left_features, right_features)
    before = shifted(own, "seg", 1)
    back = column_partials(False, left_features, prev)
    following = shifted(back, "seg", -1)
    plan, own, back = row_pass(
        left_features, right_features, prev, own, following, before, back, block
    )
    before = shifted(own, "seg", 1)
    following = shifted(back, "seg", -1)
    state, disparity = transport(
        plan, left_features, right_features, prev, own, following, before, back, block
    )
    bottom = shifted(state[:layers], "lines", -1)
    top = shifted(state[-layers:], "lines", 1)
    left_px = shifted(state[:, -EDGE:], "seg", 1)
    right_px = shifted(state[:, :EDGE], "seg", -1)
    edges = jnp.concatenate([left_px, right_px], axis=1)
    corners_bottom = shifted(edges[:layers], "lines", -1)
    corners_top = shifted(edges[-layers:], "lines", 1)
    refined = conv_layers(
        state, top, bottom, left_px, right_px, corners_top, corners_bottom, conv_weight, conv_bias
    )
    return (refined, disparity)


def solution(mesh):
    return jax.shard_map(
        shards,
        mesh=mesh,
        in_specs=(P("lines", "seg", None), P("lines", "seg", None), P(), P()),
        out_specs=(P("lines", "seg", None), P("lines", "seg")),
        check_vma=False,
    )
```

```python
import functools
import math

import jax
import jax.numpy as jnp
from jax import lax
from jax.experimental import pallas as pl
from jax.experimental.pallas import tpu as pltpu
from jax.sharding import PartitionSpec as P

DISP = 1024
NEG = -1e30
EDGE = 16
VMEM_BYTES = 56 * 1024 * 1024


def shifted(block, axis, step):
    count = lax.axis_size(axis)
    route = [(i, i + step) for i in range(count) if 0 <= i + step < count]
    return lax.ppermute(block, axis, route)


def whole(shape):
    return pl.BlockSpec(shape, lambda l: (0,) * len(shape))


def per_line(shape):
    return pl.BlockSpec((1,) + shape, lambda l: (l,) + (0,) * len(shape))


def params():
    return pltpu.CompilerParams(vmem_limit_bytes=VMEM_BYTES)


def scores_of(left, right):
    return lax.dot_general(
        left, right, (((1,), (1,)), ((), ())), preferred_element_type=jnp.float32
    )


def log2_scale(channels):
    return math.log2(math.e) / math.sqrt(channels)


def column_kernel(own, block, left_ref, right_ref, *refs):
    line = pl.program_id(0)
    out_ref = refs[-1]
    if own:
        weight_ref, stacked_ref, out_ref = refs

        @pl.when(line == 0)
        def _():
            stack_weights(weight_ref, stacked_ref)

    lines_here = out_ref.shape[0] // 2
    seg_len, channels = left_ref.shape[1:]
    scale = log2_scale(channels)
    row_ids = lax.broadcasted_iota(jnp.int32, (block, block), 0)
    col_ids = lax.broadcasted_iota(jnp.int32, (block, block), 1)
    for first in range(0, seg_len, block):
        cols = slice(first, first + block)
        rows = slice(first, seg_len) if own else slice(0, first + block)
        raw = scores_of(left_ref[0, rows], right_ref[0, cols])
        if own:
            edge = jnp.where(col_ids <= row_ids, raw[:block], NEG)
            rest = raw[block:]
        else:
            edge = jnp.where(col_ids > row_ids, raw[first:], NEG)
            rest = raw[:first]
        peak = jnp.max(edge, axis=0, keepdims=True)
        if rest.shape[0]:
            peak = jnp.maximum(peak, jnp.max(rest, axis=0, keepdims=True))
        total = jnp.sum(jnp.exp2((edge - peak) * scale), axis=0, keepdims=True)
        if rest.shape[0]:
            total += jnp.sum(jnp.exp2((rest - peak) * scale), axis=0, keepdims=True)
        out_ref[pl.ds(line, 1), cols] = peak * scale
        out_ref[pl.ds(lines_here + line, 1), cols] = total


def column_partials(left, right, weight=None):
    lines_here, seg_len, channels = left.shape
    block = min(256, seg_len)
    own = weight is not None
    in_specs = [per_line((seg_len, channels))] * 2
    out_specs = [whole((2 * lines_here, seg_len))]
    out_shape = [jax.ShapeDtypeStruct((2 * lines_here, seg_len), jnp.float32)]
    operands = [left, right]
    if own:
        stacked = (weight.shape[0], 12 * channels, 2 * channels)
        in_specs.append(whole(weight.shape))
        out_specs.insert(0, whole(stacked))
        out_shape.insert(0, jax.ShapeDtypeStruct(stacked, weight.dtype))
        operands.append(weight)
    return pl.pallas_call(
        functools.partial(column_kernel, own, block),
        grid=(lines_here,),
        in_specs=in_specs,
        out_specs=out_specs,
        out_shape=out_shape,
        compiler_params=params(),
        cost_estimate=pl.CostEstimate(
            flops=lines_here * seg_len * seg_len * channels,
            bytes_accessed=4 * lines_here * seg_len * channels,
            transcendentals=lines_here * seg_len * seg_len // 2,
        ),
        name="column_own" if own else "column_prev",
    )(*operands)


def merged_potential(first, second, lines_here):
    first_max = jnp.where(first[lines_here:] > 0, first[:lines_here], NEG)
    second_max = jnp.where(second[lines_here:] > 0, second[:lines_here], NEG)
    peak = jnp.maximum(first_max, second_max)
    total = first[lines_here:] * jnp.exp2(first_max - peak) + second[
        lines_here:
    ] * jnp.exp2(second_max - peak)
    return -(peak + jnp.log2(total))


def row_kernel(
    block,
    left_ref,
    right_ref,
    prev_ref,
    own_ref,
    next_ref,
    before_ref,
    back_ref,
    plan_ref,
    own_out,
    prev_out,
    ext,
    pot,
    sums,
):
    line = pl.program_id(0)
    lines_here = own_out.shape[0]
    seg_len, channels = left_ref.shape[1:]
    scale = log2_scale(channels)

    @pl.when(line == 0)
    def _():
        pot[:, seg_len:] = merged_potential(own_ref[...], next_ref[...], lines_here)
        before = before_ref[...]
        pot[:, :seg_len] = jnp.where(
            before[lines_here:] > 0,
            merged_potential(before, back_ref[...], lines_here),
            NEG,
        )

    ext[:seg_len] = prev_ref[0]
    ext[seg_len:] = right_ref[0]
    sums[...] = jnp.zeros_like(sums)
    row_ids = lax.broadcasted_iota(jnp.int32, (block, block), 0)
    col_ids = lax.broadcasted_iota(jnp.int32, (block, block), 1)
    window = seg_len + block
    col_pot = pot[pl.ds(line, 1), :]
    for index in range(seg_len // block):
        first = index * block
        raw = scores_of(left_ref[0, first : first + block], ext[first : first + window])
        logits = raw * scale + col_pot[:, first : first + window]
        logits = jnp.concatenate(
            [
                jnp.where(col_ids > row_ids, logits[:, :block], NEG),
                logits[:, block:seg_len],
                jnp.where(col_ids <= row_ids, logits[:, seg_len:], NEG),
            ],
            axis=1,
        )
        peak = jnp.max(logits, axis=1, keepdims=True)
        terms = jnp.exp2(logits - peak)
        plan_ref[0, index] = terms.astype(plan_ref.dtype)
        plan = terms * (1.0 / jnp.sum(terms, axis=1, keepdims=True))
        sums[:, first : first + window] += jnp.sum(
            plan.reshape(block // 8, 8, window), axis=0
        )
    totals = jnp.sum(sums[...], axis=0, keepdims=True)
    prev_out[pl.ds(line, 1), :] = totals[:, :seg_len]
    own_out[pl.ds(line, 1), :] = totals[:, seg_len:]


def row_pass(left, right, prev, own, following, before, back, block):
    lines_here, seg_len, channels = left.shape
    window = seg_len + block
    part = (2 * lines_here, seg_len)
    marginal = jax.ShapeDtypeStruct((lines_here, seg_len), jnp.float32)
    return pl.pallas_call(
        functools.partial(row_kernel, block),
        grid=(lines_here,),
        in_specs=[per_line((seg_len, channels))] * 3 + [whole(part)] * 4,
        out_specs=[
            per_line((seg_len // block, block, window)),
            whole((lines_here, seg_len)),
            whole((lines_here, seg_len)),
        ],
        out_shape=[
            jax.ShapeDtypeStruct(
                (lines_here, seg_len // block, block, window), jnp.bfloat16
            ),
            marginal,
            marginal,
        ],
        scratch_shapes=[
            pltpu.VMEM((2 * seg_len, channels), jnp.bfloat16),
            pltpu.VMEM((lines_here, 2 * seg_len), jnp.float32),
            pltpu.VMEM((8, 2 * seg_len), jnp.float32),
        ],
        compiler_params=params(),
        name="row_pass",
    )(left, right, prev, own, following, before, back)


def transport_kernel(
    block,
    edge_lines,
    plan_ref,
    left_ref,
    right_ref,
    prev_ref,
    own_ref,
    next_ref,
    before_ref,
    back_ref,
    state_ref,
    disp_ref,
    first_ref,
    last_ref,
    low_ref,
    high_ref,
    ext,
    gain,
    marks,
):
    line = pl.program_id(0)
    layers, lines_here = edge_lines, gain.shape[0]
    seg_len, channels = left_ref.shape[1:]
    window = seg_len + block

    @pl.when(line == 0)
    def _():
        gain[:, seg_len:] = 1.0 / (own_ref[...] + next_ref[...])
        total = before_ref[...] + back_ref[...]
        gain[:, :seg_len] = jnp.where(
            total > 0, 1.0 / jnp.where(total > 0, total, 1.0), 0.0
        )
        lane = lax.broadcasted_iota(jnp.int32, (window, channels), 1)
        distance = seg_len - lax.broadcasted_iota(jnp.int32, (window, channels), 0)
        low = jnp.bitwise_and(distance, 15)
        values = jnp.where(
            lane == 0,
            1,
            jnp.where(lane == 1, distance - low, jnp.where(lane == 2, low, 0)),
        )
        marks[...] = values.astype(jnp.float32).astype(jnp.bfloat16)

    ext[:seg_len] = prev_ref[0]
    ext[seg_len:] = right_ref[0]
    line_gain = gain[pl.ds(line, 1), :]
    offsets = lax.broadcasted_iota(jnp.int32, (1, block), 1).astype(jnp.float32)
    disparity = []
    for index in range(seg_len // block):
        first = index * block
        rows = slice(first, first + block)
        weights = (
            plan_ref[0, index].astype(jnp.float32)
            * line_gain[:, first : first + window]
        ).astype(jnp.bfloat16)
        table = jnp.concatenate([ext[first : first + window], marks[...]], axis=1)
        result = jnp.dot(weights, table, preferred_element_type=jnp.float32)
        total = result[:, channels : channels + 1]
        matched = result[:, :channels] * (1.0 / total)
        state_ref[0, rows] = (matched - left_ref[0, rows].astype(jnp.float32)).astype(
            state_ref.dtype
        )
        moments = result[:, channels:].T
        disparity.append(offsets + (moments[1:2] + moments[2:3]) / moments[0:1])
    disp_ref[pl.ds(line, 1), :] = jnp.concatenate(disparity, axis=1)
    low_ref[...] = state_ref[:, :EDGE]
    high_ref[...] = state_ref[:, seg_len - EDGE :]

    @pl.when(line < layers)
    def _():
        first_ref[...] = state_ref[...]

    @pl.when(line >= lines_here - layers)
    def _():
        last_ref[...] = state_ref[...]


def transport(plan, left, right, prev, own, following, before, back, block, layers):
    lines_here, seg_len, channels = left.shape
    window = seg_len + block
    return pl.pallas_call(
        functools.partial(transport_kernel, block, layers),
        grid=(lines_here,),
        in_specs=[per_line((seg_len // block, block, window))]
        + [per_line((seg_len, channels))] * 3
        + [whole((lines_here, seg_len))] * 4,
        out_specs=[
            per_line((seg_len, channels)),
            whole((lines_here, seg_len)),
            pl.BlockSpec((1, seg_len, channels), lambda l: (jnp.minimum(l, layers - 1), 0, 0)),
            pl.BlockSpec(
                (1, seg_len, channels),
                lambda l: (jnp.maximum(l - (lines_here - layers), 0), 0, 0),
            ),
            per_line((EDGE, channels)),
            per_line((EDGE, channels)),
        ],
        out_shape=[
            jax.ShapeDtypeStruct(left.shape, jnp.bfloat16),
            jax.ShapeDtypeStruct((lines_here, seg_len), jnp.float32),
            jax.ShapeDtypeStruct((layers, seg_len, channels), jnp.bfloat16),
            jax.ShapeDtypeStruct((layers, seg_len, channels), jnp.bfloat16),
            jax.ShapeDtypeStruct((lines_here, EDGE, channels), jnp.bfloat16),
            jax.ShapeDtypeStruct((lines_here, EDGE, channels), jnp.bfloat16),
        ],
        scratch_shapes=[
            pltpu.VMEM((2 * seg_len, channels), jnp.bfloat16),
            pltpu.VMEM((lines_here, 2 * seg_len), jnp.float32),
            pltpu.VMEM((window, channels), jnp.bfloat16),
        ],
        compiler_params=params(),
        name="transport",
    )(plan, left, right, prev, own, following, before, back)


def stack_weights(weight_ref, stacked_ref):
    layers, taps, _, channels, _ = weight_ref.shape
    zeros = jnp.zeros((channels, channels), stacked_ref.dtype)
    for layer in range(layers):
        for col_tap in range(taps):
            for line in range(taps + 1):
                row = (col_tap * (taps + 1) + line) * channels
                for out in range(2):
                    row_tap = line - out
                    stacked_ref[
                        layer, row : row + channels, out * channels : (out + 1) * channels
                    ] = weight_ref[layer, row_tap, col_tap] if 0 <= row_tap < taps else zeros


def conv_kernel(
    state_ref,
    top_ref,
    bottom_ref,
    left_ref,
    right_ref,
    corner_top_ref,
    corner_bottom_ref,
    weight_ref,
    bias_ref,
    out_ref,
    first_image,
    second_image,
):
    lines_here, seg_len, channels = state_ref.shape
    layers = weight_ref.shape[0]
    after = layers + lines_here
    right = EDGE + seg_len
    f32 = jnp.float32
    first_image[:layers, EDGE:right] = top_ref[...].astype(f32)
    first_image[layers:after, EDGE:right] = state_ref[...].astype(f32)
    first_image[after:, EDGE:right] = bottom_ref[...].astype(f32)
    first_image[layers:after, :EDGE] = left_ref[...].astype(f32)
    first_image[layers:after, right:] = right_ref[...].astype(f32)
    for rows, corner_ref in ((slice(0, layers), corner_top_ref), (slice(after, None), corner_bottom_ref)):
        first_image[rows, :EDGE] = corner_ref[:, :EDGE].astype(f32)
        first_image[rows, right:] = corner_ref[:, EDGE:].astype(f32)
    line0 = lax.axis_index("lines") * lines_here - layers
    all_lines = lax.axis_size("lines") * lines_here
    px0 = lax.axis_index("seg") * seg_len - EDGE
    all_px = lax.axis_size("seg") * seg_len
    source, target = first_image, second_image
    for layer in range(layers):
        reach = layers - 1 - layer
        begin, end = (EDGE // 2, right + EDGE // 2) if reach else (EDGE, right)
        pieces = 5 if reach else 4
        size = (end - begin) // pieces

        def pair(index, carry, layer=layer, reach=reach, begin=begin, pieces=pieces, size=size, source=source, target=target):
            base = layer + 2 * index
            for piece in range(pieces):
                start = begin + piece * size
                taps = [
                    source[base + line, start + col_tap - 1 : start + col_tap - 1 + size].astype(jnp.bfloat16)
                    for col_tap in range(3)
                    for line in range(4)
                ]
                total = jnp.dot(
                    jnp.concatenate(taps, axis=1), weight_ref[layer], preferred_element_type=f32
                )
                for out in range(2):
                    line = base + 1 + out
                    part = total[:, out * channels : (out + 1) * channels] + bias_ref[layer : layer + 1]
                    updated = source[line, start : start + size] + jnp.maximum(part, 0.0)
                    if not reach:
                        out_ref[line - layers, start - EDGE : start - EDGE + size] = updated.astype(out_ref.dtype)
                        continue
                    image_line = line0 + line
                    inside = (image_line >= 0) & (image_line < all_lines)
                    if piece in (0, pieces - 1):
                        px = px0 + start + lax.broadcasted_iota(jnp.int32, updated.shape, 0)
                        inside = inside & (px >= 0) & (px < all_px)
                    updated = jnp.where(inside, updated, 0.0)
                    target[line, start : start + size] = updated.astype(jnp.bfloat16).astype(f32)
            return carry

        lax.fori_loop(0, (lines_here + 2 * reach) // 2, pair, 0)
        source, target = target, source


def conv_layers(state, top, bottom, left_px, right_px, corners_top, corners_bottom, weight, bias):
    layers = weight.shape[0]
    lines_here, seg_len, channels = state.shape
    image = pltpu.VMEM((lines_here + 2 * layers, seg_len + 2 * EDGE, channels), jnp.float32)
    return pl.pallas_call(
        conv_kernel,
        in_specs=[pl.BlockSpec(memory_space=pltpu.VMEM)] * 9,
        out_specs=pl.BlockSpec(memory_space=pltpu.VMEM),
        out_shape=jax.ShapeDtypeStruct(state.shape, state.dtype),
        scratch_shapes=[image, image],
        compiler_params=params(),
        name="conv_layers",
    )(state, top, bottom, left_px, right_px, corners_top, corners_bottom, weight, bias)


def shards(left_features, right_features, conv_weight, conv_bias):
    seg_len = left_features.shape[1]
    block = min(128, seg_len)
    layers = conv_weight.shape[0]
    prev = shifted(right_features, "seg", 1)
    stacked, own = column_partials(left_features, right_features, conv_weight)
    before = shifted(own, "seg", 1)
    (back,) = column_partials(left_features, prev)
    following = shifted(back, "seg", -1)
    plan, own, back = row_pass(
        left_features, right_features, prev, own, following, before, back, block
    )
    before = shifted(own, "seg", 1)
    following = shifted(back, "seg", -1)
    state, disparity, first, last, low, high = transport(
        plan, left_features, right_features, prev, own, following, before, back, block, layers
    )
    bottom = shifted(first, "lines", -1)
    top = shifted(last, "lines", 1)
    left_px = shifted(high, "seg", 1)
    right_px = shifted(low, "seg", -1)
    edges = jnp.concatenate([left_px, right_px], axis=1)
    corners_bottom = shifted(edges[:layers], "lines", -1)
    corners_top = shifted(edges[-layers:], "lines", 1)
    refined = conv_layers(
        state, top, bottom, left_px, right_px, corners_top, corners_bottom, stacked, conv_bias
    )
    return (refined, disparity)


def solution(mesh):
    return jax.shard_map(
        shards,
        mesh=mesh,
        in_specs=(P("lines", "seg", None), P("lines", "seg", None), P(), P()),
        out_specs=(P("lines", "seg", None), P("lines", "seg")),
        check_vma=False,
    )
```

```python
import functools
import math

import jax
import jax.numpy as jnp
from jax import lax
from jax.experimental import pallas as pl
from jax.experimental.pallas import tpu as pltpu
from jax.sharding import PartitionSpec as P

DISP = 1024
NEG = -1e30
EDGE = 16
VMEM_BYTES = 56 * 1024 * 1024


def shifted(block, axis, step):
    count = lax.axis_size(axis)
    route = [(i, i + step) for i in range(count) if 0 <= i + step < count]
    return lax.ppermute(block, axis, route)


def whole(shape):
    return pl.BlockSpec(shape, lambda l: (0,) * len(shape))


def per_line(shape):
    return pl.BlockSpec((1,) + shape, lambda l: (l,) + (0,) * len(shape))


def params():
    return pltpu.CompilerParams(vmem_limit_bytes=VMEM_BYTES)


def scores_of(left, right):
    return lax.dot_general(
        left, right, (((1,), (1,)), ((), ())), preferred_element_type=jnp.float32
    )


def log2_scale(channels):
    return math.log2(math.e) / math.sqrt(channels)


def over_rows(reduce, values, chains=64):
    count, width = values.shape
    while count > chains >= 8 and count % chains == 0:
        values = reduce(values.reshape(count // chains, chains, width), axis=0)
        count, chains = chains, chains // 8
    return reduce(values, axis=0, keepdims=True)


def column_block(left, right, diagonal_first):
    block, channels = right.shape
    scale = log2_scale(channels)
    raw = scores_of(left, right)
    row_ids = lax.broadcasted_iota(jnp.int32, (block, block), 0)
    col_ids = lax.broadcasted_iota(jnp.int32, (block, block), 1)
    if diagonal_first:
        parts = [jnp.where(col_ids <= row_ids, raw[:block], NEG), raw[block:]]
    else:
        parts = [raw[:-block], jnp.where(col_ids > row_ids, raw[-block:], NEG)]
    parts = [part for part in parts if part.shape[0]]
    peak = functools.reduce(jnp.maximum, [over_rows(jnp.max, part) for part in parts])
    total = sum(over_rows(jnp.sum, jnp.exp2((part - peak) * scale)) for part in parts)
    return (peak * scale, total)


def own_kernel(block, left_ref, right_ref, weight_ref, stacked_ref, out_ref):
    line = pl.program_id(0)
    lines_here = out_ref.shape[0] // 2
    seg_len = left_ref.shape[1]

    @pl.when(line == 0)
    def _():
        stack_weights(weight_ref, stacked_ref)

    for first in range(0, seg_len, block):
        cols = slice(first, first + block)
        peak, total = column_block(left_ref[0, first:], right_ref[0, cols], True)
        out_ref[pl.ds(line, 1), cols] = peak
        out_ref[pl.ds(lines_here + line, 1), cols] = total


def own_partials(left, right, weight):
    lines_here, seg_len, channels = left.shape
    stacked = (weight.shape[0], 12 * channels, 2 * channels)
    part = (2 * lines_here, seg_len)
    return pl.pallas_call(
        functools.partial(own_kernel, min(256, seg_len)),
        grid=(lines_here,),
        in_specs=[per_line((seg_len, channels))] * 2 + [whole(weight.shape)],
        out_specs=[whole(stacked), whole(part)],
        out_shape=[
            jax.ShapeDtypeStruct(stacked, weight.dtype),
            jax.ShapeDtypeStruct(part, jnp.float32),
        ],
        compiler_params=params(),
        cost_estimate=pl.CostEstimate(
            flops=2 * lines_here * seg_len * seg_len * channels,
            bytes_accessed=8 * lines_here * seg_len * channels,
            transcendentals=lines_here * seg_len * seg_len // 2,
        ),
        name="column_own",
    )(left, right, weight)


def cross_kernel(block, left_ref, prev_ref, next_ref, right_ref, own_ref, merged_ref, back_ref):
    line = pl.program_id(0)
    lines_here = own_ref.shape[0] // 2
    half = next_ref.shape[1]
    last = lax.axis_index("seg") == lax.axis_size("seg") - 1
    top, bottom = pl.ds(line, 1), pl.ds(lines_here + line, 1)
    for first in range(0, prev_ref.shape[1], block):
        cols = slice(first, first + block)
        peak, total = column_block(
            left_ref[0, : half + first + block], prev_ref[0, cols], False
        )
        back_ref[top, cols] = peak
        back_ref[bottom, cols] = total
    for first in range(0, half, block):
        cols = slice(first, first + block)
        peak, total = column_block(next_ref[0, : first + block], right_ref[0, cols], False)
        peak = jnp.where(last, NEG, peak)
        total = jnp.where(last, 0.0, total)
        own_peak = own_ref[top, cols]
        merged = jnp.maximum(own_peak, peak)
        merged_ref[top, cols] = merged
        merged_ref[bottom, cols] = own_ref[bottom, cols] * jnp.exp2(
            own_peak - merged
        ) + total * jnp.exp2(peak - merged)
    merged_ref[top, half:] = own_ref[top, half:]
    merged_ref[bottom, half:] = own_ref[bottom, half:]


def cross_partials(left, prev_high, next_low, right, own):
    lines_here, seg_len, channels = left.shape
    half = next_low.shape[1]
    back = (2 * lines_here, seg_len - half)
    return pl.pallas_call(
        functools.partial(cross_kernel, min(256, half)),
        grid=(lines_here,),
        in_specs=[
            per_line((seg_len, channels)),
            per_line((seg_len - half, channels)),
            per_line((half, channels)),
            per_line((seg_len, channels)),
            whole(own.shape),
        ],
        out_specs=[whole(own.shape), whole(back)],
        out_shape=[
            jax.ShapeDtypeStruct(own.shape, jnp.float32),
            jax.ShapeDtypeStruct(back, jnp.float32),
        ],
        compiler_params=params(),
        cost_estimate=pl.CostEstimate(
            flops=2 * lines_here * seg_len * seg_len * channels,
            bytes_accessed=8 * lines_here * seg_len * channels,
            transcendentals=lines_here * seg_len * seg_len // 2,
        ),
        name="column_cross",
    )(left, prev_high, next_low, right, own)


def potential(peak, total):
    return -(peak + jnp.log2(total))


def merged_potential(first, second):
    first_max = jnp.where(first[1] > 0, first[0], NEG)
    second_max = jnp.where(second[1] > 0, second[0], NEG)
    peak = jnp.maximum(first_max, second_max)
    total = first[1] * jnp.exp2(first_max - peak) + second[1] * jnp.exp2(second_max - peak)
    return potential(peak, total)


def row_kernel(
    block,
    left_ref,
    right_ref,
    prev_low_ref,
    prev_high_ref,
    own_ref,
    next_ref,
    before_ref,
    back_ref,
    plan_ref,
    own_out,
    prev_out,
    ext,
    pot,
    sums,
    raw,
):
    line = pl.program_id(0)
    lines_here = own_out.shape[0]
    seg_len, channels = left_ref.shape[1:]
    half = prev_low_ref.shape[1]
    scale = log2_scale(channels)

    @pl.when(line == 0)
    def _():
        def parts(ref, start, stop):
            return ref[:lines_here, start:stop], ref[lines_here:, start:stop]

        rest = seg_len - half
        pot[:, seg_len : seg_len + half] = potential(*parts(own_ref, 0, half))
        pot[:, seg_len + half :] = merged_potential(
            parts(own_ref, half, seg_len), parts(next_ref, 0, rest)
        )
        low = parts(before_ref, 0, half)
        high = parts(before_ref, half, seg_len)
        pot[:, :half] = jnp.where(low[1] > 0, potential(*low), NEG)
        pot[:, half:seg_len] = jnp.where(
            high[1] > 0, merged_potential(high, parts(back_ref, 0, rest)), NEG
        )

    ext[:half] = prev_low_ref[0]
    ext[half:seg_len] = prev_high_ref[0]
    ext[seg_len:] = right_ref[0]
    sums[...] = jnp.zeros_like(sums)
    window = seg_len + block
    big = 2 * block
    strip = 16
    col_ids = lax.broadcasted_iota(jnp.int32, (strip, block), 1)
    row_ids = lax.broadcasted_iota(jnp.int32, (strip, block), 0)
    col_pot = pot[pl.ds(line, 1), :]
    corner = jnp.zeros((block, block), plan_ref.dtype)
    for index in range(seg_len // big):
        start = index * big
        slot = index % 2
        raw[slot] = scores_of(
            left_ref[0, start : start + big], ext[start : start + seg_len + big]
        )
        plan_ref[0, index, :block, window:] = corner
        plan_ref[0, index, block:, :block] = corner
        for side in range(2):
            shift = side * block
            first = start + shift
            window_pot = col_pot[:, first : first + window]
            column_sum = jnp.zeros((8, window), jnp.float32)
            for row in range(0, block, strip):
                rows = slice(shift + row, shift + row + strip)
                logits = raw[slot, rows, shift : shift + window] * scale + window_pot
                logits = jnp.concatenate(
                    [
                        jnp.where(col_ids > row_ids + row, logits[:, :block], NEG),
                        logits[:, block:seg_len],
                        jnp.where(col_ids <= row_ids + row, logits[:, seg_len:], NEG),
                    ],
                    axis=1,
                )
                peak = jnp.max(logits, axis=1, keepdims=True)
                terms = jnp.exp2(logits - peak)
                plan_ref[0, index, rows, shift : shift + window] = terms.astype(plan_ref.dtype)
                plan = terms * (1.0 / jnp.sum(terms, axis=1, keepdims=True))
                column_sum += plan[:8] + plan[8:]
            sums[:, first : first + window] += column_sum
    totals = jnp.sum(sums[...], axis=0, keepdims=True)
    prev_out[pl.ds(line, 1), :] = totals[:, :seg_len]
    own_out[pl.ds(line, 1), :] = totals[:, seg_len:]


def plan_shape(seg_len, block):
    return (seg_len // (2 * block), 2 * block, seg_len + 2 * block)


def row_pass(left, right, prev_low, prev_high, own, following, before, back, block):
    lines_here, seg_len, channels = left.shape
    half = prev_low.shape[1]
    marginal = jax.ShapeDtypeStruct((lines_here, seg_len), jnp.float32)
    plan = plan_shape(seg_len, block)
    return pl.pallas_call(
        functools.partial(row_kernel, block),
        grid=(lines_here,),
        in_specs=[per_line((seg_len, channels))] * 2
        + [per_line((half, channels)), per_line((seg_len - half, channels))]
        + [whole(part.shape) for part in (own, following, before, back)],
        out_specs=[
            per_line(plan),
            whole((lines_here, seg_len)),
            whole((lines_here, seg_len)),
        ],
        out_shape=[
            jax.ShapeDtypeStruct((lines_here,) + plan, jnp.bfloat16),
            marginal,
            marginal,
        ],
        scratch_shapes=[
            pltpu.VMEM((2 * seg_len, channels), jnp.bfloat16),
            pltpu.VMEM((lines_here, 2 * seg_len), jnp.float32),
            pltpu.VMEM((8, 2 * seg_len), jnp.float32),
            pltpu.VMEM((2, 2 * block, seg_len + 2 * block), jnp.float32),
        ],
        compiler_params=params(),
        name="row_pass",
    )(left, right, prev_low, prev_high, own, following, before, back)


def transport_kernel(
    block,
    layers,
    plan_ref,
    left_ref,
    right_ref,
    prev_low_ref,
    prev_high_ref,
    own_ref,
    next_ref,
    before_ref,
    back_ref,
    state_ref,
    disp_ref,
    first_ref,
    last_ref,
    low_ref,
    high_ref,
    ext,
    gain,
    marks,
):
    line = pl.program_id(0)
    lines_here = gain.shape[0]
    seg_len, channels = left_ref.shape[1:]
    half = prev_low_ref.shape[1]
    window = seg_len + block

    @pl.when(line == 0)
    def _():
        gain[:, seg_len:] = 1.0 / (own_ref[...] + next_ref[...])
        total = before_ref[...] + back_ref[...]
        gain[:, :seg_len] = jnp.where(
            total > 0, 1.0 / jnp.where(total > 0, total, 1.0), 0.0
        )
        lane = lax.broadcasted_iota(jnp.int32, (window, channels), 1)
        distance = seg_len - lax.broadcasted_iota(jnp.int32, (window, channels), 0)
        low = jnp.bitwise_and(distance, 15)
        values = jnp.where(
            lane == 0,
            1,
            jnp.where(lane == 1, distance - low, jnp.where(lane == 2, low, 0)),
        )
        marks[...] = values.astype(jnp.float32).astype(jnp.bfloat16)

    ext[:half] = prev_low_ref[0]
    ext[half:seg_len] = prev_high_ref[0]
    ext[seg_len:] = right_ref[0]
    line_gain = gain[pl.ds(line, 1), :]
    offsets = lax.broadcasted_iota(jnp.int32, (1, block), 1).astype(jnp.float32)
    disparity = []
    for index in range(seg_len // block):
        first = index * block
        rows = slice(first, first + block)
        weights = (
            plan_ref[0, index].astype(jnp.float32)
            * line_gain[:, first : first + window]
        ).astype(jnp.bfloat16)
        table = jnp.concatenate([ext[first : first + window], marks[...]], axis=1)
        result = jnp.dot(weights, table, preferred_element_type=jnp.float32)
        matched = result[:, :channels] * (1.0 / result[:, channels : channels + 1])
        state_ref[0, rows] = (matched - left_ref[0, rows].astype(jnp.float32)).astype(
            state_ref.dtype
        )
        moments = result[:, channels:].T
        disparity.append(offsets + (moments[1:2] + moments[2:3]) / moments[0:1])
    disp_ref[pl.ds(line, 1), :] = jnp.concatenate(disparity, axis=1)
    low_ref[...] = state_ref[:, :EDGE]
    high_ref[...] = state_ref[:, seg_len - EDGE :]

    @pl.when(line < layers)
    def _():
        first_ref[...] = state_ref[...]

    @pl.when(line >= lines_here - layers)
    def _():
        last_ref[...] = state_ref[...]


def transport(plan, left, right, prev_low, prev_high, own, following, before, back, layers):
    lines_here, seg_len, channels = left.shape
    half = prev_low.shape[1]
    block = plan.shape[2]
    edge = jax.ShapeDtypeStruct((layers, seg_len, channels), jnp.bfloat16)
    side = jax.ShapeDtypeStruct((lines_here, EDGE, channels), jnp.bfloat16)
    return pl.pallas_call(
        functools.partial(transport_kernel, block, layers),
        grid=(lines_here,),
        in_specs=[per_line(plan.shape[1:])]
        + [per_line((seg_len, channels))] * 2
        + [per_line((half, channels)), per_line((seg_len - half, channels))]
        + [whole((lines_here, seg_len))] * 4,
        out_specs=[
            per_line((seg_len, channels)),
            whole((lines_here, seg_len)),
            pl.BlockSpec((1, seg_len, channels), lambda l: (jnp.minimum(l, layers - 1), 0, 0)),
            pl.BlockSpec(
                (1, seg_len, channels),
                lambda l: (jnp.maximum(l - (lines_here - layers), 0), 0, 0),
            ),
            per_line((EDGE, channels)),
            per_line((EDGE, channels)),
        ],
        out_shape=[
            jax.ShapeDtypeStruct(left.shape, jnp.bfloat16),
            jax.ShapeDtypeStruct((lines_here, seg_len), jnp.float32),
            edge,
            edge,
            side,
            side,
        ],
        scratch_shapes=[
            pltpu.VMEM((2 * seg_len, channels), jnp.bfloat16),
            pltpu.VMEM((lines_here, 2 * seg_len), jnp.float32),
            pltpu.VMEM((seg_len + block, channels), jnp.bfloat16),
        ],
        compiler_params=params(),
        name="transport",
    )(plan, left, right, prev_low, prev_high, own, following, before, back)


def stack_weights(weight_ref, stacked_ref):
    layers, taps, _, channels, _ = weight_ref.shape
    zeros = jnp.zeros((channels, channels), stacked_ref.dtype)
    for layer in range(layers):
        for col_tap in range(taps):
            for line in range(taps + 1):
                row = (col_tap * (taps + 1) + line) * channels
                for out in range(2):
                    row_tap = line - out
                    stacked_ref[
                        layer, row : row + channels, out * channels : (out + 1) * channels
                    ] = weight_ref[layer, row_tap, col_tap] if 0 <= row_tap < taps else zeros


def conv_kernel(
    state_ref,
    top_ref,
    bottom_ref,
    left_ref,
    right_ref,
    corner_top_ref,
    corner_bottom_ref,
    weight_ref,
    bias_ref,
    out_ref,
    first_image,
    second_image,
):
    lines_here, seg_len, channels = state_ref.shape
    layers = weight_ref.shape[0]
    after = layers + lines_here
    right = EDGE + seg_len
    f32 = jnp.float32
    first_image[:layers, EDGE:right] = top_ref[...].astype(f32)
    first_image[layers:after, EDGE:right] = state_ref[...].astype(f32)
    first_image[after:, EDGE:right] = bottom_ref[...].astype(f32)
    first_image[layers:after, :EDGE] = left_ref[...].astype(f32)
    first_image[layers:after, right:] = right_ref[...].astype(f32)
    for rows, corner_ref in ((slice(0, layers), corner_top_ref), (slice(after, None), corner_bottom_ref)):
        first_image[rows, :EDGE] = corner_ref[:, :EDGE].astype(f32)
        first_image[rows, right:] = corner_ref[:, EDGE:].astype(f32)
    line0 = lax.axis_index("lines") * lines_here - layers
    all_lines = lax.axis_size("lines") * lines_here
    px0 = lax.axis_index("seg") * seg_len - EDGE
    all_px = lax.axis_size("seg") * seg_len
    source, target = first_image, second_image
    for layer in range(layers):
        reach = layers - 1 - layer
        begin, end = (EDGE // 2, right + EDGE // 2) if reach else (EDGE, right)
        pieces = 5 if reach else 4
        size = (end - begin) // pieces

        def pair(index, carry, layer=layer, reach=reach, begin=begin, pieces=pieces, size=size, source=source, target=target):
            base = layer + 2 * index
            for piece in range(pieces):
                start = begin + piece * size
                taps = [
                    source[base + line, start + col_tap - 1 : start + col_tap - 1 + size].astype(jnp.bfloat16)
                    for col_tap in range(3)
                    for line in range(4)
                ]
                total = jnp.dot(
                    jnp.concatenate(taps, axis=1), weight_ref[layer], preferred_element_type=f32
                )
                for out in range(2):
                    line = base + 1 + out
                    part = total[:, out * channels : (out + 1) * channels] + bias_ref[layer : layer + 1]
                    updated = source[line, start : start + size] + jnp.maximum(part, 0.0)
                    if not reach:
                        out_ref[line - layers, start - EDGE : start - EDGE + size] = updated.astype(out_ref.dtype)
                        continue
                    image_line = line0 + line
                    inside = (image_line >= 0) & (image_line < all_lines)
                    if piece in (0, pieces - 1):
                        px = px0 + start + lax.broadcasted_iota(jnp.int32, updated.shape, 0)
                        inside = inside & (px >= 0) & (px < all_px)
                    updated = jnp.where(inside, updated, 0.0)
                    target[line, start : start + size] = updated.astype(jnp.bfloat16).astype(f32)
            return carry

        lax.fori_loop(0, (lines_here + 2 * reach) // 2, pair, 0)
        source, target = target, source


def conv_layers(state, top, bottom, left_px, right_px, corners_top, corners_bottom, weight, bias):
    layers = weight.shape[0]
    lines_here, seg_len, channels = state.shape
    image = pltpu.VMEM((lines_here + 2 * layers, seg_len + 2 * EDGE, channels), jnp.float32)
    return pl.pallas_call(
        conv_kernel,
        in_specs=[pl.BlockSpec(memory_space=pltpu.VMEM)] * 9,
        out_specs=pl.BlockSpec(memory_space=pltpu.VMEM),
        out_shape=jax.ShapeDtypeStruct(state.shape, state.dtype),
        scratch_shapes=[image, image],
        compiler_params=params(),
        name="conv_layers",
    )(state, top, bottom, left_px, right_px, corners_top, corners_bottom, weight, bias)


def shards(left_features, right_features, conv_weight, conv_bias):
    seg_len = left_features.shape[1]
    half = seg_len // 2
    layers = conv_weight.shape[0]
    prev_high = shifted(right_features[:, half:], "seg", 1)
    next_low = shifted(left_features[:, :half], "seg", -1)
    prev_low = shifted(right_features[:, :half], "seg", 1)
    stacked, own = own_partials(left_features, right_features, conv_weight)
    own, back = cross_partials(left_features, prev_high, next_low, right_features, own)
    before = shifted(own, "seg", 1)
    following = shifted(back, "seg", -1)
    plan, own, back = row_pass(
        left_features, right_features, prev_low, prev_high, own, following, before, back, min(128, half)
    )
    before = shifted(own, "seg", 1)
    following = shifted(back, "seg", -1)
    state, disparity, first, last, low, high = transport(
        plan, left_features, right_features, prev_low, prev_high, own, following, before, back, layers
    )
    bottom = shifted(first, "lines", -1)
    top = shifted(last, "lines", 1)
    left_px = shifted(high, "seg", 1)
    right_px = shifted(low, "seg", -1)
    edges = jnp.concatenate([left_px, right_px], axis=1)
    corners_bottom = shifted(edges[:layers], "lines", -1)
    corners_top = shifted(edges[-layers:], "lines", 1)
    refined = conv_layers(
        state, top, bottom, left_px, right_px, corners_top, corners_bottom, stacked, conv_bias
    )
    return (refined, disparity)


def solution(mesh):
    return jax.shard_map(
        shards,
        mesh=mesh,
        in_specs=(P("lines", "seg", None), P("lines", "seg", None), P(), P()),
        out_specs=(P("lines", "seg", None), P("lines", "seg")),
        check_vma=False,
    )
```

```python
import functools
import math

import jax
import jax.numpy as jnp
from jax import lax
from jax.experimental import pallas as pl
from jax.experimental.pallas import tpu as pltpu
from jax.sharding import PartitionSpec as P

DISP = 1024
NEG = -1e30
EDGE = 16
VMEM_BYTES = 56 * 1024 * 1024


def shifted(block, axis, step):
    count = lax.axis_size(axis)
    route = [(i, i + step) for i in range(count) if 0 <= i + step < count]
    return lax.ppermute(block, axis, route)


def whole(shape):
    return pl.BlockSpec(shape, lambda l: (0,) * len(shape))


def per_line(shape):
    return pl.BlockSpec((1,) + shape, lambda l: (l,) + (0,) * len(shape))


def params():
    return pltpu.CompilerParams(vmem_limit_bytes=VMEM_BYTES)


def scores_of(left, right):
    return lax.dot_general(
        left, right, (((1,), (1,)), ((), ())), preferred_element_type=jnp.float32
    )


def log2_scale(channels):
    return math.log2(math.e) / math.sqrt(channels)


def over_rows(reduce, values, chains=64):
    count, width = values.shape
    while count > chains >= 8 and count % chains == 0:
        values = reduce(values.reshape(count // chains, chains, width), axis=0)
        count, chains = chains, chains // 8
    return reduce(values, axis=0, keepdims=True)


def column_block(left, right, diagonal_first):
    block, channels = right.shape
    scale = log2_scale(channels)
    raw = scores_of(left, right)
    row_ids = lax.broadcasted_iota(jnp.int32, (block, block), 0)
    col_ids = lax.broadcasted_iota(jnp.int32, (block, block), 1)
    if diagonal_first:
        parts = [jnp.where(col_ids <= row_ids, raw[:block], NEG), raw[block:]]
    else:
        parts = [raw[:-block], jnp.where(col_ids > row_ids, raw[-block:], NEG)]
    parts = [part for part in parts if part.shape[0]]
    peak = functools.reduce(jnp.maximum, [over_rows(jnp.max, part) for part in parts])
    total = sum(over_rows(jnp.sum, jnp.exp2((part - peak) * scale)) for part in parts)
    return (peak * scale, total)


def own_kernel(block, left_ref, right_ref, weight_ref, stacked_ref, out_ref):
    line = pl.program_id(0)
    lines_here = out_ref.shape[0] // 2
    seg_len = left_ref.shape[1]

    @pl.when(line == 0)
    def _():
        stack_weights(weight_ref, stacked_ref)

    for first in range(0, seg_len, block):
        cols = slice(first, first + block)
        peak, total = column_block(left_ref[0, first:], right_ref[0, cols], True)
        out_ref[pl.ds(line, 1), cols] = peak
        out_ref[pl.ds(lines_here + line, 1), cols] = total


def own_partials(left, right, weight):
    lines_here, seg_len, channels = left.shape
    stacked = (weight.shape[0], 12 * channels, 2 * channels)
    part = (2 * lines_here, seg_len)
    return pl.pallas_call(
        functools.partial(own_kernel, min(256, seg_len)),
        grid=(lines_here,),
        in_specs=[per_line((seg_len, channels))] * 2 + [whole(weight.shape)],
        out_specs=[whole(stacked), whole(part)],
        out_shape=[
            jax.ShapeDtypeStruct(stacked, weight.dtype),
            jax.ShapeDtypeStruct(part, jnp.float32),
        ],
        compiler_params=params(),
        cost_estimate=pl.CostEstimate(
            flops=2 * lines_here * seg_len * seg_len * channels,
            bytes_accessed=8 * lines_here * seg_len * channels,
            transcendentals=lines_here * seg_len * seg_len // 2,
        ),
        name="column_own",
    )(left, right, weight)


def cross_kernel(block, left_ref, prev_ref, next_ref, right_ref, own_ref, merged_ref, back_ref):
    line = pl.program_id(0)
    lines_here = own_ref.shape[0] // 2
    half = next_ref.shape[1]
    last = lax.axis_index("seg") == lax.axis_size("seg") - 1
    top, bottom = pl.ds(line, 1), pl.ds(lines_here + line, 1)
    for first in range(0, prev_ref.shape[1], block):
        cols = slice(first, first + block)
        peak, total = column_block(
            left_ref[0, : half + first + block], prev_ref[0, cols], False
        )
        back_ref[top, cols] = peak
        back_ref[bottom, cols] = total
    for first in range(0, half, block):
        cols = slice(first, first + block)
        peak, total = column_block(next_ref[0, : first + block], right_ref[0, cols], False)
        peak = jnp.where(last, NEG, peak)
        total = jnp.where(last, 0.0, total)
        own_peak = own_ref[top, cols]
        merged = jnp.maximum(own_peak, peak)
        merged_ref[top, cols] = merged
        merged_ref[bottom, cols] = own_ref[bottom, cols] * jnp.exp2(
            own_peak - merged
        ) + total * jnp.exp2(peak - merged)
    merged_ref[top, half:] = own_ref[top, half:]
    merged_ref[bottom, half:] = own_ref[bottom, half:]


def cross_partials(left, prev_high, next_low, right, own):
    lines_here, seg_len, channels = left.shape
    half = next_low.shape[1]
    back = (2 * lines_here, seg_len - half)
    return pl.pallas_call(
        functools.partial(cross_kernel, min(256, half)),
        grid=(lines_here,),
        in_specs=[
            per_line((seg_len, channels)),
            per_line((seg_len - half, channels)),
            per_line((half, channels)),
            per_line((seg_len, channels)),
            whole(own.shape),
        ],
        out_specs=[whole(own.shape), whole(back)],
        out_shape=[
            jax.ShapeDtypeStruct(own.shape, jnp.float32),
            jax.ShapeDtypeStruct(back, jnp.float32),
        ],
        compiler_params=params(),
        cost_estimate=pl.CostEstimate(
            flops=2 * lines_here * seg_len * seg_len * channels,
            bytes_accessed=8 * lines_here * seg_len * channels,
            transcendentals=lines_here * seg_len * seg_len // 2,
        ),
        name="column_cross",
    )(left, prev_high, next_low, right, own)


def potential(peak, total):
    return -(peak + jnp.log2(total))


def merged_potential(first, second):
    first_max = jnp.where(first[1] > 0, first[0], NEG)
    second_max = jnp.where(second[1] > 0, second[0], NEG)
    peak = jnp.maximum(first_max, second_max)
    total = first[1] * jnp.exp2(first_max - peak) + second[1] * jnp.exp2(second_max - peak)
    return potential(peak, total)


def split(values, parts):
    pieces = []
    for _ in range(parts):
        piece = values.astype(jnp.bfloat16).astype(jnp.float32)
        pieces.append(piece)
        values = values - piece
    return pieces


SHIFT = 2


def potential_lanes(pot, channels):
    lines_here, count = pot.shape
    parts = split(pot, 3)
    filler = jnp.zeros((channels - 3 * lines_here, count), jnp.float32)
    lanes = jnp.concatenate(parts + [filler], axis=0).T
    lane = lax.broadcasted_iota(jnp.int32, lanes.shape, 1)
    return jnp.where(lane >= channels - SHIFT, -1.0, lanes).astype(jnp.bfloat16)


def line_lanes(line, lines_here, shape):
    lane = lax.broadcasted_iota(jnp.int32, shape, 1)
    mine = jnp.zeros(shape, jnp.float32)
    for part in range(3):
        mine = jnp.where(lane == part * lines_here + line, 1.0, mine)
    return mine


def banded(values, row, block):
    rows, window = values.shape
    col_ids = lax.broadcasted_iota(jnp.int32, (rows, block), 1)
    row_ids = lax.broadcasted_iota(jnp.int32, (rows, block), 0) + row
    return jnp.concatenate(
        [
            jnp.where(col_ids > row_ids, values[:, :block], NEG),
            values[:, block : window - block],
            jnp.where(col_ids <= row_ids, values[:, window - block :], NEG),
        ],
        axis=1,
    )


def row_kernel(
    block,
    left_ref,
    right_ref,
    prev_low_ref,
    prev_high_ref,
    own_ref,
    next_ref,
    before_ref,
    back_ref,
    pot,
    lanes_ref,
    own_out,
    prev_out,
    ext,
    sums,
    raw,
):
    line = pl.program_id(0)
    lines_here = own_out.shape[0]
    seg_len, channels = left_ref.shape[1:]
    half = prev_low_ref.shape[1]
    scale = log2_scale(channels)

    @pl.when(line == 0)
    def _():
        def parts(ref, start, stop):
            return ref[:lines_here, start:stop], ref[lines_here:, start:stop]

        rest = seg_len - half
        pot[:, seg_len : seg_len + half] = potential(*parts(own_ref, 0, half))
        pot[:, seg_len + half :] = merged_potential(
            parts(own_ref, half, seg_len), parts(next_ref, 0, rest)
        )
        low = parts(before_ref, 0, half)
        high = parts(before_ref, half, seg_len)
        pot[:, :half] = jnp.where(low[1] > 0, potential(*low), NEG)
        pot[:, half:seg_len] = jnp.where(
            high[1] > 0, merged_potential(high, parts(back_ref, 0, rest)), NEG
        )
        ext[:, channels:] = potential_lanes(pot[...] * (1.0 / scale), channels)

    ext[:half, :channels] = prev_low_ref[0]
    ext[half:seg_len, :channels] = prev_high_ref[0]
    ext[seg_len:, :channels] = right_ref[0]
    sums[...] = jnp.zeros_like(sums)
    window = seg_len + block
    big = 2 * block
    strip = 16
    mine = line_lanes(line, lines_here, (big, channels)).astype(jnp.bfloat16)
    strip_lanes = line_lanes(line, lines_here, (strip, channels))
    lane = lax.broadcasted_iota(jnp.int32, (strip, channels), 1)
    for index in range(seg_len // big):
        start = index * big
        slot = index % 2
        raw[slot] = scores_of(
            jnp.concatenate([left_ref[0, start : start + big], mine], axis=1),
            ext[start : start + seg_len + big],
        )
        for side in range(2):
            shift = side * block
            first = start + shift
            column_sum = jnp.zeros((8, window), jnp.float32)
            for row in range(0, block, strip):
                rows = slice(shift + row, shift + row + strip)
                logits = banded(raw[slot, rows, shift : shift + window], row, block)
                peak = jnp.max(logits, axis=1, keepdims=True)
                terms = jnp.exp2((logits - peak) * scale)
                plan = terms * (1.0 / jnp.sum(terms, axis=1, keepdims=True))
                column_sum += plan[:8] + plan[8:]
                lanes = strip_lanes
                for part, piece in enumerate(split(peak, SHIFT)):
                    lanes = jnp.where(lane == channels - SHIFT + part, piece, lanes)
                lanes_ref[0, first + row : first + row + strip] = lanes.astype(jnp.bfloat16)
            sums[:, first : first + window] += column_sum
    totals = jnp.sum(sums[...], axis=0, keepdims=True)
    prev_out[pl.ds(line, 1), :] = totals[:, :seg_len]
    own_out[pl.ds(line, 1), :] = totals[:, seg_len:]


def row_pass(left, right, prev_low, prev_high, own, following, before, back, block):
    lines_here, seg_len, channels = left.shape
    half = prev_low.shape[1]
    marginal = jax.ShapeDtypeStruct((lines_here, seg_len), jnp.float32)
    return pl.pallas_call(
        functools.partial(row_kernel, block),
        grid=(lines_here,),
        in_specs=[per_line((seg_len, channels))] * 2
        + [per_line((half, channels)), per_line((seg_len - half, channels))]
        + [whole(part.shape) for part in (own, following, before, back)],
        out_specs=[
            whole((lines_here, 2 * seg_len)),
            per_line((seg_len, channels)),
            whole((lines_here, seg_len)),
            whole((lines_here, seg_len)),
        ],
        out_shape=[
            jax.ShapeDtypeStruct((lines_here, 2 * seg_len), jnp.float32),
            jax.ShapeDtypeStruct(left.shape, jnp.bfloat16),
            marginal,
            marginal,
        ],
        scratch_shapes=[
            pltpu.VMEM((2 * seg_len, 2 * channels), jnp.bfloat16),
            pltpu.VMEM((8, 2 * seg_len), jnp.float32),
            pltpu.VMEM((2, 2 * block, seg_len + 2 * block), jnp.float32),
        ],
        compiler_params=params(),
        name="row_pass",
    )(left, right, prev_low, prev_high, own, following, before, back)


def transport_kernel(
    block,
    layers,
    pot_ref,
    lanes_ref,
    left_ref,
    right_ref,
    prev_low_ref,
    prev_high_ref,
    own_ref,
    next_ref,
    before_ref,
    back_ref,
    state_ref,
    disp_ref,
    first_ref,
    last_ref,
    low_ref,
    high_ref,
    ext,
    marks,
    raw,
):
    line = pl.program_id(0)
    lines_here = pot_ref.shape[0]
    seg_len, channels = left_ref.shape[1:]
    half = prev_low_ref.shape[1]
    scale = log2_scale(channels)
    big = 2 * block
    window = seg_len + big

    @pl.when(line == 0)
    def _():
        total = jnp.concatenate(
            [before_ref[...] + back_ref[...], own_ref[...] + next_ref[...]], axis=1
        )
        pot = jnp.where(total > 0, pot_ref[...] - jnp.log2(total), NEG)
        ext[:, channels:] = potential_lanes(pot * (1.0 / scale), channels)
        lane = lax.broadcasted_iota(jnp.int32, (window, channels), 1)
        distance = seg_len - lax.broadcasted_iota(jnp.int32, (window, channels), 0)
        low = jnp.bitwise_and(distance, 15)
        values = jnp.where(
            lane == 0,
            1,
            jnp.where(lane == 1, distance - low, jnp.where(lane == 2, low, 0)),
        )
        marks[...] = values.astype(jnp.float32).astype(jnp.bfloat16)

    ext[:half, :channels] = prev_low_ref[0]
    ext[half:seg_len, :channels] = prev_high_ref[0]
    ext[seg_len:, :channels] = right_ref[0]
    offsets = lax.broadcasted_iota(jnp.int32, (1, big), 1).astype(jnp.float32)
    corner = jnp.zeros((block, block), jnp.bfloat16)
    disparity = []
    for index in range(seg_len // big):
        first = index * big
        slot = index % 2
        rows = slice(first, first + big)
        raw[slot] = scores_of(
            jnp.concatenate([left_ref[0, rows], lanes_ref[0, rows]], axis=1),
            ext[first : first + window],
        )
        upper = jnp.exp2(banded(raw[slot, :block, : window - block], 0, block) * scale)
        lower = jnp.exp2(banded(raw[slot, block:, block:], 0, block) * scale)
        weights = jnp.concatenate(
            [
                jnp.concatenate([upper.astype(jnp.bfloat16), corner], axis=1),
                jnp.concatenate([corner, lower.astype(jnp.bfloat16)], axis=1),
            ],
            axis=0,
        )
        table = jnp.concatenate([ext[first : first + window, :channels], marks[...]], axis=1)
        result = jnp.dot(weights, table, preferred_element_type=jnp.float32)
        matched = result[:, :channels] * (1.0 / result[:, channels : channels + 1])
        state_ref[0, rows] = (matched - left_ref[0, rows].astype(jnp.float32)).astype(
            state_ref.dtype
        )
        moments = result[:, channels:].T
        disparity.append(offsets + (moments[1:2] + moments[2:3]) / moments[0:1])
    disp_ref[pl.ds(line, 1), :] = jnp.concatenate(disparity, axis=1)
    low_ref[...] = state_ref[:, :EDGE]
    high_ref[...] = state_ref[:, seg_len - EDGE :]

    @pl.when(line < layers)
    def _():
        first_ref[...] = state_ref[...]

    @pl.when(line >= lines_here - layers)
    def _():
        last_ref[...] = state_ref[...]


def transport(pot, lanes, left, right, prev_low, prev_high, own, following, before, back, block, layers):
    lines_here, seg_len, channels = left.shape
    half = prev_low.shape[1]
    edge = jax.ShapeDtypeStruct((layers, seg_len, channels), jnp.bfloat16)
    side = jax.ShapeDtypeStruct((lines_here, EDGE, channels), jnp.bfloat16)
    return pl.pallas_call(
        functools.partial(transport_kernel, block, layers),
        grid=(lines_here,),
        in_specs=[whole(pot.shape)]
        + [per_line((seg_len, channels))] * 3
        + [per_line((half, channels)), per_line((seg_len - half, channels))]
        + [whole((lines_here, seg_len))] * 4,
        out_specs=[
            per_line((seg_len, channels)),
            whole((lines_here, seg_len)),
            pl.BlockSpec((1, seg_len, channels), lambda l: (jnp.minimum(l, layers - 1), 0, 0)),
            pl.BlockSpec(
                (1, seg_len, channels),
                lambda l: (jnp.maximum(l - (lines_here - layers), 0), 0, 0),
            ),
            per_line((EDGE, channels)),
            per_line((EDGE, channels)),
        ],
        out_shape=[
            jax.ShapeDtypeStruct(left.shape, jnp.bfloat16),
            jax.ShapeDtypeStruct((lines_here, seg_len), jnp.float32),
            edge,
            edge,
            side,
            side,
        ],
        scratch_shapes=[
            pltpu.VMEM((2 * seg_len, 2 * channels), jnp.bfloat16),
            pltpu.VMEM((seg_len + 2 * block, channels), jnp.bfloat16),
            pltpu.VMEM((2, 2 * block, seg_len + 2 * block), jnp.float32),
        ],
        compiler_params=params(),
        name="transport",
    )(pot, lanes, left, right, prev_low, prev_high, own, following, before, back)


def stack_weights(weight_ref, stacked_ref):
    layers, taps, _, channels, _ = weight_ref.shape
    zeros = jnp.zeros((channels, channels), stacked_ref.dtype)
    for layer in range(layers):
        for col_tap in range(taps):
            for line in range(taps + 1):
                row = (col_tap * (taps + 1) + line) * channels
                for out in range(2):
                    row_tap = line - out
                    stacked_ref[
                        layer, row : row + channels, out * channels : (out + 1) * channels
                    ] = weight_ref[layer, row_tap, col_tap] if 0 <= row_tap < taps else zeros


def conv_kernel(
    state_ref,
    top_ref,
    bottom_ref,
    left_ref,
    right_ref,
    corner_top_ref,
    corner_bottom_ref,
    weight_ref,
    bias_ref,
    out_ref,
    first_image,
    second_image,
):
    lines_here, seg_len, channels = state_ref.shape
    layers = weight_ref.shape[0]
    after = layers + lines_here
    right = EDGE + seg_len
    f32 = jnp.float32
    first_image[:layers, EDGE:right] = top_ref[...].astype(f32)
    first_image[layers:after, EDGE:right] = state_ref[...].astype(f32)
    first_image[after:, EDGE:right] = bottom_ref[...].astype(f32)
    first_image[layers:after, :EDGE] = left_ref[...].astype(f32)
    first_image[layers:after, right:] = right_ref[...].astype(f32)
    for rows, corner_ref in ((slice(0, layers), corner_top_ref), (slice(after, None), corner_bottom_ref)):
        first_image[rows, :EDGE] = corner_ref[:, :EDGE].astype(f32)
        first_image[rows, right:] = corner_ref[:, EDGE:].astype(f32)
    line0 = lax.axis_index("lines") * lines_here - layers
    all_lines = lax.axis_size("lines") * lines_here
    px0 = lax.axis_index("seg") * seg_len - EDGE
    all_px = lax.axis_size("seg") * seg_len
    source, target = first_image, second_image
    for layer in range(layers):
        reach = layers - 1 - layer
        begin, end = (EDGE // 2, right + EDGE // 2) if reach else (EDGE, right)
        pieces = 5 if reach else 4
        size = (end - begin) // pieces

        def pair(index, carry, layer=layer, reach=reach, begin=begin, pieces=pieces, size=size, source=source, target=target):
            base = layer + 2 * index
            for piece in range(pieces):
                start = begin + piece * size
                taps = [
                    source[base + line, start + col_tap - 1 : start + col_tap - 1 + size].astype(jnp.bfloat16)
                    for col_tap in range(3)
                    for line in range(4)
                ]
                total = jnp.dot(
                    jnp.concatenate(taps, axis=1), weight_ref[layer], preferred_element_type=f32
                )
                for out in range(2):
                    line = base + 1 + out
                    part = total[:, out * channels : (out + 1) * channels] + bias_ref[layer : layer + 1]
                    updated = source[line, start : start + size] + jnp.maximum(part, 0.0)
                    if not reach:
                        out_ref[line - layers, start - EDGE : start - EDGE + size] = updated.astype(out_ref.dtype)
                        continue
                    image_line = line0 + line
                    inside = (image_line >= 0) & (image_line < all_lines)
                    if piece in (0, pieces - 1):
                        px = px0 + start + lax.broadcasted_iota(jnp.int32, updated.shape, 0)
                        inside = inside & (px >= 0) & (px < all_px)
                    updated = jnp.where(inside, updated, 0.0)
                    target[line, start : start + size] = updated.astype(jnp.bfloat16).astype(f32)
            return carry

        lax.fori_loop(0, (lines_here + 2 * reach) // 2, pair, 0)
        source, target = target, source


def conv_layers(state, top, bottom, left_px, right_px, corners_top, corners_bottom, weight, bias):
    layers = weight.shape[0]
    lines_here, seg_len, channels = state.shape
    image = pltpu.VMEM((lines_here + 2 * layers, seg_len + 2 * EDGE, channels), jnp.float32)
    return pl.pallas_call(
        conv_kernel,
        in_specs=[pl.BlockSpec(memory_space=pltpu.VMEM)] * 9,
        out_specs=pl.BlockSpec(memory_space=pltpu.VMEM),
        out_shape=jax.ShapeDtypeStruct(state.shape, state.dtype),
        scratch_shapes=[image, image],
        compiler_params=params(),
        name="conv_layers",
    )(state, top, bottom, left_px, right_px, corners_top, corners_bottom, weight, bias)


def shards(left_features, right_features, conv_weight, conv_bias):
    seg_len = left_features.shape[1]
    half = seg_len // 2
    layers = conv_weight.shape[0]
    prev_high = shifted(right_features[:, half:], "seg", 1)
    next_low = shifted(left_features[:, :half], "seg", -1)
    prev_low = shifted(right_features[:, :half], "seg", 1)
    stacked, own = own_partials(left_features, right_features, conv_weight)
    own, back = cross_partials(left_features, prev_high, next_low, right_features, own)
    before = shifted(own, "seg", 1)
    following = shifted(back, "seg", -1)
    block = min(128, half)
    pot, lanes, own, back = row_pass(
        left_features, right_features, prev_low, prev_high, own, following, before, back, block
    )
    before = shifted(own, "seg", 1)
    following = shifted(back, "seg", -1)
    state, disparity, first, last, low, high = transport(
        pot, lanes, left_features, right_features, prev_low, prev_high, own, following, before, back, block, layers
    )
    bottom = shifted(first, "lines", -1)
    top = shifted(last, "lines", 1)
    left_px = shifted(high, "seg", 1)
    right_px = shifted(low, "seg", -1)
    edges = jnp.concatenate([left_px, right_px], axis=1)
    corners_bottom = shifted(edges[:layers], "lines", -1)
    corners_top = shifted(edges[-layers:], "lines", 1)
    refined = conv_layers(
        state, top, bottom, left_px, right_px, corners_top, corners_bottom, stacked, conv_bias
    )
    return (refined, disparity)


def solution(mesh):
    return jax.shard_map(
        shards,
        mesh=mesh,
        in_specs=(P("lines", "seg", None), P("lines", "seg", None), P(), P()),
        out_specs=(P("lines", "seg", None), P("lines", "seg")),
        check_vma=False,
    )
```

```python
import functools
import math

import jax
import jax.numpy as jnp
from jax import lax
from jax.experimental import pallas as pl
from jax.experimental.pallas import tpu as pltpu
from jax.sharding import PartitionSpec as P

DISP = 1024
NEG = -1e30
EDGE = 16
VMEM_BYTES = 32 * 1024 * 1024


def shifted(block, axis, step):
    count = lax.axis_size(axis)
    route = [(i, i + step) for i in range(count) if 0 <= i + step < count]
    return lax.ppermute(block, axis, route)


def params():
    return pltpu.CompilerParams(vmem_limit_bytes=VMEM_BYTES)


ANYWHERE = pl.BlockSpec(memory_space=pl.ANY)


def kernel_call(kernel, operands, results, scratch, copies, name, cost=None):
    return pl.pallas_call(
        kernel,
        in_specs=[ANYWHERE] * len(operands),
        out_specs=[ANYWHERE] * len(results),
        out_shape=[jax.ShapeDtypeStruct(shape, dtype) for shape, dtype in results],
        scratch_shapes=[pltpu.VMEM(shape, dtype) for shape, dtype in scratch]
        + [pltpu.SemaphoreType.DMA((count,)) for count in copies],
        compiler_params=params(),
        cost_estimate=cost,
        name=name,
    )(*operands)


def copies_of(pairs, sems):
    return [
        pltpu.make_async_copy(source, target, sems.at[index])
        for index, (source, target) in enumerate(pairs)
    ]


def line_copies(pairs, sems, line, lines_here):
    return [
        pltpu.make_async_copy(source.at[line], target.at[line], sems.at[index * lines_here + line])
        for index, (source, target) in enumerate(pairs)
    ]


def begin_copies(copies):
    for copy in copies:
        copy.start()


def wait(copies):
    for copy in copies:
        copy.wait()


def scores_of(left, right):
    return lax.dot_general(
        left, right, (((1,), (1,)), ((), ())), preferred_element_type=jnp.float32
    )


def log2_scale(channels):
    return math.log2(math.e) / math.sqrt(channels)


def over_rows(reduce, values, chains=64):
    count, width = values.shape
    while count > chains >= 8 and count % chains == 0:
        values = reduce(values.reshape(count // chains, chains, width), axis=0)
        count, chains = chains, chains // 8
    return reduce(values, axis=0, keepdims=True)


def column_block(left, right, diagonal_first):
    block, channels = right.shape
    scale = log2_scale(channels)
    raw = scores_of(left, right)
    row_ids = lax.broadcasted_iota(jnp.int32, (block, block), 0)
    col_ids = lax.broadcasted_iota(jnp.int32, (block, block), 1)
    if diagonal_first:
        parts = [jnp.where(col_ids <= row_ids, raw[:block], NEG), raw[block:]]
    else:
        parts = [raw[:-block], jnp.where(col_ids > row_ids, raw[-block:], NEG)]
    parts = [part for part in parts if part.shape[0]]
    peak = functools.reduce(jnp.maximum, [over_rows(jnp.max, part) for part in parts])
    total = sum(over_rows(jnp.sum, jnp.exp2((part - peak) * scale)) for part in parts)
    return (peak * scale, total)


def own_kernel(
    block,
    left_in,
    right_in,
    weight_in,
    stacked_out,
    part_out,
    left,
    right,
    weight,
    stacked,
    part,
    line_sems,
    sems,
):
    lines_here, seg_len = left.shape[:2]
    pairs = ((left_in, left), (right_in, right))
    for line in range(lines_here):
        begin_copies(line_copies(pairs, line_sems, line, lines_here))
    fetch, send_stacked, send_part = copies_of(
        ((weight_in, weight), (stacked, stacked_out), (part, part_out)), sems
    )
    fetch.start()

    def one_line(line, carry):
        wait(line_copies(pairs, line_sems, line, lines_here))
        for first in range(0, seg_len, block):
            cols = slice(first, first + block)
            peak, total = column_block(left[line, first:], right[line, cols], True)
            part[pl.ds(line, 1), cols] = peak
            part[pl.ds(lines_here + line, 1), cols] = total
        return carry

    lax.fori_loop(0, lines_here, one_line, 0)
    send_part.start()
    fetch.wait()
    stack_weights(weight, stacked)
    send_stacked.start()
    send_part.wait()
    send_stacked.wait()


def column_cost(lines_here, seg_len, channels):
    return pl.CostEstimate(
        flops=2 * lines_here * seg_len * seg_len * channels,
        bytes_accessed=8 * lines_here * seg_len * channels,
        transcendentals=lines_here * seg_len * seg_len // 2,
    )


def own_partials(left, right, weight):
    lines_here, seg_len, channels = left.shape
    bf16, f32 = jnp.bfloat16, jnp.float32
    stacked = ((weight.shape[0], 12 * channels, 2 * channels), bf16)
    part = ((2 * lines_here, seg_len), f32)
    return kernel_call(
        functools.partial(own_kernel, min(256, seg_len)),
        (left, right, weight),
        (stacked, part),
        ((left.shape, bf16), (right.shape, bf16), (weight.shape, bf16), stacked, part),
        (2 * lines_here, 3),
        "column_own",
        column_cost(*left.shape),
    )


def cross_kernel(
    block,
    left_in,
    prev_in,
    next_in,
    right_in,
    own_in,
    merged_out,
    back_out,
    left,
    prev,
    following,
    right,
    own,
    merged,
    back,
    line_sems,
    sems,
):
    lines_here, half = following.shape[:2]
    pairs = (
        (left_in, left),
        (prev_in, prev),
        (next_in, following),
        (right_in.at[:, pl.ds(0, half)], right),
    )
    fetch, send_merged, send_back = copies_of(
        ((own_in, own), (merged, merged_out), (back, back_out)), sems
    )
    fetch.start()
    for line in range(lines_here):
        begin_copies(line_copies(pairs, line_sems, line, lines_here))
    fetch.wait()
    last = lax.axis_index("seg") == lax.axis_size("seg") - 1
    merged[:, half:] = own[:, half:]

    def one_line(line, carry):
        wait(line_copies(pairs, line_sems, line, lines_here))
        top, bottom = pl.ds(line, 1), pl.ds(lines_here + line, 1)
        for first in range(0, prev.shape[1], block):
            cols = slice(first, first + block)
            peak, total = column_block(
                left[line, : half + first + block], prev[line, cols], False
            )
            back[top, cols] = peak
            back[bottom, cols] = total
        for first in range(0, half, block):
            cols = slice(first, first + block)
            peak, total = column_block(following[line, : first + block], right[line, cols], False)
            peak = jnp.where(last, NEG, peak)
            total = jnp.where(last, 0.0, total)
            own_peak = own[top, cols]
            joint = jnp.maximum(own_peak, peak)
            merged[top, cols] = joint
            merged[bottom, cols] = own[bottom, cols] * jnp.exp2(
                own_peak - joint
            ) + total * jnp.exp2(peak - joint)
        return carry

    lax.fori_loop(0, lines_here, one_line, 0)
    begin_copies((send_merged, send_back))
    wait((send_merged, send_back))


def cross_partials(left, prev_high, next_low, right, own):
    lines_here, seg_len, channels = left.shape
    half = next_low.shape[1]
    bf16, f32 = jnp.bfloat16, jnp.float32
    back = ((2 * lines_here, seg_len - half), f32)
    merged = (own.shape, f32)
    return kernel_call(
        functools.partial(cross_kernel, min(256, half)),
        (left, prev_high, next_low, right, own),
        (merged, back),
        (
            (left.shape, bf16),
            (prev_high.shape, bf16),
            (next_low.shape, bf16),
            (next_low.shape, bf16),
            merged,
            merged,
            back,
        ),
        (4 * lines_here, 3),
        "column_cross",
        column_cost(*left.shape),
    )


def potential(peak, total):
    return -(peak + jnp.log2(total))


def merged_potential(first, second):
    first_max = jnp.where(first[1] > 0, first[0], NEG)
    second_max = jnp.where(second[1] > 0, second[0], NEG)
    peak = jnp.maximum(first_max, second_max)
    total = first[1] * jnp.exp2(first_max - peak) + second[1] * jnp.exp2(second_max - peak)
    return potential(peak, total)


def split(values, parts):
    pieces = []
    for _ in range(parts):
        piece = values.astype(jnp.bfloat16).astype(jnp.float32)
        pieces.append(piece)
        values = values - piece
    return pieces


SHIFT = 2


def potential_lanes(pot, channels):
    lines_here, count = pot.shape
    parts = split(pot, 3)
    filler = jnp.zeros((channels - 3 * lines_here, count), jnp.float32)
    lanes = jnp.concatenate(parts + [filler], axis=0).T
    lane = lax.broadcasted_iota(jnp.int32, lanes.shape, 1)
    return jnp.where(lane >= channels - SHIFT, -1.0, lanes).astype(jnp.bfloat16)


def line_lanes(line, lines_here, shape):
    lane = lax.broadcasted_iota(jnp.int32, shape, 1)
    mine = jnp.zeros(shape, jnp.float32)
    for part in range(3):
        mine = jnp.where(lane == part * lines_here + line, 1.0, mine)
    return mine


def banded(values, row, block):
    rows, window = values.shape
    col_ids = lax.broadcasted_iota(jnp.int32, (rows, block), 1)
    row_ids = lax.broadcasted_iota(jnp.int32, (rows, block), 0) + row
    return jnp.concatenate(
        [
            jnp.where(col_ids > row_ids, values[:, :block], NEG),
            values[:, block : window - block],
            jnp.where(col_ids <= row_ids, values[:, window - block :], NEG),
        ],
        axis=1,
    )


def feature_pairs(left_in, right_in, prev_low_in, prev_high_in, left, ext):
    seg_len, half = left.shape[1], prev_low_in.shape[1]
    return (
        (left_in, left),
        (prev_low_in, ext.at[:, pl.ds(0, half)]),
        (prev_high_in, ext.at[:, pl.ds(half, seg_len - half)]),
        (right_in, ext.at[:, pl.ds(seg_len, seg_len)]),
    )


def row_kernel(
    block,
    left_in,
    right_in,
    prev_low_in,
    prev_high_in,
    own_in,
    next_in,
    before_in,
    back_in,
    pot_out,
    lanes_out,
    own_out,
    prev_out,
    left,
    ext,
    own,
    following,
    before,
    back,
    pot,
    lanes,
    own_sum,
    prev_sum,
    pot_lanes,
    sums,
    raw,
    line_sems,
    sems,
):
    lines_here, seg_len, channels = left.shape
    half = prev_low_in.shape[1]
    scale = log2_scale(channels)
    fetches = copies_of(
        ((own_in, own), (next_in, following), (before_in, before), (back_in, back)), sems
    )
    begin_copies(fetches)
    pairs = feature_pairs(left_in, right_in, prev_low_in, prev_high_in, left, ext)
    for line in range(lines_here):
        begin_copies(line_copies(pairs, line_sems, line, lines_here))
    wait(fetches)

    def parts(ref, first, stop):
        return ref[:lines_here, first:stop], ref[lines_here:, first:stop]

    rest = seg_len - half
    pot[:, seg_len : seg_len + half] = potential(*parts(own, 0, half))
    pot[:, seg_len + half :] = merged_potential(
        parts(own, half, seg_len), parts(following, 0, rest)
    )
    low = parts(before, 0, half)
    high = parts(before, half, seg_len)
    pot[:, :half] = jnp.where(low[1] > 0, potential(*low), NEG)
    pot[:, half:seg_len] = jnp.where(
        high[1] > 0, merged_potential(high, parts(back, 0, rest)), NEG
    )
    pot_lanes[...] = potential_lanes(pot[...] * (1.0 / scale), channels)
    window = seg_len + block
    big = 2 * block
    steps = seg_len // big
    strip = 16
    lane = lax.broadcasted_iota(jnp.int32, (strip, channels), 1)

    def one_line(line, carry):
        wait(line_copies(pairs, line_sems, line, lines_here))
        sums[...] = jnp.zeros_like(sums)
        mine = line_lanes(line, lines_here, (big, channels)).astype(jnp.bfloat16)
        strip_lanes = line_lanes(line, lines_here, (strip, channels))

        def score(index):
            first = index * big
            reach = slice(first, first + seg_len + big)
            raw[index % 2] = scores_of(
                jnp.concatenate([left[line, first : first + big], mine], axis=1),
                jnp.concatenate([ext[line, reach], pot_lanes[reach]], axis=1),
            )

        score(0)
        for index in range(steps):
            slot = index % 2
            if index + 1 < steps:
                score(index + 1)
            for side in range(2):
                shift = side * block
                first = index * big + shift
                column_sum = jnp.zeros((8, window), jnp.float32)
                for row in range(0, block, strip):
                    rows = slice(shift + row, shift + row + strip)
                    logits = banded(raw[slot, rows, shift : shift + window], row, block)
                    peak = jnp.max(logits, axis=1, keepdims=True)
                    terms = jnp.exp2((logits - peak) * scale)
                    plan = terms * (1.0 / jnp.sum(terms, axis=1, keepdims=True))
                    column_sum += plan[:8] + plan[8:]
                    marked = strip_lanes
                    for part, piece in enumerate(split(peak, SHIFT)):
                        marked = jnp.where(lane == channels - SHIFT + part, piece, marked)
                    lanes[line, first + row : first + row + strip] = marked.astype(jnp.bfloat16)
                sums[:, first : first + window] += column_sum
        totals = jnp.sum(sums[...], axis=0, keepdims=True)
        prev_sum[pl.ds(line, 1), :] = totals[:, :seg_len]
        own_sum[pl.ds(line, 1), :] = totals[:, seg_len:]
        return carry

    lax.fori_loop(0, lines_here, one_line, 0)
    sends = copies_of(
        ((own_sum, own_out), (prev_sum, prev_out), (pot, pot_out), (lanes, lanes_out)), sems
    )
    begin_copies(sends)
    wait(sends)


def row_pass(left, right, prev_low, prev_high, own, following, before, back, block):
    lines_here, seg_len, channels = left.shape
    bf16, f32 = jnp.bfloat16, jnp.float32
    marginal = ((lines_here, seg_len), f32)
    pot = ((lines_here, 2 * seg_len), f32)
    lanes = (left.shape, bf16)
    return kernel_call(
        functools.partial(row_kernel, block),
        (left, right, prev_low, prev_high, own, following, before, back),
        (pot, lanes, marginal, marginal),
        (
            (left.shape, bf16),
            ((lines_here, 2 * seg_len, channels), bf16),
            (own.shape, f32),
            (following.shape, f32),
            (before.shape, f32),
            (back.shape, f32),
            pot,
            lanes,
            marginal,
            marginal,
            ((2 * seg_len, channels), bf16),
            ((8, 2 * seg_len), f32),
            ((2, 2 * block, seg_len + 2 * block), f32),
        ),
        (4 * lines_here, 4),
        "row_pass",
    )


def transport_kernel(
    block,
    pot_in,
    lanes_in,
    left_in,
    right_in,
    prev_low_in,
    prev_high_in,
    own_in,
    next_in,
    before_in,
    back_in,
    state_out,
    disp_out,
    first_out,
    last_out,
    low_out,
    high_out,
    pot,
    lanes,
    left,
    ext,
    own,
    following,
    before,
    back,
    state,
    disp,
    pot_lanes,
    marks,
    raw,
    weights,
    line_sems,
    sems,
    send_sems,
):
    lines_here, seg_len, channels = left.shape
    layers = first_out.shape[0]
    scale = log2_scale(channels)
    big = 2 * block
    window = seg_len + big
    fetches = copies_of(
        ((pot_in, pot), (own_in, own), (next_in, following), (before_in, before), (back_in, back)),
        sems,
    )
    begin_copies(fetches)
    pairs = feature_pairs(left_in, right_in, prev_low_in, prev_high_in, left, ext) + (
        (lanes_in, lanes),
    )
    for line in range(lines_here):
        begin_copies(line_copies(pairs, line_sems, line, lines_here))
    lane = lax.broadcasted_iota(jnp.int32, (window, channels), 1)
    distance = seg_len - lax.broadcasted_iota(jnp.int32, (window, channels), 0)
    fine = jnp.bitwise_and(distance, 15)
    values = jnp.where(
        lane == 0,
        1,
        jnp.where(lane == 1, distance - fine, jnp.where(lane == 2, fine, 0)),
    )
    marks[...] = values.astype(jnp.float32).astype(jnp.bfloat16)
    wait(fetches)
    total = jnp.concatenate([before[...] + back[...], own[...] + following[...]], axis=1)
    final = jnp.where(total > 0, pot[...] - jnp.log2(total), NEG)
    pot_lanes[...] = potential_lanes(final * (1.0 / scale), channels)
    offsets = lax.broadcasted_iota(jnp.int32, (1, big), 1).astype(jnp.float32)
    corner = jnp.zeros((block, block), jnp.bfloat16)
    steps = seg_len // big
    edges = ((state.at[:, pl.ds(0, EDGE)], low_out), (state.at[:, pl.ds(seg_len - EDGE, EDGE)], high_out))

    def one_line(line, carry):
        wait(line_copies(pairs, line_sems, line, lines_here))

        def score(index):
            first = index * big
            rows, reach = slice(first, first + big), slice(first, first + window)
            raw[index % 2] = scores_of(
                jnp.concatenate([left[line, rows], lanes[line, rows]], axis=1),
                jnp.concatenate([ext[line, reach], pot_lanes[reach]], axis=1),
            )

        def weigh(index):
            slot = index % 2
            upper = jnp.exp2(banded(raw[slot, :block, : window - block], 0, block) * scale)
            lower = jnp.exp2(banded(raw[slot, block:, block:], 0, block) * scale)
            weights[slot, :block, : window - block] = upper.astype(jnp.bfloat16)
            weights[slot, :block, window - block :] = corner
            weights[slot, block:, block:] = lower.astype(jnp.bfloat16)
            weights[slot, block:, :block] = corner

        def gather(index):
            first = index * big
            rows = slice(first, first + big)
            table = jnp.concatenate([ext[line, first : first + window], marks[...]], axis=1)
            result = jnp.dot(weights[index % 2], table, preferred_element_type=jnp.float32)
            matched = result[:, :channels] * (1.0 / result[:, channels : channels + 1])
            state[line, rows] = (matched - left[line, rows].astype(jnp.float32)).astype(
                state.dtype
            )
            moments = result[:, channels:].T
            return offsets + (moments[1:2] + moments[2:3]) / moments[0:1]

        disparity = []
        for index in range(steps + 2):
            if index < steps:
                score(index)
            if index >= 2:
                disparity.append(gather(index - 2))
            if 1 <= index <= steps:
                weigh(index - 1)
        disp[pl.ds(line, 1), :] = jnp.concatenate(disparity, axis=1)
        begin_copies(line_copies(((state, state_out),) + edges, send_sems, line, lines_here))

        @pl.when(line < layers)
        def _():
            pltpu.make_async_copy(state.at[line], first_out.at[line], sems.at[line]).start()

        @pl.when(line >= lines_here - layers)
        def _():
            target = line - (lines_here - layers)
            pltpu.make_async_copy(
                state.at[line], last_out.at[target], sems.at[layers + target]
            ).start()

        return carry

    lax.fori_loop(0, lines_here, one_line, 0)
    send = pltpu.make_async_copy(disp, disp_out, sems.at[2 * layers])
    send.start()
    for line in range(layers):
        pltpu.make_async_copy(state.at[line], first_out.at[line], sems.at[line]).wait()
        source = line + lines_here - layers
        pltpu.make_async_copy(state.at[source], last_out.at[line], sems.at[layers + line]).wait()
    for line in range(lines_here):
        wait(line_copies(((state, state_out),) + edges, send_sems, line, lines_here))
    send.wait()


def transport(pot, lanes, left, right, prev_low, prev_high, own, following, before, back, block, layers):
    lines_here, seg_len, channels = left.shape
    bf16, f32 = jnp.bfloat16, jnp.float32
    edge = ((layers, seg_len, channels), bf16)
    side = ((lines_here, EDGE, channels), bf16)
    state = (left.shape, bf16)
    marginal = ((lines_here, seg_len), f32)
    window = seg_len + 2 * block
    return kernel_call(
        functools.partial(transport_kernel, block),
        (pot, lanes, left, right, prev_low, prev_high, own, following, before, back),
        (state, marginal, edge, edge, side, side),
        (
            (pot.shape, f32),
            (lanes.shape, bf16),
            state,
            ((lines_here, 2 * seg_len, channels), bf16),
            marginal,
            marginal,
            marginal,
            marginal,
            state,
            marginal,
            ((2 * seg_len, channels), bf16),
            ((window, channels), bf16),
            ((2, 2 * block, window), f32),
            ((2, 2 * block, window), bf16),
        ),
        (5 * lines_here, max(5, 2 * layers + 1), 3 * lines_here),
        "transport",
    )


def stack_weights(weight_ref, stacked_ref):
    layers, taps, _, channels, _ = weight_ref.shape
    zeros = jnp.zeros((channels, channels), stacked_ref.dtype)
    for layer in range(layers):
        for col_tap in range(taps):
            for line in range(taps + 1):
                row = (col_tap * (taps + 1) + line) * channels
                for out in range(2):
                    row_tap = line - out
                    stacked_ref[
                        layer, row : row + channels, out * channels : (out + 1) * channels
                    ] = weight_ref[layer, row_tap, col_tap] if 0 <= row_tap < taps else zeros


def conv_kernel(
    state_in,
    top_in,
    bottom_in,
    left_in,
    right_in,
    corner_top_in,
    corner_bottom_in,
    weight_in,
    bias_in,
    result_out,
    state_ref,
    top_ref,
    bottom_ref,
    left_ref,
    right_ref,
    corner_top_ref,
    corner_bottom_ref,
    weight_ref,
    bias_ref,
    out_ref,
    first_image,
    second_image,
    sems,
    send_sems,
):
    fetches = copies_of(
        (
            (state_in, state_ref),
            (left_in, left_ref),
            (right_in, right_ref),
            (corner_top_in, corner_top_ref),
            (corner_bottom_in, corner_bottom_ref),
            (top_in, top_ref),
            (bottom_in, bottom_ref),
            (weight_in, weight_ref),
            (bias_in, bias_ref),
        ),
        sems,
    )
    begin_copies(fetches)
    lines_here, seg_len, channels = state_ref.shape
    layers = weight_ref.shape[0]
    after = layers + lines_here
    right = EDGE + seg_len
    f32 = jnp.float32
    wait(fetches[:1])
    first_image[layers:after, EDGE:right] = state_ref[...].astype(f32)
    wait(fetches[1:])
    first_image[:layers, EDGE:right] = top_ref[...].astype(f32)
    first_image[after:, EDGE:right] = bottom_ref[...].astype(f32)
    first_image[layers:after, :EDGE] = left_ref[...].astype(f32)
    first_image[layers:after, right:] = right_ref[...].astype(f32)
    for rows, corner_ref in ((slice(0, layers), corner_top_ref), (slice(after, None), corner_bottom_ref)):
        first_image[rows, :EDGE] = corner_ref[:, :EDGE].astype(f32)
        first_image[rows, right:] = corner_ref[:, EDGE:].astype(f32)
    line0 = lax.axis_index("lines") * lines_here - layers
    all_lines = lax.axis_size("lines") * lines_here
    px0 = lax.axis_index("seg") * seg_len - EDGE
    all_px = lax.axis_size("seg") * seg_len
    source, target = first_image, second_image
    for layer in range(layers):
        reach = layers - 1 - layer
        begin, end = (EDGE // 2, right + EDGE // 2) if reach else (EDGE, right)
        pieces = 5 if reach else 4
        size = (end - begin) // pieces

        def pair(index, carry, layer=layer, reach=reach, begin=begin, pieces=pieces, size=size, source=source, target=target):
            base = layer + 2 * index
            for piece in range(pieces):
                start = begin + piece * size
                taps = [
                    source[base + line, start + col_tap - 1 : start + col_tap - 1 + size].astype(jnp.bfloat16)
                    for col_tap in range(3)
                    for line in range(4)
                ]
                total = jnp.dot(
                    jnp.concatenate(taps, axis=1), weight_ref[layer], preferred_element_type=f32
                )
                for out in range(2):
                    line = base + 1 + out
                    part = total[:, out * channels : (out + 1) * channels] + bias_ref[layer : layer + 1]
                    updated = source[line, start : start + size] + jnp.maximum(part, 0.0)
                    if not reach:
                        out_ref[line - layers, start - EDGE : start - EDGE + size] = updated.astype(out_ref.dtype)
                        continue
                    image_line = line0 + line
                    inside = (image_line >= 0) & (image_line < all_lines)
                    if piece in (0, pieces - 1):
                        px = px0 + start + lax.broadcasted_iota(jnp.int32, updated.shape, 0)
                        inside = inside & (px >= 0) & (px < all_px)
                    updated = jnp.where(inside, updated, 0.0)
                    target[line, start : start + size] = updated.astype(jnp.bfloat16).astype(f32)
            if not reach:
                for line in (base + 1, base + 2):
                    begin_copies(line_copies(((out_ref, result_out),), send_sems, line - layers, lines_here))
            return carry

        lax.fori_loop(0, (lines_here + 2 * reach) // 2, pair, 0)
        source, target = target, source
    for line in range(lines_here):
        wait(line_copies(((out_ref, result_out),), send_sems, line, lines_here))


def conv_layers(state, top, bottom, left_px, right_px, corners_top, corners_bottom, weight, bias):
    layers = weight.shape[0]
    lines_here, seg_len, channels = state.shape
    image = ((lines_here + 2 * layers, seg_len + 2 * EDGE, channels), jnp.float32)
    operands = (state, top, bottom, left_px, right_px, corners_top, corners_bottom, weight, bias)
    result = (state.shape, state.dtype)
    return kernel_call(
        conv_kernel,
        operands,
        (result,),
        tuple((operand.shape, operand.dtype) for operand in operands) + (result, image, image),
        (len(operands), lines_here),
        "conv_layers",
    )[0]


def shards(left_features, right_features, conv_weight, conv_bias):
    seg_len = left_features.shape[1]
    half = seg_len // 2
    layers = conv_weight.shape[0]
    prev_high = shifted(right_features[:, half:], "seg", 1)
    next_low = shifted(left_features[:, :half], "seg", -1)
    prev_low = shifted(right_features[:, :half], "seg", 1)
    stacked, own = own_partials(left_features, right_features, conv_weight)
    own, back = cross_partials(left_features, prev_high, next_low, right_features, own)
    before = shifted(own, "seg", 1)
    following = shifted(back, "seg", -1)
    block = min(128, half)
    pot, lanes, own, back = row_pass(
        left_features, right_features, prev_low, prev_high, own, following, before, back, block
    )
    before = shifted(own, "seg", 1)
    following = shifted(back, "seg", -1)
    state, disparity, first, last, low, high = transport(
        pot, lanes, left_features, right_features, prev_low, prev_high, own, following, before, back, block, layers
    )
    bottom = shifted(first, "lines", -1)
    top = shifted(last, "lines", 1)
    left_px = shifted(high, "seg", 1)
    right_px = shifted(low, "seg", -1)
    edges = jnp.concatenate([left_px, right_px], axis=1)
    corners_bottom = shifted(edges[:layers], "lines", -1)
    corners_top = shifted(edges[-layers:], "lines", 1)
    refined = conv_layers(
        state, top, bottom, left_px, right_px, corners_top, corners_bottom, stacked, conv_bias
    )
    return (refined, disparity)


def solution(mesh):
    return jax.shard_map(
        shards,
        mesh=mesh,
        in_specs=(P("lines", "seg", None), P("lines", "seg", None), P(), P()),
        out_specs=(P("lines", "seg", None), P("lines", "seg")),
        check_vma=False,
    )
```

```python
import functools
import math

import jax
import jax.numpy as jnp
from jax import lax
from jax.experimental import pallas as pl
from jax.experimental.pallas import tpu as pltpu
from jax.sharding import PartitionSpec as P

DISP = 1024
NEG = -1e30
EDGE = 16
VMEM_BYTES = 32 * 1024 * 1024


def shifted(block, axis, step):
    count = lax.axis_size(axis)
    route = [(i, i + step) for i in range(count) if 0 <= i + step < count]
    return lax.ppermute(block, axis, route)


def exchanged(block, axis, odd):
    route = []
    for low in range(odd, lax.axis_size(axis) - 1, 2):
        route += [(low, low + 1), (low + 1, low)]
    return lax.ppermute(block, axis, route)


def even_segment():
    return lax.rem(lax.axis_index("seg"), 2) == 0


def by_parity(following, previous):
    even = even_segment()
    return jnp.where(even, following, previous), jnp.where(even, previous, following)


def params():
    return pltpu.CompilerParams(vmem_limit_bytes=VMEM_BYTES)


ANYWHERE = pl.BlockSpec(memory_space=pl.ANY)


def kernel_call(kernel, operands, results, scratch, copies, name, cost=None):
    return pl.pallas_call(
        kernel,
        in_specs=[ANYWHERE] * len(operands),
        out_specs=[ANYWHERE] * len(results),
        out_shape=[jax.ShapeDtypeStruct(shape, dtype) for shape, dtype in results],
        scratch_shapes=[pltpu.VMEM(shape, dtype) for shape, dtype in scratch]
        + [pltpu.SemaphoreType.DMA((count,)) for count in copies],
        compiler_params=params(),
        cost_estimate=cost,
        name=name,
    )(*operands)


def copies_of(pairs, sems):
    return [
        pltpu.make_async_copy(source, target, sems.at[index])
        for index, (source, target) in enumerate(pairs)
    ]


def line_copies(pairs, sems, line, lines_here):
    return [
        pltpu.make_async_copy(source.at[line], target.at[line], sems.at[index * lines_here + line])
        for index, (source, target) in enumerate(pairs)
    ]


def begin_copies(copies):
    for copy in copies:
        copy.start()


def wait(copies):
    for copy in copies:
        copy.wait()


def scores_of(left, right):
    return lax.dot_general(
        left, right, (((1,), (1,)), ((), ())), preferred_element_type=jnp.float32
    )


def log2_scale(channels):
    return math.log2(math.e) / math.sqrt(channels)


def over_rows(reduce, values, chains=64):
    count, width = values.shape
    while count > chains >= 8 and count % chains == 0:
        values = reduce(values.reshape(count // chains, chains, width), axis=0)
        count, chains = chains, chains // 8
    return reduce(values, axis=0, keepdims=True)


def column_block(left, right, diagonal_first):
    block, channels = right.shape
    scale = log2_scale(channels)
    raw = scores_of(left, right)
    row_ids = lax.broadcasted_iota(jnp.int32, (block, block), 0)
    col_ids = lax.broadcasted_iota(jnp.int32, (block, block), 1)
    if diagonal_first:
        parts = [jnp.where(col_ids <= row_ids, raw[:block], NEG), raw[block:]]
    else:
        parts = [raw[:-block], jnp.where(col_ids > row_ids, raw[-block:], NEG)]
    parts = [part for part in parts if part.shape[0]]
    peak = functools.reduce(jnp.maximum, [over_rows(jnp.max, part) for part in parts])
    total = sum(over_rows(jnp.sum, jnp.exp2((part - peak) * scale)) for part in parts)
    return (peak * scale, total)


def own_kernel(
    block,
    left_in,
    right_in,
    weight_in,
    stacked_out,
    part_out,
    left,
    right,
    weight,
    stacked,
    part,
    line_sems,
    sems,
):
    lines_here, seg_len = left.shape[:2]
    pairs = ((left_in, left), (right_in, right))
    for line in range(lines_here):
        begin_copies(line_copies(pairs, line_sems, line, lines_here))
    fetch, send_stacked, send_part = copies_of(
        ((weight_in, weight), (stacked, stacked_out), (part, part_out)), sems
    )
    fetch.start()

    def one_line(line, carry):
        wait(line_copies(pairs, line_sems, line, lines_here))
        for first in range(0, seg_len, block):
            cols = slice(first, first + block)
            peak, total = column_block(left[line, first:], right[line, cols], True)
            part[pl.ds(line, 1), cols] = peak
            part[pl.ds(lines_here + line, 1), cols] = total
        return carry

    lax.fori_loop(0, lines_here, one_line, 0)
    send_part.start()
    fetch.wait()
    stack_weights(weight, stacked)
    send_stacked.start()
    send_part.wait()
    send_stacked.wait()


def column_cost(lines_here, seg_len, channels):
    return pl.CostEstimate(
        flops=2 * lines_here * seg_len * seg_len * channels,
        bytes_accessed=8 * lines_here * seg_len * channels,
        transcendentals=lines_here * seg_len * seg_len // 2,
    )


def own_partials(left, right, weight):
    lines_here, seg_len, channels = left.shape
    bf16, f32 = jnp.bfloat16, jnp.float32
    stacked = ((weight.shape[0], 12 * channels, 2 * channels), bf16)
    part = ((2 * lines_here, seg_len), f32)
    return kernel_call(
        functools.partial(own_kernel, min(256, seg_len)),
        (left, right, weight),
        (stacked, part),
        ((left.shape, bf16), (right.shape, bf16), (weight.shape, bf16), stacked, part),
        (2 * lines_here, 3),
        "column_own",
        column_cost(*left.shape),
    )


def next_kernel(
    block, next_in, right_in, own_in, merged_out, following, right, merged, line_sems, sems
):
    lines_here, half = following.shape[:2]
    pairs = ((next_in, following), (right_in.at[:, pl.ds(0, half)], right))
    fetch, send = copies_of(((own_in, merged), (merged, merged_out)), sems)
    fetch.start()
    for line in range(lines_here):
        begin_copies(line_copies(pairs, line_sems, line, lines_here))
    fetch.wait()
    last = lax.axis_index("seg") == lax.axis_size("seg") - 1

    def one_line(line, carry):
        wait(line_copies(pairs, line_sems, line, lines_here))
        top, bottom = pl.ds(line, 1), pl.ds(lines_here + line, 1)
        for first in range(0, half, block):
            cols = slice(first, first + block)
            peak, total = column_block(following[line, : first + block], right[line, cols], False)
            peak = jnp.where(last, NEG, peak)
            total = jnp.where(last, 0.0, total)
            own_peak = merged[top, cols]
            joint = jnp.maximum(own_peak, peak)
            merged[bottom, cols] = merged[bottom, cols] * jnp.exp2(
                own_peak - joint
            ) + total * jnp.exp2(peak - joint)
            merged[top, cols] = joint
        return carry

    lax.fori_loop(0, lines_here, one_line, 0)
    send.start()
    send.wait()


def next_partials(next_low, right, own):
    lines_here, half, channels = next_low.shape
    merged = (own.shape, jnp.float32)
    features = (next_low.shape, jnp.bfloat16)
    return kernel_call(
        functools.partial(next_kernel, min(256, half)),
        (next_low, right, own),
        (merged,),
        (features, features, merged),
        (2 * lines_here, 2),
        "column_next",
        column_cost(lines_here, half, channels),
    )[0]


def cross_kernel(
    block,
    left_in,
    prev_in,
    own_in,
    back_out,
    first_out,
    second_out,
    left,
    prev,
    own,
    back,
    first_part,
    second_part,
    line_sems,
    sems,
):
    lines_here, seg_len = left.shape[:2]
    half = seg_len - prev.shape[1]
    pairs = ((left_in, left), (prev_in, prev))
    fetch, *sends = copies_of(
        ((own_in, own), (back, back_out), (first_part, first_out), (second_part, second_out)), sems
    )
    fetch.start()
    for line in range(lines_here):
        begin_copies(line_copies(pairs, line_sems, line, lines_here))
    fetch.wait()
    back[...] = jnp.zeros_like(back)

    def one_line(line, carry):
        wait(line_copies(pairs, line_sems, line, lines_here))
        top, bottom = pl.ds(line, 1), pl.ds(lines_here + line, 1)
        for first in range(0, prev.shape[1], block):
            cols = slice(first, first + block)
            peak, total = column_block(
                left[line, : half + first + block], prev[line, cols], False
            )
            back[top, cols] = peak
            back[bottom, cols] = total
        return carry

    lax.fori_loop(0, lines_here, one_line, 0)
    first_part[...], second_part[...] = by_parity(own[...], back[...])
    begin_copies(sends)
    wait(sends)


def cross_partials(left, prev_high, own):
    lines_here, seg_len, channels = left.shape
    part = (own.shape, jnp.float32)
    return kernel_call(
        functools.partial(cross_kernel, min(256, prev_high.shape[1])),
        (left, prev_high, own),
        (part,) * 3,
        ((left.shape, jnp.bfloat16), (prev_high.shape, jnp.bfloat16)) + (part,) * 4,
        (2 * lines_here, 4),
        "column_cross",
        column_cost(*left.shape),
    )


def potential(peak, total):
    return -(peak + jnp.log2(total))


def merged_potential(first, second):
    first_max = jnp.where(first[1] > 0, first[0], NEG)
    second_max = jnp.where(second[1] > 0, second[0], NEG)
    peak = jnp.maximum(first_max, second_max)
    total = first[1] * jnp.exp2(first_max - peak) + second[1] * jnp.exp2(second_max - peak)
    return potential(peak, total)


def split(values, parts):
    pieces = []
    for _ in range(parts):
        piece = values.astype(jnp.bfloat16).astype(jnp.float32)
        pieces.append(piece)
        values = values - piece
    return pieces


SHIFT = 2


def potential_lanes(pot, channels):
    lines_here, count = pot.shape
    parts = split(pot, 3)
    filler = jnp.zeros((channels - 3 * lines_here, count), jnp.float32)
    lanes = jnp.concatenate(parts + [filler], axis=0).T
    lane = lax.broadcasted_iota(jnp.int32, lanes.shape, 1)
    return jnp.where(lane >= channels - SHIFT, -1.0, lanes).astype(jnp.bfloat16)


def line_lanes(line, lines_here, shape):
    lane = lax.broadcasted_iota(jnp.int32, shape, 1)
    mine = jnp.zeros(shape, jnp.float32)
    for part in range(3):
        mine = jnp.where(lane == part * lines_here + line, 1.0, mine)
    return mine


def banded(values, row, block):
    rows, window = values.shape
    col_ids = lax.broadcasted_iota(jnp.int32, (rows, block), 1)
    row_ids = lax.broadcasted_iota(jnp.int32, (rows, block), 0) + row
    return jnp.concatenate(
        [
            jnp.where(col_ids > row_ids, values[:, :block], NEG),
            values[:, block : window - block],
            jnp.where(col_ids <= row_ids, values[:, window - block :], NEG),
        ],
        axis=1,
    )


def feature_pairs(left_in, right_in, prev_low_in, prev_high_in, left, ext):
    seg_len, half = left.shape[1], prev_low_in.shape[1]
    return (
        (left_in, left),
        (prev_low_in, ext.at[:, pl.ds(0, half)]),
        (prev_high_in, ext.at[:, pl.ds(half, seg_len - half)]),
        (right_in, ext.at[:, pl.ds(seg_len, seg_len)]),
    )


def row_kernel(
    block,
    left_in,
    right_in,
    prev_low_in,
    prev_high_in,
    own_in,
    back_in,
    first_in,
    second_in,
    pot_out,
    lanes_out,
    own_out,
    prev_out,
    first_out,
    second_out,
    left,
    ext,
    own,
    back,
    first_part,
    second_part,
    pot,
    lanes,
    own_sum,
    prev_sum,
    first_sum,
    second_sum,
    pot_lanes,
    sums,
    raw,
    line_sems,
    sems,
):
    lines_here, seg_len, channels = left.shape
    half = prev_low_in.shape[1]
    scale = log2_scale(channels)
    fetches = copies_of(
        ((own_in, own), (back_in, back), (first_in, first_part), (second_in, second_part)), sems
    )
    begin_copies(fetches)
    pairs = feature_pairs(left_in, right_in, prev_low_in, prev_high_in, left, ext)
    for line in range(lines_here):
        begin_copies(line_copies(pairs, line_sems, line, lines_here))
    wait(fetches)

    following, before = by_parity(first_part[...], second_part[...])

    def parts(part, first, stop):
        return part[:lines_here, first:stop], part[lines_here:, first:stop]

    rest = seg_len - half
    pot[:, seg_len : seg_len + half] = potential(*parts(own, 0, half))
    pot[:, seg_len + half :] = merged_potential(
        parts(own, half, seg_len), parts(following, 0, rest)
    )
    low = parts(before, 0, half)
    high = parts(before, half, seg_len)
    pot[:, :half] = jnp.where(low[1] > 0, potential(*low), NEG)
    pot[:, half:seg_len] = jnp.where(
        high[1] > 0, merged_potential(high, parts(back, 0, rest)), NEG
    )
    pot_lanes[...] = potential_lanes(pot[...] * (1.0 / scale), channels)
    window = seg_len + block
    big = 2 * block
    steps = seg_len // big
    strip = 16
    lane = lax.broadcasted_iota(jnp.int32, (strip, channels), 1)

    def one_line(line, carry):
        wait(line_copies(pairs, line_sems, line, lines_here))
        sums[...] = jnp.zeros_like(sums)
        mine = line_lanes(line, lines_here, (big, channels)).astype(jnp.bfloat16)
        strip_lanes = line_lanes(line, lines_here, (strip, channels))

        def score(index):
            first = index * big
            reach = slice(first, first + seg_len + big)
            raw[index % 2] = scores_of(
                jnp.concatenate([left[line, first : first + big], mine], axis=1),
                jnp.concatenate([ext[line, reach], pot_lanes[reach]], axis=1),
            )

        score(0)
        for index in range(steps):
            slot = index % 2
            if index + 1 < steps:
                score(index + 1)
            for side in range(2):
                shift = side * block
                first = index * big + shift
                column_sum = jnp.zeros((8, window), jnp.float32)
                for row in range(0, block, strip):
                    rows = slice(shift + row, shift + row + strip)
                    logits = banded(raw[slot, rows, shift : shift + window], row, block)
                    peak = jnp.max(logits, axis=1, keepdims=True)
                    terms = jnp.exp2((logits - peak) * scale)
                    plan = terms * (1.0 / jnp.sum(terms, axis=1, keepdims=True))
                    column_sum += plan[:8] + plan[8:]
                    marked = strip_lanes
                    for part, piece in enumerate(split(peak, SHIFT)):
                        marked = jnp.where(lane == channels - SHIFT + part, piece, marked)
                    lanes[line, first + row : first + row + strip] = marked.astype(jnp.bfloat16)
                sums[:, first : first + window] += column_sum
        totals = jnp.sum(sums[...], axis=0, keepdims=True)
        prev_sum[pl.ds(line, 1), :] = totals[:, :seg_len]
        own_sum[pl.ds(line, 1), :] = totals[:, seg_len:]
        return carry

    lax.fori_loop(0, lines_here, one_line, 0)
    first_sum[...], second_sum[...] = by_parity(own_sum[...], prev_sum[...])
    sends = copies_of(
        (
            (first_sum, first_out),
            (second_sum, second_out),
            (own_sum, own_out),
            (prev_sum, prev_out),
            (pot, pot_out),
            (lanes, lanes_out),
        ),
        sems,
    )
    begin_copies(sends)
    wait(sends)


def row_pass(left, right, prev_low, prev_high, own, back, first, second, block):
    lines_here, seg_len, channels = left.shape
    bf16, f32 = jnp.bfloat16, jnp.float32
    part = (own.shape, f32)
    marginal = ((lines_here, seg_len), f32)
    pot = ((lines_here, 2 * seg_len), f32)
    lanes = (left.shape, bf16)
    return kernel_call(
        functools.partial(row_kernel, block),
        (left, right, prev_low, prev_high, own, back, first, second),
        (pot, lanes) + (marginal,) * 4,
        ((left.shape, bf16), ((lines_here, 2 * seg_len, channels), bf16))
        + (part,) * 4
        + (pot, lanes)
        + (marginal,) * 4
        + (
            ((2 * seg_len, channels), bf16),
            ((8, 2 * seg_len), f32),
            ((2, 2 * block, seg_len + 2 * block), f32),
        ),
        (4 * lines_here, 6),
        "row_pass",
    )


def transport_kernel(
    block,
    pot_in,
    lanes_in,
    left_in,
    right_in,
    prev_low_in,
    prev_high_in,
    own_in,
    back_in,
    first_in,
    second_in,
    state_out,
    disp_out,
    first_out,
    last_out,
    first_px_out,
    second_px_out,
    pot,
    lanes,
    left,
    ext,
    own,
    back,
    first_part,
    second_part,
    state,
    disp,
    first_px,
    second_px,
    pot_lanes,
    marks,
    raw,
    weights,
    line_sems,
    sems,
    send_sems,
):
    lines_here, seg_len, channels = left.shape
    layers = first_out.shape[0]
    scale = log2_scale(channels)
    big = 2 * block
    window = seg_len + big
    fetches = copies_of(
        (
            (pot_in, pot),
            (own_in, own),
            (back_in, back),
            (first_in, first_part),
            (second_in, second_part),
        ),
        sems,
    )
    begin_copies(fetches)
    pairs = feature_pairs(left_in, right_in, prev_low_in, prev_high_in, left, ext) + (
        (lanes_in, lanes),
    )
    for line in range(lines_here):
        begin_copies(line_copies(pairs, line_sems, line, lines_here))
    lane = lax.broadcasted_iota(jnp.int32, (window, channels), 1)
    distance = seg_len - lax.broadcasted_iota(jnp.int32, (window, channels), 0)
    fine = jnp.bitwise_and(distance, 15)
    values = jnp.where(
        lane == 0,
        1,
        jnp.where(lane == 1, distance - fine, jnp.where(lane == 2, fine, 0)),
    )
    marks[...] = values.astype(jnp.float32).astype(jnp.bfloat16)
    wait(fetches)
    following, before = by_parity(first_part[...], second_part[...])
    total = jnp.concatenate([before + back[...], own[...] + following], axis=1)
    final = jnp.where(total > 0, pot[...] - jnp.log2(total), NEG)
    pot_lanes[...] = potential_lanes(final * (1.0 / scale), channels)
    offsets = lax.broadcasted_iota(jnp.int32, (1, big), 1).astype(jnp.float32)
    corner = jnp.zeros((block, block), jnp.bfloat16)
    steps = seg_len // big

    def one_line(line, carry):
        wait(line_copies(pairs, line_sems, line, lines_here))

        def score(index):
            first = index * big
            rows, reach = slice(first, first + big), slice(first, first + window)
            raw[index % 2] = scores_of(
                jnp.concatenate([left[line, rows], lanes[line, rows]], axis=1),
                jnp.concatenate([ext[line, reach], pot_lanes[reach]], axis=1),
            )

        def weigh(index):
            slot = index % 2
            upper = jnp.exp2(banded(raw[slot, :block, : window - block], 0, block) * scale)
            lower = jnp.exp2(banded(raw[slot, block:, block:], 0, block) * scale)
            weights[slot, :block, : window - block] = upper.astype(jnp.bfloat16)
            weights[slot, :block, window - block :] = corner
            weights[slot, block:, block:] = lower.astype(jnp.bfloat16)
            weights[slot, block:, :block] = corner

        def gather(index):
            first = index * big
            rows = slice(first, first + big)
            table = jnp.concatenate([ext[line, first : first + window], marks[...]], axis=1)
            result = jnp.dot(weights[index % 2], table, preferred_element_type=jnp.float32)
            matched = result[:, :channels] * (1.0 / result[:, channels : channels + 1])
            state[line, rows] = (matched - left[line, rows].astype(jnp.float32)).astype(
                state.dtype
            )
            moments = result[:, channels:].T
            return offsets + (moments[1:2] + moments[2:3]) / moments[0:1]

        disparity = []
        for index in range(steps + 2):
            if index < steps:
                score(index)
            if index >= 2:
                disparity.append(gather(index - 2))
            if 1 <= index <= steps:
                weigh(index - 1)
        disp[pl.ds(line, 1), :] = jnp.concatenate(disparity, axis=1)
        begin_copies(line_copies(((state, state_out),), send_sems, line, lines_here))
        high = state[line, seg_len - EDGE :].astype(jnp.float32)
        first, second = by_parity(high, state[line, :EDGE].astype(jnp.float32))
        first_px[line] = first.astype(jnp.bfloat16)
        second_px[line] = second.astype(jnp.bfloat16)

        @pl.when(line < layers)
        def _():
            pltpu.make_async_copy(state.at[line], first_out.at[line], sems.at[line]).start()

        @pl.when(line >= lines_here - layers)
        def _():
            target = line - (lines_here - layers)
            pltpu.make_async_copy(
                state.at[line], last_out.at[target], sems.at[layers + target]
            ).start()

        return carry

    lax.fori_loop(0, lines_here, one_line, 0)
    sends = copies_of(
        ((first_px, first_px_out), (second_px, second_px_out), (disp, disp_out)),
        send_sems.at[pl.ds(lines_here, 3)],
    )
    begin_copies(sends)
    for line in range(layers):
        pltpu.make_async_copy(state.at[line], first_out.at[line], sems.at[line]).wait()
        source = line + lines_here - layers
        pltpu.make_async_copy(state.at[source], last_out.at[line], sems.at[layers + line]).wait()
    for line in range(lines_here):
        wait(line_copies(((state, state_out),), send_sems, line, lines_here))
    wait(sends)


def transport(pot, lanes, left, right, prev_low, prev_high, own, back, first, second, block, layers):
    lines_here, seg_len, channels = left.shape
    bf16, f32 = jnp.bfloat16, jnp.float32
    edge = ((layers, seg_len, channels), bf16)
    side = ((lines_here, EDGE, channels), bf16)
    state = (left.shape, bf16)
    marginal = ((lines_here, seg_len), f32)
    window = seg_len + 2 * block
    return kernel_call(
        functools.partial(transport_kernel, block),
        (pot, lanes, left, right, prev_low, prev_high, own, back, first, second),
        (state, marginal, edge, edge, side, side),
        ((pot.shape, f32), (lanes.shape, bf16), state)
        + (((lines_here, 2 * seg_len, channels), bf16),)
        + (marginal,) * 4
        + (state, marginal, side, side)
        + (
            ((2 * seg_len, channels), bf16),
            ((window, channels), bf16),
            ((2, 2 * block, window), f32),
            ((2, 2 * block, window), bf16),
        ),
        (5 * lines_here, max(5, 2 * layers), lines_here + 3),
        "transport",
    )


def stack_weights(weight_ref, stacked_ref):
    layers, taps, _, channels, _ = weight_ref.shape
    zeros = jnp.zeros((channels, channels), stacked_ref.dtype)
    for layer in range(layers):
        for col_tap in range(taps):
            for line in range(taps + 1):
                row = (col_tap * (taps + 1) + line) * channels
                for out in range(2):
                    row_tap = line - out
                    stacked_ref[
                        layer, row : row + channels, out * channels : (out + 1) * channels
                    ] = weight_ref[layer, row_tap, col_tap] if 0 <= row_tap < taps else zeros


def conv_kernel(
    state_in,
    top_in,
    bottom_in,
    first_in,
    second_in,
    corner_top_in,
    corner_bottom_in,
    weight_in,
    bias_in,
    result_out,
    state_ref,
    top_ref,
    bottom_ref,
    first_ref,
    second_ref,
    corner_top_ref,
    corner_bottom_ref,
    weight_ref,
    bias_ref,
    out_ref,
    first_image,
    second_image,
    sems,
    send_sems,
):
    fetches = copies_of(
        (
            (state_in, state_ref),
            (first_in, first_ref),
            (second_in, second_ref),
            (corner_top_in, corner_top_ref),
            (corner_bottom_in, corner_bottom_ref),
            (top_in, top_ref),
            (bottom_in, bottom_ref),
            (weight_in, weight_ref),
            (bias_in, bias_ref),
        ),
        sems,
    )
    begin_copies(fetches)
    lines_here, seg_len, channels = state_ref.shape
    layers = weight_ref.shape[0]
    after = layers + lines_here
    right = EDGE + seg_len
    f32 = jnp.float32
    wait(fetches[:1])
    first_image[layers:after, EDGE:right] = state_ref[...].astype(f32)
    wait(fetches[1:])
    first_image[:layers, EDGE:right] = top_ref[...].astype(f32)
    first_image[after:, EDGE:right] = bottom_ref[...].astype(f32)
    for rows, first_px, second_px in (
        (slice(layers, after), first_ref[...], second_ref[...]),
        (slice(0, layers), corner_top_ref[:, :EDGE], corner_top_ref[:, EDGE:]),
        (slice(after, None), corner_bottom_ref[:, :EDGE], corner_bottom_ref[:, EDGE:]),
    ):
        following, before = by_parity(first_px.astype(f32), second_px.astype(f32))
        first_image[rows, :EDGE] = before
        first_image[rows, right:] = following
    line0 = lax.axis_index("lines") * lines_here - layers
    all_lines = lax.axis_size("lines") * lines_here
    px0 = lax.axis_index("seg") * seg_len - EDGE
    all_px = lax.axis_size("seg") * seg_len
    source, target = first_image, second_image
    for layer in range(layers):
        reach = layers - 1 - layer
        begin, end = (EDGE // 2, right + EDGE // 2) if reach else (EDGE, right)
        pieces = 5 if reach else 4
        size = (end - begin) // pieces

        def pair(index, carry, layer=layer, reach=reach, begin=begin, pieces=pieces, size=size, source=source, target=target):
            base = layer + 2 * index
            for piece in range(pieces):
                start = begin + piece * size
                taps = [
                    source[base + line, start + col_tap - 1 : start + col_tap - 1 + size].astype(jnp.bfloat16)
                    for col_tap in range(3)
                    for line in range(4)
                ]
                total = jnp.dot(
                    jnp.concatenate(taps, axis=1), weight_ref[layer], preferred_element_type=f32
                )
                for out in range(2):
                    line = base + 1 + out
                    part = total[:, out * channels : (out + 1) * channels] + bias_ref[layer : layer + 1]
                    updated = source[line, start : start + size] + jnp.maximum(part, 0.0)
                    if not reach:
                        out_ref[line - layers, start - EDGE : start - EDGE + size] = updated.astype(out_ref.dtype)
                        continue
                    image_line = line0 + line
                    inside = (image_line >= 0) & (image_line < all_lines)
                    if piece in (0, pieces - 1):
                        px = px0 + start + lax.broadcasted_iota(jnp.int32, updated.shape, 0)
                        inside = inside & (px >= 0) & (px < all_px)
                    updated = jnp.where(inside, updated, 0.0)
                    target[line, start : start + size] = updated.astype(jnp.bfloat16).astype(f32)
            if not reach:
                for line in (base + 1, base + 2):
                    begin_copies(line_copies(((out_ref, result_out),), send_sems, line - layers, lines_here))
            return carry

        lax.fori_loop(0, (lines_here + 2 * reach) // 2, pair, 0)
        source, target = target, source
    for line in range(lines_here):
        wait(line_copies(((out_ref, result_out),), send_sems, line, lines_here))


def conv_layers(state, top, bottom, left_px, right_px, corners_top, corners_bottom, weight, bias):
    layers = weight.shape[0]
    lines_here, seg_len, channels = state.shape
    image = ((lines_here + 2 * layers, seg_len + 2 * EDGE, channels), jnp.float32)
    operands = (state, top, bottom, left_px, right_px, corners_top, corners_bottom, weight, bias)
    result = (state.shape, state.dtype)
    return kernel_call(
        conv_kernel,
        operands,
        (result,),
        tuple((operand.shape, operand.dtype) for operand in operands) + (result, image, image),
        (len(operands), lines_here),
        "conv_layers",
    )[0]


def shards(left_features, right_features, conv_weight, conv_bias):
    seg_len = left_features.shape[1]
    half = seg_len // 2
    layers = conv_weight.shape[0]
    prev_high = shifted(right_features[:, half:], "seg", 1)
    next_low = shifted(left_features[:, :half], "seg", -1)
    prev_low = shifted(right_features[:, :half], "seg", 1)
    stacked, own = own_partials(left_features, right_features, conv_weight)
    own = next_partials(next_low, right_features, own)
    back, first, second = cross_partials(left_features, prev_high, own)
    first = exchanged(first, "seg", 0)
    second = exchanged(second, "seg", 1)
    block = min(128, half)
    pot, lanes, own, back, first, second = row_pass(
        left_features, right_features, prev_low, prev_high, own, back, first, second, block
    )
    first = exchanged(first, "seg", 0)
    second = exchanged(second, "seg", 1)
    state, disparity, first_lines, last_lines, first, second = transport(
        pot, lanes, left_features, right_features, prev_low, prev_high, own, back, first, second, block, layers
    )
    bottom = shifted(first_lines, "lines", -1)
    top = shifted(last_lines, "lines", 1)
    first = exchanged(first, "seg", 0)
    second = exchanged(second, "seg", 1)
    edges = jnp.concatenate([first, second], axis=1)
    corners_bottom = shifted(edges[:layers], "lines", -1)
    corners_top = shifted(edges[-layers:], "lines", 1)
    refined = conv_layers(
        state, top, bottom, first, second, corners_top, corners_bottom, stacked, conv_bias
    )
    return (refined, disparity)


def solution(mesh):
    return jax.shard_map(
        shards,
        mesh=mesh,
        in_specs=(P("lines", "seg", None), P("lines", "seg", None), P(), P()),
        out_specs=(P("lines", "seg", None), P("lines", "seg")),
        check_vma=False,
    )
```

```python
import functools
import math

import jax
import jax.numpy as jnp
from jax import lax
from jax.experimental import pallas as pl
from jax.experimental.pallas import tpu as pltpu
from jax.sharding import PartitionSpec as P

DISP = 1024
NEG = -1e30
EDGE = 16
VMEM_BYTES = 32 * 1024 * 1024


def shifted(block, axis, step):
    count = lax.axis_size(axis)
    route = [(i, i + step) for i in range(count) if 0 <= i + step < count]
    return lax.ppermute(block, axis, route)


def exchanged(block, axis, odd):
    route = []
    for low in range(odd, lax.axis_size(axis) - 1, 2):
        route += [(low, low + 1), (low + 1, low)]
    return lax.ppermute(block, axis, route)


def even_segment():
    return lax.rem(lax.axis_index("seg"), 2) == 0


def by_parity(following, previous):
    even = even_segment()
    return jnp.where(even, following, previous), jnp.where(even, previous, following)


def params():
    return pltpu.CompilerParams(vmem_limit_bytes=VMEM_BYTES)


ANYWHERE = pl.BlockSpec(memory_space=pl.ANY)


def kernel_call(kernel, operands, results, scratch, copies, name, cost=None):
    return pl.pallas_call(
        kernel,
        in_specs=[ANYWHERE] * len(operands),
        out_specs=[ANYWHERE] * len(results),
        out_shape=[jax.ShapeDtypeStruct(shape, dtype) for shape, dtype in results],
        scratch_shapes=[pltpu.VMEM(shape, dtype) for shape, dtype in scratch]
        + [pltpu.SemaphoreType.DMA((count,)) for count in copies],
        compiler_params=params(),
        cost_estimate=cost,
        name=name,
    )(*operands)


def copies_of(pairs, sems):
    return [
        pltpu.make_async_copy(source, target, sems.at[index])
        for index, (source, target) in enumerate(pairs)
    ]


def line_copies(pairs, sems, line, lines_here):
    return [
        pltpu.make_async_copy(source.at[line], target.at[line], sems.at[index * lines_here + line])
        for index, (source, target) in enumerate(pairs)
    ]


def begin_copies(copies):
    for copy in copies:
        copy.start()


def wait(copies):
    for copy in copies:
        copy.wait()


def scores_of(left, right):
    return lax.dot_general(
        left, right, (((1,), (1,)), ((), ())), preferred_element_type=jnp.float32
    )


def log2_scale(channels):
    return math.log2(math.e) / math.sqrt(channels)


def over_rows(reduce, values, chains=64):
    count, width = values.shape
    while count > chains >= 8 and count % chains == 0:
        values = reduce(values.reshape(count // chains, chains, width), axis=0)
        count, chains = chains, chains // 8
    return reduce(values, axis=0, keepdims=True)


def column_block(left, right, diagonal_first):
    block, channels = right.shape
    scale = log2_scale(channels)
    raw = scores_of(left, right)
    row_ids = lax.broadcasted_iota(jnp.int32, (block, block), 0)
    col_ids = lax.broadcasted_iota(jnp.int32, (block, block), 1)
    if diagonal_first:
        parts = [jnp.where(col_ids <= row_ids, raw[:block], NEG), raw[block:]]
    else:
        parts = [raw[:-block], jnp.where(col_ids > row_ids, raw[-block:], NEG)]
    parts = [part for part in parts if part.shape[0]]
    peak = functools.reduce(jnp.maximum, [over_rows(jnp.max, part) for part in parts])
    total = sum(over_rows(jnp.sum, jnp.exp2((part - peak) * scale)) for part in parts)
    return (peak * scale, total)


def own_kernel(
    block,
    left_in,
    right_in,
    weight_in,
    stacked_out,
    part_out,
    left,
    right,
    weight,
    stacked,
    part,
    line_sems,
    sems,
):
    lines_here, seg_len = left.shape[:2]
    pairs = ((left_in, left), (right_in, right))
    for line in range(lines_here):
        begin_copies(line_copies(pairs, line_sems, line, lines_here))
    fetch, send_stacked, send_part = copies_of(
        ((weight_in, weight), (stacked, stacked_out), (part, part_out)), sems
    )
    fetch.start()

    def one_line(line, carry):
        wait(line_copies(pairs, line_sems, line, lines_here))
        for first in range(0, seg_len, block):
            cols = slice(first, first + block)
            peak, total = column_block(left[line, first:], right[line, cols], True)
            part[pl.ds(line, 1), cols] = peak
            part[pl.ds(lines_here + line, 1), cols] = total
        return carry

    lax.fori_loop(0, lines_here, one_line, 0)
    send_part.start()
    fetch.wait()
    stack_weights(weight, stacked)
    send_stacked.start()
    send_part.wait()
    send_stacked.wait()


def column_cost(lines_here, seg_len, channels):
    return pl.CostEstimate(
        flops=2 * lines_here * seg_len * seg_len * channels,
        bytes_accessed=8 * lines_here * seg_len * channels,
        transcendentals=lines_here * seg_len * seg_len // 2,
    )


def own_partials(left, right, weight):
    lines_here, seg_len, channels = left.shape
    bf16, f32 = jnp.bfloat16, jnp.float32
    stacked = ((weight.shape[0], 12 * channels, 2 * channels), bf16)
    part = ((2 * lines_here, seg_len), f32)
    return kernel_call(
        functools.partial(own_kernel, min(256, seg_len)),
        (left, right, weight),
        (stacked, part),
        ((left.shape, bf16), (right.shape, bf16), (weight.shape, bf16), stacked, part),
        (2 * lines_here, 3),
        "column_own",
        column_cost(*left.shape),
    )


def next_kernel(
    block,
    next_in,
    right_in,
    own_in,
    back_in,
    merged_out,
    first_out,
    second_out,
    following,
    right,
    merged,
    back,
    first_part,
    second_part,
    line_sems,
    sems,
):
    lines_here, half = following.shape[:2]
    pairs = ((next_in, following), (right_in.at[:, pl.ds(0, half)], right))
    fetches = copies_of(((own_in, merged), (back_in, back)), sems)
    sends = copies_of(
        ((first_part, first_out), (second_part, second_out), (merged, merged_out)),
        sems.at[pl.ds(2, 3)],
    )
    begin_copies(fetches)
    for line in range(lines_here):
        begin_copies(line_copies(pairs, line_sems, line, lines_here))
    wait(fetches)
    last = lax.axis_index("seg") == lax.axis_size("seg") - 1

    def one_line(line, carry):
        wait(line_copies(pairs, line_sems, line, lines_here))
        top, bottom = pl.ds(line, 1), pl.ds(lines_here + line, 1)
        for first in range(0, half, block):
            cols = slice(first, first + block)
            peak, total = column_block(following[line, : first + block], right[line, cols], False)
            peak = jnp.where(last, NEG, peak)
            total = jnp.where(last, 0.0, total)
            own_peak = merged[top, cols]
            joint = jnp.maximum(own_peak, peak)
            merged[bottom, cols] = merged[bottom, cols] * jnp.exp2(
                own_peak - joint
            ) + total * jnp.exp2(peak - joint)
            merged[top, cols] = joint
        return carry

    lax.fori_loop(0, lines_here, one_line, 0)
    first_part[...], second_part[...] = by_parity(merged[...], back[...])
    begin_copies(sends)
    wait(sends)


def next_partials(next_low, right, own, back):
    lines_here, half, channels = next_low.shape
    part = (own.shape, jnp.float32)
    features = (next_low.shape, jnp.bfloat16)
    return kernel_call(
        functools.partial(next_kernel, min(256, half)),
        (next_low, right, own, back),
        (part,) * 3,
        (features, features) + (part,) * 4,
        (2 * lines_here, 5),
        "column_next",
        column_cost(lines_here, half, channels),
    )


def cross_kernel(block, left_in, prev_in, back_out, left, prev, back, line_sems, sems):
    lines_here, seg_len = left.shape[:2]
    half = seg_len - prev.shape[1]
    pairs = ((left_in, left), (prev_in, prev))
    for line in range(lines_here):
        begin_copies(line_copies(pairs, line_sems, line, lines_here))
    (send,) = copies_of(((back, back_out),), sems)
    back[...] = jnp.zeros_like(back)

    def one_line(line, carry):
        wait(line_copies(pairs, line_sems, line, lines_here))
        top, bottom = pl.ds(line, 1), pl.ds(lines_here + line, 1)
        for first in range(0, prev.shape[1], block):
            cols = slice(first, first + block)
            peak, total = column_block(
                left[line, : half + first + block], prev[line, cols], False
            )
            back[top, cols] = peak
            back[bottom, cols] = total
        return carry

    lax.fori_loop(0, lines_here, one_line, 0)
    send.start()
    send.wait()


def cross_partials(left, prev_high):
    lines_here, seg_len, channels = left.shape
    part = ((2 * lines_here, seg_len), jnp.float32)
    return kernel_call(
        functools.partial(cross_kernel, min(256, prev_high.shape[1])),
        (left, prev_high),
        (part,),
        ((left.shape, jnp.bfloat16), (prev_high.shape, jnp.bfloat16), part),
        (2 * lines_here, 1),
        "column_cross",
        column_cost(*left.shape),
    )[0]


def potential(peak, total):
    return -(peak + jnp.log2(total))


def merged_potential(first, second):
    first_max = jnp.where(first[1] > 0, first[0], NEG)
    second_max = jnp.where(second[1] > 0, second[0], NEG)
    peak = jnp.maximum(first_max, second_max)
    total = first[1] * jnp.exp2(first_max - peak) + second[1] * jnp.exp2(second_max - peak)
    return potential(peak, total)


def split(values, parts):
    pieces = []
    for _ in range(parts):
        piece = values.astype(jnp.bfloat16).astype(jnp.float32)
        pieces.append(piece)
        values = values - piece
    return pieces


SHIFT = 2


def potential_lanes(pot, channels):
    lines_here, count = pot.shape
    parts = split(pot, 3)
    filler = jnp.zeros((channels - 3 * lines_here, count), jnp.float32)
    lanes = jnp.concatenate(parts + [filler], axis=0).T
    lane = lax.broadcasted_iota(jnp.int32, lanes.shape, 1)
    return jnp.where(lane >= channels - SHIFT, -1.0, lanes).astype(jnp.bfloat16)


def line_lanes(line, lines_here, shape):
    lane = lax.broadcasted_iota(jnp.int32, shape, 1)
    mine = jnp.zeros(shape, jnp.float32)
    for part in range(3):
        mine = jnp.where(lane == part * lines_here + line, 1.0, mine)
    return mine


def banded(values, row, block):
    rows, window = values.shape
    col_ids = lax.broadcasted_iota(jnp.int32, (rows, block), 1)
    row_ids = lax.broadcasted_iota(jnp.int32, (rows, block), 0) + row
    return jnp.concatenate(
        [
            jnp.where(col_ids > row_ids, values[:, :block], NEG),
            values[:, block : window - block],
            jnp.where(col_ids <= row_ids, values[:, window - block :], NEG),
        ],
        axis=1,
    )


def feature_pairs(left_in, right_in, prev_low_in, prev_high_in, left, ext):
    seg_len, half = left.shape[1], prev_low_in.shape[1]
    return (
        (left_in, left),
        (prev_low_in, ext.at[:, pl.ds(0, half)]),
        (prev_high_in, ext.at[:, pl.ds(half, seg_len - half)]),
        (right_in, ext.at[:, pl.ds(seg_len, seg_len)]),
    )


def row_kernel(
    block,
    left_in,
    right_in,
    prev_low_in,
    prev_high_in,
    own_in,
    back_in,
    first_in,
    second_in,
    pot_out,
    lanes_out,
    own_out,
    prev_out,
    first_out,
    second_out,
    left,
    ext,
    own,
    back,
    first_part,
    second_part,
    pot,
    lanes,
    own_sum,
    prev_sum,
    first_sum,
    second_sum,
    pot_lanes,
    sums,
    raw,
    line_sems,
    sems,
):
    lines_here, seg_len, channels = left.shape
    half = prev_low_in.shape[1]
    scale = log2_scale(channels)
    fetches = copies_of(
        ((own_in, own), (back_in, back), (first_in, first_part), (second_in, second_part)), sems
    )
    begin_copies(fetches)
    pairs = feature_pairs(left_in, right_in, prev_low_in, prev_high_in, left, ext)
    for line in range(lines_here):
        begin_copies(line_copies(pairs, line_sems, line, lines_here))
    wait(fetches)

    following, before = by_parity(first_part[...], second_part[...])

    def parts(part, first, stop):
        return part[:lines_here, first:stop], part[lines_here:, first:stop]

    rest = seg_len - half
    pot[:, seg_len : seg_len + half] = potential(*parts(own, 0, half))
    pot[:, seg_len + half :] = merged_potential(
        parts(own, half, seg_len), parts(following, 0, rest)
    )
    low = parts(before, 0, half)
    high = parts(before, half, seg_len)
    pot[:, :half] = jnp.where(low[1] > 0, potential(*low), NEG)
    pot[:, half:seg_len] = jnp.where(
        high[1] > 0, merged_potential(high, parts(back, 0, rest)), NEG
    )
    pot_lanes[...] = potential_lanes(pot[...] * (1.0 / scale), channels)
    window = seg_len + block
    big = 2 * block
    steps = seg_len // big
    strip = 16
    lane = lax.broadcasted_iota(jnp.int32, (strip, channels), 1)

    def one_line(line, carry):
        wait(line_copies(pairs, line_sems, line, lines_here))
        sums[...] = jnp.zeros_like(sums)
        mine = line_lanes(line, lines_here, (big, channels)).astype(jnp.bfloat16)
        strip_lanes = line_lanes(line, lines_here, (strip, channels))

        def score(index):
            first = index * big
            reach = slice(first, first + seg_len + big)
            raw[index % 2] = scores_of(
                jnp.concatenate([left[line, first : first + big], mine], axis=1),
                jnp.concatenate([ext[line, reach], pot_lanes[reach]], axis=1),
            )

        score(0)
        for index in range(steps):
            slot = index % 2
            if index + 1 < steps:
                score(index + 1)
            for side in range(2):
                shift = side * block
                first = index * big + shift
                column_sum = jnp.zeros((8, window), jnp.float32)
                for row in range(0, block, strip):
                    rows = slice(shift + row, shift + row + strip)
                    logits = banded(raw[slot, rows, shift : shift + window], row, block)
                    peak = jnp.max(logits, axis=1, keepdims=True)
                    terms = jnp.exp2((logits - peak) * scale)
                    plan = terms * (1.0 / jnp.sum(terms, axis=1, keepdims=True))
                    column_sum += plan[:8] + plan[8:]
                    marked = strip_lanes
                    for part, piece in enumerate(split(peak, SHIFT)):
                        marked = jnp.where(lane == channels - SHIFT + part, piece, marked)
                    lanes[line, first + row : first + row + strip] = marked.astype(jnp.bfloat16)
                sums[:, first : first + window] += column_sum
        totals = jnp.sum(sums[...], axis=0, keepdims=True)
        prev_sum[pl.ds(line, 1), :] = totals[:, :seg_len]
        own_sum[pl.ds(line, 1), :] = totals[:, seg_len:]
        return carry

    lax.fori_loop(0, lines_here, one_line, 0)
    first_sum[...], second_sum[...] = by_parity(own_sum[...], prev_sum[...])
    sends = copies_of(
        (
            (first_sum, first_out),
            (second_sum, second_out),
            (own_sum, own_out),
            (prev_sum, prev_out),
            (pot, pot_out),
            (lanes, lanes_out),
        ),
        sems,
    )
    begin_copies(sends)
    wait(sends)


def row_pass(left, right, prev_low, prev_high, own, back, first, second, block):
    lines_here, seg_len, channels = left.shape
    bf16, f32 = jnp.bfloat16, jnp.float32
    part = (own.shape, f32)
    marginal = ((lines_here, seg_len), f32)
    pot = ((lines_here, 2 * seg_len), f32)
    lanes = (left.shape, bf16)
    return kernel_call(
        functools.partial(row_kernel, block),
        (left, right, prev_low, prev_high, own, back, first, second),
        (pot, lanes) + (marginal,) * 4,
        ((left.shape, bf16), ((lines_here, 2 * seg_len, channels), bf16))
        + (part,) * 4
        + (pot, lanes)
        + (marginal,) * 4
        + (
            ((2 * seg_len, channels), bf16),
            ((8, 2 * seg_len), f32),
            ((2, 2 * block, seg_len + 2 * block), f32),
        ),
        (4 * lines_here, 6),
        "row_pass",
    )


def transport_kernel(
    block,
    pot_in,
    lanes_in,
    left_in,
    right_in,
    prev_low_in,
    prev_high_in,
    own_in,
    back_in,
    first_in,
    second_in,
    state_out,
    disp_out,
    first_out,
    last_out,
    first_px_out,
    second_px_out,
    pot,
    lanes,
    left,
    ext,
    own,
    back,
    first_part,
    second_part,
    state,
    disp,
    first_px,
    second_px,
    pot_lanes,
    marks,
    raw,
    weights,
    line_sems,
    sems,
    send_sems,
):
    lines_here, seg_len, channels = left.shape
    layers = first_out.shape[0]
    scale = log2_scale(channels)
    big = 2 * block
    window = seg_len + big
    fetches = copies_of(
        (
            (pot_in, pot),
            (own_in, own),
            (back_in, back),
            (first_in, first_part),
            (second_in, second_part),
        ),
        sems,
    )
    begin_copies(fetches)
    pairs = feature_pairs(left_in, right_in, prev_low_in, prev_high_in, left, ext) + (
        (lanes_in, lanes),
    )
    for line in range(lines_here):
        begin_copies(line_copies(pairs, line_sems, line, lines_here))
    lane = lax.broadcasted_iota(jnp.int32, (window, channels), 1)
    distance = seg_len - lax.broadcasted_iota(jnp.int32, (window, channels), 0)
    fine = jnp.bitwise_and(distance, 15)
    values = jnp.where(
        lane == 0,
        1,
        jnp.where(lane == 1, distance - fine, jnp.where(lane == 2, fine, 0)),
    )
    marks[...] = values.astype(jnp.float32).astype(jnp.bfloat16)
    wait(fetches)
    following, before = by_parity(first_part[...], second_part[...])
    total = jnp.concatenate([before + back[...], own[...] + following], axis=1)
    final = jnp.where(total > 0, pot[...] - jnp.log2(total), NEG)
    pot_lanes[...] = potential_lanes(final * (1.0 / scale), channels)
    offsets = lax.broadcasted_iota(jnp.int32, (1, big), 1).astype(jnp.float32)
    corner = jnp.zeros((block, block), jnp.bfloat16)
    steps = seg_len // big

    def one_line(line, carry):
        wait(line_copies(pairs, line_sems, line, lines_here))

        def score(index):
            first = index * big
            rows, reach = slice(first, first + big), slice(first, first + window)
            raw[index % 2] = scores_of(
                jnp.concatenate([left[line, rows], lanes[line, rows]], axis=1),
                jnp.concatenate([ext[line, reach], pot_lanes[reach]], axis=1),
            )

        def weigh(index):
            slot = index % 2
            upper = jnp.exp2(banded(raw[slot, :block, : window - block], 0, block) * scale)
            lower = jnp.exp2(banded(raw[slot, block:, block:], 0, block) * scale)
            weights[slot, :block, : window - block] = upper.astype(jnp.bfloat16)
            weights[slot, :block, window - block :] = corner
            weights[slot, block:, block:] = lower.astype(jnp.bfloat16)
            weights[slot, block:, :block] = corner

        def gather(index):
            first = index * big
            rows = slice(first, first + big)
            table = jnp.concatenate([ext[line, first : first + window], marks[...]], axis=1)
            result = jnp.dot(weights[index % 2], table, preferred_element_type=jnp.float32)
            matched = result[:, :channels] * (1.0 / result[:, channels : channels + 1])
            state[line, rows] = (matched - left[line, rows].astype(jnp.float32)).astype(
                state.dtype
            )
            moments = result[:, channels:].T
            return offsets + (moments[1:2] + moments[2:3]) / moments[0:1]

        disparity = []
        for index in range(steps + 2):
            if index < steps:
                score(index)
            if index >= 2:
                disparity.append(gather(index - 2))
            if 1 <= index <= steps:
                weigh(index - 1)
        disp[pl.ds(line, 1), :] = jnp.concatenate(disparity, axis=1)
        begin_copies(line_copies(((state, state_out),), send_sems, line, lines_here))
        high = state[line, seg_len - EDGE :].astype(jnp.float32)
        first, second = by_parity(high, state[line, :EDGE].astype(jnp.float32))
        first_px[line] = first.astype(jnp.bfloat16)
        second_px[line] = second.astype(jnp.bfloat16)

        @pl.when(line < layers)
        def _():
            pltpu.make_async_copy(state.at[line], first_out.at[line], sems.at[line]).start()

        @pl.when(line >= lines_here - layers)
        def _():
            target = line - (lines_here - layers)
            pltpu.make_async_copy(
                state.at[line], last_out.at[target], sems.at[layers + target]
            ).start()

        return carry

    lax.fori_loop(0, lines_here, one_line, 0)
    sends = copies_of(
        ((first_px, first_px_out), (second_px, second_px_out), (disp, disp_out)),
        send_sems.at[pl.ds(lines_here, 3)],
    )
    begin_copies(sends)
    for line in range(layers):
        pltpu.make_async_copy(state.at[line], first_out.at[line], sems.at[line]).wait()
        source = line + lines_here - layers
        pltpu.make_async_copy(state.at[source], last_out.at[line], sems.at[layers + line]).wait()
    for line in range(lines_here):
        wait(line_copies(((state, state_out),), send_sems, line, lines_here))
    wait(sends)


def transport(pot, lanes, left, right, prev_low, prev_high, own, back, first, second, block, layers):
    lines_here, seg_len, channels = left.shape
    bf16, f32 = jnp.bfloat16, jnp.float32
    edge = ((layers, seg_len, channels), bf16)
    side = ((lines_here, EDGE, channels), bf16)
    state = (left.shape, bf16)
    marginal = ((lines_here, seg_len), f32)
    window = seg_len + 2 * block
    return kernel_call(
        functools.partial(transport_kernel, block),
        (pot, lanes, left, right, prev_low, prev_high, own, back, first, second),
        (state, marginal, edge, edge, side, side),
        ((pot.shape, f32), (lanes.shape, bf16), state)
        + (((lines_here, 2 * seg_len, channels), bf16),)
        + (marginal,) * 4
        + (state, marginal, side, side)
        + (
            ((2 * seg_len, channels), bf16),
            ((window, channels), bf16),
            ((2, 2 * block, window), f32),
            ((2, 2 * block, window), bf16),
        ),
        (5 * lines_here, max(5, 2 * layers), lines_here + 3),
        "transport",
    )


def stack_weights(weight_ref, stacked_ref):
    layers, taps, _, channels, _ = weight_ref.shape
    zeros = jnp.zeros((channels, channels), stacked_ref.dtype)
    for layer in range(layers):
        for col_tap in range(taps):
            for line in range(taps + 1):
                row = (col_tap * (taps + 1) + line) * channels
                for out in range(2):
                    row_tap = line - out
                    stacked_ref[
                        layer, row : row + channels, out * channels : (out + 1) * channels
                    ] = weight_ref[layer, row_tap, col_tap] if 0 <= row_tap < taps else zeros


def conv_kernel(
    state_in,
    top_in,
    bottom_in,
    first_in,
    second_in,
    corner_top_in,
    corner_bottom_in,
    weight_in,
    bias_in,
    result_out,
    state_ref,
    top_ref,
    bottom_ref,
    first_ref,
    second_ref,
    corner_top_ref,
    corner_bottom_ref,
    weight_ref,
    bias_ref,
    out_ref,
    first_image,
    second_image,
    sems,
    send_sems,
):
    fetches = copies_of(
        (
            (state_in, state_ref),
            (first_in, first_ref),
            (second_in, second_ref),
            (corner_top_in, corner_top_ref),
            (corner_bottom_in, corner_bottom_ref),
            (top_in, top_ref),
            (bottom_in, bottom_ref),
            (weight_in, weight_ref),
            (bias_in, bias_ref),
        ),
        sems,
    )
    begin_copies(fetches)
    lines_here, seg_len, channels = state_ref.shape
    layers = weight_ref.shape[0]
    after = layers + lines_here
    right = EDGE + seg_len
    f32 = jnp.float32
    wait(fetches[:1])
    first_image[layers:after, EDGE:right] = state_ref[...].astype(f32)
    wait(fetches[1:])
    first_image[:layers, EDGE:right] = top_ref[...].astype(f32)
    first_image[after:, EDGE:right] = bottom_ref[...].astype(f32)
    for rows, first_px, second_px in (
        (slice(layers, after), first_ref[...], second_ref[...]),
        (slice(0, layers), corner_top_ref[:, :EDGE], corner_top_ref[:, EDGE:]),
        (slice(after, None), corner_bottom_ref[:, :EDGE], corner_bottom_ref[:, EDGE:]),
    ):
        following, before = by_parity(first_px.astype(f32), second_px.astype(f32))
        first_image[rows, :EDGE] = before
        first_image[rows, right:] = following
    line0 = lax.axis_index("lines") * lines_here - layers
    all_lines = lax.axis_size("lines") * lines_here
    px0 = lax.axis_index("seg") * seg_len - EDGE
    all_px = lax.axis_size("seg") * seg_len
    source, target = first_image, second_image
    for layer in range(layers):
        reach = layers - 1 - layer
        begin, end = (EDGE // 2, right + EDGE // 2) if reach else (EDGE, right)
        middle = begin + seg_len // 2
        pieces = ((begin, middle), (middle, end))

        def pair(index, carry, layer=layer, reach=reach, pieces=pieces, source=source, target=target):
            base = layer + 2 * index
            for start, stop in pieces:
                size = stop - start
                taps = [
                    source[base + line, start + col_tap - 1 : start + col_tap - 1 + size].astype(jnp.bfloat16)
                    for col_tap in range(3)
                    for line in range(4)
                ]
                total = jnp.dot(
                    jnp.concatenate(taps, axis=1), weight_ref[layer], preferred_element_type=f32
                )
                for out in range(2):
                    line = base + 1 + out
                    part = total[:, out * channels : (out + 1) * channels] + bias_ref[layer : layer + 1]
                    updated = source[line, start : start + size] + jnp.maximum(part, 0.0)
                    if not reach:
                        out_ref[line - layers, start - EDGE : start - EDGE + size] = updated.astype(out_ref.dtype)
                        continue
                    image_line = line0 + line
                    inside = (image_line >= 0) & (image_line < all_lines)
                    if reach:
                        px = px0 + start + lax.broadcasted_iota(jnp.int32, updated.shape, 0)
                        inside = inside & (px >= 0) & (px < all_px)
                    updated = jnp.where(inside, updated, 0.0)
                    target[line, start : start + size] = updated.astype(jnp.bfloat16).astype(f32)
            if not reach:
                for line in (base + 1, base + 2):
                    begin_copies(line_copies(((out_ref, result_out),), send_sems, line - layers, lines_here))
            return carry

        lax.fori_loop(0, (lines_here + 2 * reach) // 2, pair, 0)
        source, target = target, source
    for line in range(lines_here):
        wait(line_copies(((out_ref, result_out),), send_sems, line, lines_here))


def conv_layers(state, top, bottom, left_px, right_px, corners_top, corners_bottom, weight, bias):
    layers = weight.shape[0]
    lines_here, seg_len, channels = state.shape
    image = ((lines_here + 2 * layers, seg_len + 2 * EDGE, channels), jnp.float32)
    operands = (state, top, bottom, left_px, right_px, corners_top, corners_bottom, weight, bias)
    result = (state.shape, state.dtype)
    return kernel_call(
        conv_kernel,
        operands,
        (result,),
        tuple((operand.shape, operand.dtype) for operand in operands) + (result, image, image),
        (len(operands), lines_here),
        "conv_layers",
    )[0]


def shards(left_features, right_features, conv_weight, conv_bias):
    seg_len = left_features.shape[1]
    half = seg_len // 2
    layers = conv_weight.shape[0]
    prev_high = shifted(right_features[:, half:], "seg", 1)
    next_low = shifted(left_features[:, :half], "seg", -1)
    stacked, own = own_partials(left_features, right_features, conv_weight)
    right_low, own = lax.optimization_barrier((right_features[:, :half], own))
    prev_low = shifted(right_low, "seg", 1)
    back = cross_partials(left_features, prev_high)
    own, first, second = next_partials(next_low, right_features, own, back)
    first = exchanged(first, "seg", 0)
    second = exchanged(second, "seg", 1)
    block = min(128, half)
    pot, lanes, own, back, first, second = row_pass(
        left_features, right_features, prev_low, prev_high, own, back, first, second, block
    )
    first = exchanged(first, "seg", 0)
    second = exchanged(second, "seg", 1)
    state, disparity, first_lines, last_lines, first, second = transport(
        pot, lanes, left_features, right_features, prev_low, prev_high, own, back, first, second, block, layers
    )
    bottom = shifted(first_lines, "lines", -1)
    top = shifted(last_lines, "lines", 1)
    first = exchanged(first, "seg", 0)
    second = exchanged(second, "seg", 1)
    edges = jnp.concatenate([first, second], axis=1)
    corners_bottom = shifted(edges[:layers], "lines", -1)
    corners_top = shifted(edges[-layers:], "lines", 1)
    refined = conv_layers(
        state, top, bottom, first, second, corners_top, corners_bottom, stacked, conv_bias
    )
    return (refined, disparity)


def solution(mesh):
    return jax.shard_map(
        shards,
        mesh=mesh,
        in_specs=(P("lines", "seg", None), P("lines", "seg", None), P(), P()),
        out_specs=(P("lines", "seg", None), P("lines", "seg")),
        check_vma=False,
    )
```

```python
import functools
import math

import jax
import jax.numpy as jnp
from jax import lax
from jax.experimental import pallas as pl
from jax.experimental.pallas import tpu as pltpu
from jax.sharding import PartitionSpec as P

DISP = 1024
NEG = -1e30
EDGE = 16
VMEM_BYTES = 32 * 1024 * 1024


def shifted(block, axis, step):
    count = lax.axis_size(axis)
    route = [(i, i + step) for i in range(count) if 0 <= i + step < count]
    return lax.ppermute(block, axis, route)


def exchanged(block, axis, odd):
    route = []
    for low in range(odd, lax.axis_size(axis) - 1, 2):
        route += [(low, low + 1), (low + 1, low)]
    return lax.ppermute(block, axis, route)


def even_segment():
    return lax.rem(lax.axis_index("seg"), 2) == 0


def by_parity(following, previous):
    even = even_segment()
    return jnp.where(even, following, previous), jnp.where(even, previous, following)


def params():
    return pltpu.CompilerParams(vmem_limit_bytes=VMEM_BYTES)


ANYWHERE = pl.BlockSpec(memory_space=pl.ANY)


def kernel_call(kernel, operands, results, scratch, copies, name, cost=None):
    return pl.pallas_call(
        kernel,
        in_specs=[ANYWHERE] * len(operands),
        out_specs=[ANYWHERE] * len(results),
        out_shape=[jax.ShapeDtypeStruct(shape, dtype) for shape, dtype in results],
        scratch_shapes=[pltpu.VMEM(shape, dtype) for shape, dtype in scratch]
        + [pltpu.SemaphoreType.DMA((count,)) for count in copies],
        compiler_params=params(),
        cost_estimate=cost,
        name=name,
    )(*operands)


def copies_of(pairs, sems):
    return [
        pltpu.make_async_copy(source, target, sems.at[index])
        for index, (source, target) in enumerate(pairs)
    ]


def line_copies(pairs, sems, line, lines_here):
    return [
        pltpu.make_async_copy(source.at[line], target.at[line], sems.at[index * lines_here + line])
        for index, (source, target) in enumerate(pairs)
    ]


def begin_copies(copies):
    for copy in copies:
        copy.start()


def wait(copies):
    for copy in copies:
        copy.wait()


def scores_of(left, right):
    return lax.dot_general(
        left, right, (((1,), (1,)), ((), ())), preferred_element_type=jnp.float32
    )


def log2_scale(channels):
    return math.log2(math.e) / math.sqrt(channels)


def over_rows(reduce, values, chains=64):
    count, width = values.shape
    while count > chains >= 8 and count % chains == 0:
        values = reduce(values.reshape(count // chains, chains, width), axis=0)
        count, chains = chains, chains // 8
    return reduce(values, axis=0, keepdims=True)


def column_block(left, right, diagonal_first):
    block, channels = right.shape
    scale = log2_scale(channels)
    raw = scores_of(left, right)
    row_ids = lax.broadcasted_iota(jnp.int32, (block, block), 0)
    col_ids = lax.broadcasted_iota(jnp.int32, (block, block), 1)
    if diagonal_first:
        parts = [jnp.where(col_ids <= row_ids, raw[:block], NEG), raw[block:]]
    else:
        parts = [raw[:-block], jnp.where(col_ids > row_ids, raw[-block:], NEG)]
    parts = [part for part in parts if part.shape[0]]
    peak = functools.reduce(jnp.maximum, [over_rows(jnp.max, part) for part in parts])
    total = sum(over_rows(jnp.sum, jnp.exp2((part - peak) * scale)) for part in parts)
    return (peak * scale, total)


def own_kernel(
    block,
    left_in,
    right_in,
    weight_in,
    stacked_out,
    part_out,
    left,
    right,
    weight,
    stacked,
    part,
    line_sems,
    sems,
):
    lines_here, seg_len = left.shape[:2]
    pairs = ((left_in, left), (right_in, right))
    for line in range(lines_here):
        begin_copies(line_copies(pairs, line_sems, line, lines_here))
    fetch, send_stacked, send_part = copies_of(
        ((weight_in, weight), (stacked, stacked_out), (part, part_out)), sems
    )
    fetch.start()

    def one_line(line, carry):
        wait(line_copies(pairs, line_sems, line, lines_here))
        for first in range(0, seg_len, block):
            cols = slice(first, first + block)
            peak, total = column_block(left[line, first:], right[line, cols], True)
            part[pl.ds(line, 1), cols] = peak
            part[pl.ds(lines_here + line, 1), cols] = total
        return carry

    lax.fori_loop(0, lines_here, one_line, 0)
    send_part.start()
    fetch.wait()
    stack_weights(weight, stacked)
    send_stacked.start()
    send_part.wait()
    send_stacked.wait()


def column_cost(lines_here, seg_len, channels):
    return pl.CostEstimate(
        flops=2 * lines_here * seg_len * seg_len * channels,
        bytes_accessed=8 * lines_here * seg_len * channels,
        transcendentals=lines_here * seg_len * seg_len // 2,
    )


def own_partials(left, right, weight):
    lines_here, seg_len, channels = left.shape
    bf16, f32 = jnp.bfloat16, jnp.float32
    stacked = ((weight.shape[0], 12 * channels, 2 * channels), bf16)
    part = ((2 * lines_here, seg_len), f32)
    return kernel_call(
        functools.partial(own_kernel, min(256, seg_len)),
        (left, right, weight),
        (stacked, part),
        ((left.shape, bf16), (right.shape, bf16), (weight.shape, bf16), stacked, part),
        (2 * lines_here, 3),
        "column_own",
        column_cost(*left.shape),
    )


def next_kernel(
    block,
    next_in,
    right_in,
    own_in,
    back_in,
    merged_out,
    first_out,
    second_out,
    following,
    right,
    merged,
    back,
    first_part,
    second_part,
    line_sems,
    sems,
):
    lines_here, half = following.shape[:2]
    pairs = ((next_in, following), (right_in.at[:, pl.ds(0, half)], right))
    fetches = copies_of(((own_in, merged), (back_in, back)), sems)
    sends = copies_of(
        ((first_part, first_out), (second_part, second_out), (merged, merged_out)),
        sems.at[pl.ds(2, 3)],
    )
    begin_copies(fetches)
    for line in range(lines_here):
        begin_copies(line_copies(pairs, line_sems, line, lines_here))
    wait(fetches)
    last = lax.axis_index("seg") == lax.axis_size("seg") - 1

    def one_line(line, carry):
        wait(line_copies(pairs, line_sems, line, lines_here))
        top, bottom = pl.ds(line, 1), pl.ds(lines_here + line, 1)
        for first in range(0, half, block):
            cols = slice(first, first + block)
            peak, total = column_block(following[line, : first + block], right[line, cols], False)
            peak = jnp.where(last, NEG, peak)
            total = jnp.where(last, 0.0, total)
            own_peak = merged[top, cols]
            joint = jnp.maximum(own_peak, peak)
            merged[bottom, cols] = merged[bottom, cols] * jnp.exp2(
                own_peak - joint
            ) + total * jnp.exp2(peak - joint)
            merged[top, cols] = joint
        return carry

    lax.fori_loop(0, lines_here, one_line, 0)
    first_part[...], second_part[...] = by_parity(merged[...], back[...])
    begin_copies(sends)
    wait(sends)


def next_partials(next_low, right, own, back):
    lines_here, half, channels = next_low.shape
    part = (own.shape, jnp.float32)
    features = (next_low.shape, jnp.bfloat16)
    return kernel_call(
        functools.partial(next_kernel, min(256, half)),
        (next_low, right, own, back),
        (part,) * 3,
        (features, features) + (part,) * 4,
        (2 * lines_here, 5),
        "column_next",
        column_cost(lines_here, half, channels),
    )


def cross_kernel(block, left_in, prev_in, back_out, left, prev, back, line_sems, sems):
    lines_here, seg_len = left.shape[:2]
    half = seg_len - prev.shape[1]
    pairs = ((left_in, left), (prev_in, prev))
    for line in range(lines_here):
        begin_copies(line_copies(pairs, line_sems, line, lines_here))
    (send,) = copies_of(((back, back_out),), sems)
    back[...] = jnp.zeros_like(back)

    def one_line(line, carry):
        wait(line_copies(pairs, line_sems, line, lines_here))
        top, bottom = pl.ds(line, 1), pl.ds(lines_here + line, 1)
        for first in range(0, prev.shape[1], block):
            cols = slice(first, first + block)
            peak, total = column_block(
                left[line, : half + first + block], prev[line, cols], False
            )
            back[top, cols] = peak
            back[bottom, cols] = total
        return carry

    lax.fori_loop(0, lines_here, one_line, 0)
    send.start()
    send.wait()


def cross_partials(left, prev_high):
    lines_here, seg_len, channels = left.shape
    part = ((2 * lines_here, seg_len), jnp.float32)
    return kernel_call(
        functools.partial(cross_kernel, min(256, prev_high.shape[1])),
        (left, prev_high),
        (part,),
        ((left.shape, jnp.bfloat16), (prev_high.shape, jnp.bfloat16), part),
        (2 * lines_here, 1),
        "column_cross",
        column_cost(*left.shape),
    )[0]


def potential(peak, total):
    return -(peak + jnp.log2(total))


def merged_potential(first, second):
    first_max = jnp.where(first[1] > 0, first[0], NEG)
    second_max = jnp.where(second[1] > 0, second[0], NEG)
    peak = jnp.maximum(first_max, second_max)
    total = first[1] * jnp.exp2(first_max - peak) + second[1] * jnp.exp2(second_max - peak)
    return potential(peak, total)


def split(values, parts):
    pieces = []
    for _ in range(parts):
        piece = values.astype(jnp.bfloat16).astype(jnp.float32)
        pieces.append(piece)
        values = values - piece
    return pieces


SHIFT = 2


def potential_lanes(pot, channels):
    lines_here, count = pot.shape
    parts = split(pot, 3)
    filler = jnp.zeros((channels - 3 * lines_here, count), jnp.float32)
    lanes = jnp.concatenate(parts + [filler], axis=0).T
    lane = lax.broadcasted_iota(jnp.int32, lanes.shape, 1)
    return jnp.where(lane >= channels - SHIFT, -1.0, lanes).astype(jnp.bfloat16)


def line_lanes(line, lines_here, shape):
    lane = lax.broadcasted_iota(jnp.int32, shape, 1)
    mine = jnp.zeros(shape, jnp.float32)
    for part in range(3):
        mine = jnp.where(lane == part * lines_here + line, 1.0, mine)
    return mine


def banded(values, row, block):
    rows, window = values.shape
    col_ids = lax.broadcasted_iota(jnp.int32, (rows, block), 1)
    row_ids = lax.broadcasted_iota(jnp.int32, (rows, block), 0) + row
    return jnp.concatenate(
        [
            jnp.where(col_ids > row_ids, values[:, :block], NEG),
            values[:, block : window - block],
            jnp.where(col_ids <= row_ids, values[:, window - block :], NEG),
        ],
        axis=1,
    )


def feature_pairs(left_in, right_in, prev_low_in, prev_high_in, left, ext):
    seg_len, half = left.shape[1], prev_low_in.shape[1]
    return (
        (left_in, left),
        (prev_low_in, ext.at[:, pl.ds(0, half)]),
        (prev_high_in, ext.at[:, pl.ds(half, seg_len - half)]),
        (right_in, ext.at[:, pl.ds(seg_len, seg_len)]),
    )


def row_kernel(
    block,
    left_in,
    right_in,
    prev_low_in,
    prev_high_in,
    own_in,
    back_in,
    first_in,
    second_in,
    pot_out,
    lanes_out,
    own_out,
    prev_out,
    first_out,
    second_out,
    left,
    ext,
    own,
    back,
    first_part,
    second_part,
    pot,
    lanes,
    own_sum,
    prev_sum,
    first_sum,
    second_sum,
    pot_lanes,
    sums,
    raw,
    line_sems,
    sems,
):
    lines_here, seg_len, channels = left.shape
    half = prev_low_in.shape[1]
    scale = log2_scale(channels)
    fetches = copies_of(
        ((own_in, own), (back_in, back), (first_in, first_part), (second_in, second_part)), sems
    )
    begin_copies(fetches)
    pairs = feature_pairs(left_in, right_in, prev_low_in, prev_high_in, left, ext)
    for line in range(lines_here):
        begin_copies(line_copies(pairs, line_sems, line, lines_here))
    wait(fetches)

    following, before = by_parity(first_part[...], second_part[...])

    def parts(part, first, stop):
        return part[:lines_here, first:stop], part[lines_here:, first:stop]

    rest = seg_len - half
    pot[:, seg_len : seg_len + half] = potential(*parts(own, 0, half))
    pot[:, seg_len + half :] = merged_potential(
        parts(own, half, seg_len), parts(following, 0, rest)
    )
    low = parts(before, 0, half)
    high = parts(before, half, seg_len)
    pot[:, :half] = jnp.where(low[1] > 0, potential(*low), NEG)
    pot[:, half:seg_len] = jnp.where(
        high[1] > 0, merged_potential(high, parts(back, 0, rest)), NEG
    )
    pot_lanes[...] = potential_lanes(pot[...] * (1.0 / scale), channels)
    window = seg_len + block
    big = 2 * block
    steps = seg_len // big
    strip = 16
    lane = lax.broadcasted_iota(jnp.int32, (strip, channels), 1)

    def one_line(line, carry):
        wait(line_copies(pairs, line_sems, line, lines_here))
        sums[...] = jnp.zeros_like(sums)
        mine = line_lanes(line, lines_here, (big, channels)).astype(jnp.bfloat16)
        strip_lanes = line_lanes(line, lines_here, (strip, channels))

        def score(index):
            first = index * big
            reach = slice(first, first + seg_len + big)
            raw[index % 2] = scores_of(
                jnp.concatenate([left[line, first : first + big], mine], axis=1),
                jnp.concatenate([ext[line, reach], pot_lanes[reach]], axis=1),
            )

        score(0)
        for index in range(steps):
            slot = index % 2
            if index + 1 < steps:
                score(index + 1)
            for side in range(2):
                shift = side * block
                first = index * big + shift
                column_sum = jnp.zeros((8, window), jnp.float32)
                for row in range(0, block, strip):
                    rows = slice(shift + row, shift + row + strip)
                    logits = banded(raw[slot, rows, shift : shift + window], row, block)
                    peak = jnp.max(logits, axis=1, keepdims=True)
                    terms = jnp.exp2((logits - peak) * scale)
                    plan = terms * (1.0 / jnp.sum(terms, axis=1, keepdims=True))
                    column_sum += plan[:8] + plan[8:]
                    marked = strip_lanes
                    for part, piece in enumerate(split(peak, SHIFT)):
                        marked = jnp.where(lane == channels - SHIFT + part, piece, marked)
                    lanes[line, first + row : first + row + strip] = marked.astype(jnp.bfloat16)
                sums[:, first : first + window] += column_sum
        totals = jnp.sum(sums[...], axis=0, keepdims=True)
        prev_sum[pl.ds(line, 1), :] = totals[:, :seg_len]
        own_sum[pl.ds(line, 1), :] = totals[:, seg_len:]
        return carry

    lax.fori_loop(0, lines_here, one_line, 0)
    first_sum[...], second_sum[...] = by_parity(own_sum[...], prev_sum[...])
    sends = copies_of(
        (
            (first_sum, first_out),
            (second_sum, second_out),
            (own_sum, own_out),
            (prev_sum, prev_out),
            (pot, pot_out),
            (lanes, lanes_out),
        ),
        sems,
    )
    begin_copies(sends)
    wait(sends)


def row_pass(left, right, prev_low, prev_high, own, back, first, second, block):
    lines_here, seg_len, channels = left.shape
    bf16, f32 = jnp.bfloat16, jnp.float32
    part = (own.shape, f32)
    marginal = ((lines_here, seg_len), f32)
    pot = ((lines_here, 2 * seg_len), f32)
    lanes = (left.shape, bf16)
    return kernel_call(
        functools.partial(row_kernel, block),
        (left, right, prev_low, prev_high, own, back, first, second),
        (pot, lanes) + (marginal,) * 4,
        ((left.shape, bf16), ((lines_here, 2 * seg_len, channels), bf16))
        + (part,) * 4
        + (pot, lanes)
        + (marginal,) * 4
        + (
            ((2 * seg_len, channels), bf16),
            ((8, 2 * seg_len), f32),
            ((2, 2 * block, seg_len + 2 * block), f32),
        ),
        (4 * lines_here, 6),
        "row_pass",
    )


def transport_kernel(
    block,
    pot_in,
    lanes_in,
    left_in,
    right_in,
    prev_low_in,
    prev_high_in,
    own_in,
    back_in,
    first_in,
    second_in,
    state_out,
    disp_out,
    first_out,
    last_out,
    first_px_out,
    second_px_out,
    pot,
    lanes,
    left,
    ext,
    own,
    back,
    first_part,
    second_part,
    state,
    disp,
    first_px,
    second_px,
    pot_lanes,
    marks,
    raw,
    weights,
    line_sems,
    sems,
    send_sems,
):
    lines_here, seg_len, channels = left.shape
    layers = first_out.shape[0]
    scale = log2_scale(channels)
    big = 2 * block
    window = seg_len + big
    fetches = copies_of(
        (
            (pot_in, pot),
            (own_in, own),
            (back_in, back),
            (first_in, first_part),
            (second_in, second_part),
        ),
        sems,
    )
    begin_copies(fetches)
    pairs = feature_pairs(left_in, right_in, prev_low_in, prev_high_in, left, ext) + (
        (lanes_in, lanes),
    )
    for line in range(lines_here):
        begin_copies(line_copies(pairs, line_sems, line, lines_here))
    lane = lax.broadcasted_iota(jnp.int32, (window, channels), 1)
    distance = seg_len - lax.broadcasted_iota(jnp.int32, (window, channels), 0)
    fine = jnp.bitwise_and(distance, 15)
    values = jnp.where(
        lane == 0,
        1,
        jnp.where(lane == 1, distance - fine, jnp.where(lane == 2, fine, 0)),
    )
    marks[...] = values.astype(jnp.float32).astype(jnp.bfloat16)
    wait(fetches)
    following, before = by_parity(first_part[...], second_part[...])
    total = jnp.concatenate([before + back[...], own[...] + following], axis=1)
    final = jnp.where(total > 0, pot[...] - jnp.log2(total), NEG)
    pot_lanes[...] = potential_lanes(final * (1.0 / scale), channels)
    offsets = lax.broadcasted_iota(jnp.int32, (1, big), 1).astype(jnp.float32)
    corner = jnp.zeros((block, block), jnp.bfloat16)
    steps = seg_len // big

    def one_line(line, carry):
        wait(line_copies(pairs, line_sems, line, lines_here))

        def score(index):
            first = index * big
            rows, reach = slice(first, first + big), slice(first, first + window)
            raw[index % 2] = scores_of(
                jnp.concatenate([left[line, rows], lanes[line, rows]], axis=1),
                jnp.concatenate([ext[line, reach], pot_lanes[reach]], axis=1),
            )

        def weigh(index):
            slot = index % 2
            upper = jnp.exp2(banded(raw[slot, :block, : window - block], 0, block) * scale)
            lower = jnp.exp2(banded(raw[slot, block:, block:], 0, block) * scale)
            weights[slot, :block, : window - block] = upper.astype(jnp.bfloat16)
            weights[slot, :block, window - block :] = corner
            weights[slot, block:, block:] = lower.astype(jnp.bfloat16)
            weights[slot, block:, :block] = corner

        def gather(index):
            first = index * big
            rows = slice(first, first + big)
            table = jnp.concatenate([ext[line, first : first + window], marks[...]], axis=1)
            result = jnp.dot(weights[index % 2], table, preferred_element_type=jnp.float32)
            matched = result[:, :channels] * (1.0 / result[:, channels : channels + 1])
            state[line, rows] = (matched - left[line, rows].astype(jnp.float32)).astype(
                state.dtype
            )
            moments = result[:, channels:].T
            return offsets + (moments[1:2] + moments[2:3]) / moments[0:1]

        disparity = []
        for index in range(steps + 2):
            if index < steps:
                score(index)
            if index >= 2:
                disparity.append(gather(index - 2))
            if 1 <= index <= steps:
                weigh(index - 1)
        disp[pl.ds(line, 1), :] = jnp.concatenate(disparity, axis=1)
        begin_copies(line_copies(((state, state_out),), send_sems, line, lines_here))
        high = state[line, seg_len - EDGE :].astype(jnp.float32)
        first, second = by_parity(high, state[line, :EDGE].astype(jnp.float32))
        first_px[line] = first.astype(jnp.bfloat16)
        second_px[line] = second.astype(jnp.bfloat16)

        @pl.when(line < layers)
        def _():
            pltpu.make_async_copy(state.at[line], first_out.at[line], sems.at[line]).start()

        @pl.when(line >= lines_here - layers)
        def _():
            target = line - (lines_here - layers)
            pltpu.make_async_copy(
                state.at[line], last_out.at[target], sems.at[layers + target]
            ).start()

        return carry

    lax.fori_loop(0, lines_here, one_line, 0)
    sends = copies_of(
        ((first_px, first_px_out), (second_px, second_px_out), (disp, disp_out)),
        send_sems.at[pl.ds(lines_here, 3)],
    )
    begin_copies(sends)
    for line in range(layers):
        pltpu.make_async_copy(state.at[line], first_out.at[line], sems.at[line]).wait()
        source = line + lines_here - layers
        pltpu.make_async_copy(state.at[source], last_out.at[line], sems.at[layers + line]).wait()
    for line in range(lines_here):
        wait(line_copies(((state, state_out),), send_sems, line, lines_here))
    wait(sends)


def transport(pot, lanes, left, right, prev_low, prev_high, own, back, first, second, block, layers):
    lines_here, seg_len, channels = left.shape
    bf16, f32 = jnp.bfloat16, jnp.float32
    edge = ((layers, seg_len, channels), bf16)
    side = ((lines_here, EDGE, channels), bf16)
    state = (left.shape, bf16)
    marginal = ((lines_here, seg_len), f32)
    window = seg_len + 2 * block
    return kernel_call(
        functools.partial(transport_kernel, block),
        (pot, lanes, left, right, prev_low, prev_high, own, back, first, second),
        (state, marginal, edge, edge, side, side),
        ((pot.shape, f32), (lanes.shape, bf16), state)
        + (((lines_here, 2 * seg_len, channels), bf16),)
        + (marginal,) * 4
        + (state, marginal, side, side)
        + (
            ((2 * seg_len, channels), bf16),
            ((window, channels), bf16),
            ((2, 2 * block, window), f32),
            ((2, 2 * block, window), bf16),
        ),
        (5 * lines_here, max(5, 2 * layers), lines_here + 3),
        "transport",
    )


def stack_weights(weight_ref, stacked_ref):
    layers, taps, _, channels, _ = weight_ref.shape
    zeros = jnp.zeros((channels, channels), stacked_ref.dtype)
    for layer in range(layers):
        for col_tap in range(taps):
            for line in range(taps + 1):
                row = (col_tap * (taps + 1) + line) * channels
                for out in range(2):
                    row_tap = line - out
                    stacked_ref[
                        layer, row : row + channels, out * channels : (out + 1) * channels
                    ] = weight_ref[layer, row_tap, col_tap] if 0 <= row_tap < taps else zeros


def conv_kernel(
    state_in,
    top_in,
    bottom_in,
    first_in,
    second_in,
    corner_top_in,
    corner_bottom_in,
    weight_in,
    bias_in,
    result_out,
    state_ref,
    top_ref,
    bottom_ref,
    first_ref,
    second_ref,
    corner_top_ref,
    corner_bottom_ref,
    weight_ref,
    bias_ref,
    out_ref,
    first_image,
    second_image,
    sems,
    send_sems,
):
    fetches = copies_of(
        (
            (state_in, state_ref),
            (first_in, first_ref),
            (second_in, second_ref),
            (corner_top_in, corner_top_ref),
            (corner_bottom_in, corner_bottom_ref),
            (top_in, top_ref),
            (bottom_in, bottom_ref),
            (weight_in, weight_ref),
            (bias_in, bias_ref),
        ),
        sems,
    )
    begin_copies(fetches)
    lines_here, seg_len, channels = state_ref.shape
    layers = weight_ref.shape[0]
    after = layers + lines_here
    right = EDGE + seg_len
    f32 = jnp.float32
    wait(fetches[:1])
    first_image[layers:after, EDGE:right] = state_ref[...].astype(f32)
    wait(fetches[1:])
    first_image[:layers, EDGE:right] = top_ref[...].astype(f32)
    first_image[after:, EDGE:right] = bottom_ref[...].astype(f32)
    for rows, first_px, second_px in (
        (slice(layers, after), first_ref[...], second_ref[...]),
        (slice(0, layers), corner_top_ref[:, :EDGE], corner_top_ref[:, EDGE:]),
        (slice(after, None), corner_bottom_ref[:, :EDGE], corner_bottom_ref[:, EDGE:]),
    ):
        following, before = by_parity(first_px.astype(f32), second_px.astype(f32))
        first_image[rows, :EDGE] = before
        first_image[rows, right:] = following
    line0 = lax.axis_index("lines") * lines_here - layers
    all_lines = lax.axis_size("lines") * lines_here
    px0 = lax.axis_index("seg") * seg_len - EDGE
    all_px = lax.axis_size("seg") * seg_len
    source, target = first_image, second_image
    for layer in range(layers):
        reach = layers - 1 - layer
        begin, end = (EDGE // 2, right + EDGE // 2) if reach else (EDGE, right)
        middle = begin + seg_len // 2
        pieces = ((begin, middle), (middle, end))

        def pair(index, carry, layer=layer, reach=reach, pieces=pieces, source=source, target=target):
            base = layer + 2 * index
            for start, stop in pieces:
                size = stop - start
                taps = [
                    source[base + line, start + col_tap - 1 : start + col_tap - 1 + size].astype(jnp.bfloat16)
                    for col_tap in range(3)
                    for line in range(4)
                ]
                total = jnp.dot(
                    jnp.concatenate(taps, axis=1), weight_ref[layer], preferred_element_type=f32
                )
                for out in range(2):
                    line = base + 1 + out
                    part = total[:, out * channels : (out + 1) * channels] + bias_ref[layer : layer + 1]
                    updated = source[line, start : start + size] + jnp.maximum(part, 0.0)
                    if not reach:
                        out_ref[line - layers, start - EDGE : start - EDGE + size] = updated.astype(out_ref.dtype)
                        continue
                    image_line = line0 + line
                    inside = (image_line >= 0) & (image_line < all_lines)
                    if reach:
                        px = px0 + start + lax.broadcasted_iota(jnp.int32, updated.shape, 0)
                        inside = inside & (px >= 0) & (px < all_px)
                    updated = jnp.where(inside, updated, 0.0)
                    target[line, start : start + size] = updated.astype(jnp.bfloat16).astype(f32)
            if not reach:
                for line in (base + 1, base + 2):
                    begin_copies(line_copies(((out_ref, result_out),), send_sems, line - layers, lines_here))
            return carry

        lax.fori_loop(0, (lines_here + 2 * reach) // 2, pair, 0, unroll=True)
        source, target = target, source
    for line in range(lines_here):
        wait(line_copies(((out_ref, result_out),), send_sems, line, lines_here))


def conv_layers(state, top, bottom, left_px, right_px, corners_top, corners_bottom, weight, bias):
    layers = weight.shape[0]
    lines_here, seg_len, channels = state.shape
    image = ((lines_here + 2 * layers, seg_len + 2 * EDGE, channels), jnp.float32)
    operands = (state, top, bottom, left_px, right_px, corners_top, corners_bottom, weight, bias)
    result = (state.shape, state.dtype)
    return kernel_call(
        conv_kernel,
        operands,
        (result,),
        tuple((operand.shape, operand.dtype) for operand in operands) + (result, image, image),
        (len(operands), lines_here),
        "conv_layers",
    )[0]


def shards(left_features, right_features, conv_weight, conv_bias):
    seg_len = left_features.shape[1]
    half = seg_len // 2
    layers = conv_weight.shape[0]
    prev_high = shifted(right_features[:, half:], "seg", 1)
    next_low = shifted(left_features[:, :half], "seg", -1)
    stacked, own = own_partials(left_features, right_features, conv_weight)
    right_low, own = lax.optimization_barrier((right_features[:, :half], own))
    prev_low = shifted(right_low, "seg", 1)
    back = cross_partials(left_features, prev_high)
    own, first, second = next_partials(next_low, right_features, own, back)
    first = exchanged(first, "seg", 0)
    second = exchanged(second, "seg", 1)
    block = min(128, half)
    pot, lanes, own, back, first, second = row_pass(
        left_features, right_features, prev_low, prev_high, own, back, first, second, block
    )
    first = exchanged(first, "seg", 0)
    second = exchanged(second, "seg", 1)
    state, disparity, first_lines, last_lines, first, second = transport(
        pot, lanes, left_features, right_features, prev_low, prev_high, own, back, first, second, block, layers
    )
    bottom = shifted(first_lines, "lines", -1)
    top = shifted(last_lines, "lines", 1)
    first = exchanged(first, "seg", 0)
    second = exchanged(second, "seg", 1)
    edges = jnp.concatenate([first, second], axis=1)
    corners_bottom = shifted(edges[:layers], "lines", -1)
    corners_top = shifted(edges[-layers:], "lines", 1)
    refined = conv_layers(
        state, top, bottom, first, second, corners_top, corners_bottom, stacked, conv_bias
    )
    return (refined, disparity)


def solution(mesh):
    return jax.shard_map(
        shards,
        mesh=mesh,
        in_specs=(P("lines", "seg", None), P("lines", "seg", None), P(), P()),
        out_specs=(P("lines", "seg", None), P("lines", "seg")),
        check_vma=False,
    )
```

```python
import functools
import math

import jax
import jax.numpy as jnp
from jax import lax
from jax.experimental import pallas as pl
from jax.experimental.pallas import tpu as pltpu
from jax.sharding import PartitionSpec as P

DISP = 1024
NEG = -1e30
EDGE = 16
VMEM_BYTES = 32 * 1024 * 1024


def shifted(block, axis, step):
    count = lax.axis_size(axis)
    route = [(i, i + step) for i in range(count) if 0 <= i + step < count]
    return lax.ppermute(block, axis, route)


def exchanged(block, axis, odd):
    route = []
    for low in range(odd, lax.axis_size(axis) - 1, 2):
        route += [(low, low + 1), (low + 1, low)]
    return lax.ppermute(block, axis, route)


def even_segment():
    return lax.rem(lax.axis_index("seg"), 2) == 0


def by_parity(following, previous):
    even = even_segment()
    return jnp.where(even, following, previous), jnp.where(even, previous, following)


def params():
    return pltpu.CompilerParams(vmem_limit_bytes=VMEM_BYTES)


ANYWHERE = pl.BlockSpec(memory_space=pl.ANY)


def kernel_call(kernel, operands, results, scratch, copies, name, cost=None):
    return pl.pallas_call(
        kernel,
        in_specs=[ANYWHERE] * len(operands),
        out_specs=[ANYWHERE] * len(results),
        out_shape=[jax.ShapeDtypeStruct(shape, dtype) for shape, dtype in results],
        scratch_shapes=[pltpu.VMEM(shape, dtype) for shape, dtype in scratch]
        + [pltpu.SemaphoreType.DMA((count,)) for count in copies],
        compiler_params=params(),
        cost_estimate=cost,
        name=name,
    )(*operands)


def copies_of(pairs, sems):
    return [
        pltpu.make_async_copy(source, target, sems.at[index])
        for index, (source, target) in enumerate(pairs)
    ]


def line_copies(pairs, sems, line, lines_here):
    return [
        pltpu.make_async_copy(source.at[line], target.at[line], sems.at[index * lines_here + line])
        for index, (source, target) in enumerate(pairs)
    ]


def begin_copies(copies):
    for copy in copies:
        copy.start()


def wait(copies):
    for copy in copies:
        copy.wait()


def scores_of(left, right):
    return lax.dot_general(
        left, right, (((1,), (1,)), ((), ())), preferred_element_type=jnp.float32
    )


def log2_scale(channels):
    return math.log2(math.e) / math.sqrt(channels)


def over_rows(reduce, values, chains=64):
    count, width = values.shape
    while count > chains >= 8 and count % chains == 0:
        values = reduce(values.reshape(count // chains, chains, width), axis=0)
        count, chains = chains, chains // 8
    return reduce(values, axis=0, keepdims=True)


def column_block(left, right, diagonal_first):
    block, channels = right.shape
    scale = log2_scale(channels)
    raw = scores_of(left, right)
    row_ids = lax.broadcasted_iota(jnp.int32, (block, block), 0)
    col_ids = lax.broadcasted_iota(jnp.int32, (block, block), 1)
    if diagonal_first:
        parts = [jnp.where(col_ids <= row_ids, raw[:block], NEG), raw[block:]]
    else:
        parts = [raw[:-block], jnp.where(col_ids > row_ids, raw[-block:], NEG)]
    parts = [part for part in parts if part.shape[0]]
    peak = functools.reduce(jnp.maximum, [over_rows(jnp.max, part) for part in parts])
    total = sum(over_rows(jnp.sum, jnp.exp2((part - peak) * scale)) for part in parts)
    return (peak * scale, total)


def own_kernel(
    block,
    left_in,
    right_in,
    weight_in,
    stacked_out,
    part_out,
    left,
    right,
    weight,
    stacked,
    part,
    line_sems,
    sems,
):
    lines_here, seg_len = left.shape[:2]
    pairs = ((left_in, left), (right_in, right))
    for line in range(lines_here):
        begin_copies(line_copies(pairs, line_sems, line, lines_here))
    fetch, send_stacked, send_part = copies_of(
        ((weight_in, weight), (stacked, stacked_out), (part, part_out)), sems
    )
    fetch.start()

    def one_line(line, carry):
        wait(line_copies(pairs, line_sems, line, lines_here))
        for first in range(0, seg_len, block):
            cols = slice(first, first + block)
            peak, total = column_block(left[line, first:], right[line, cols], True)
            part[pl.ds(line, 1), cols] = peak
            part[pl.ds(lines_here + line, 1), cols] = total
        return carry

    lax.fori_loop(0, lines_here, one_line, 0)
    send_part.start()
    fetch.wait()
    stack_weights(weight, stacked)
    send_stacked.start()
    send_part.wait()
    send_stacked.wait()


def column_cost(lines_here, seg_len, channels):
    return pl.CostEstimate(
        flops=2 * lines_here * seg_len * seg_len * channels,
        bytes_accessed=8 * lines_here * seg_len * channels,
        transcendentals=lines_here * seg_len * seg_len // 2,
    )


def own_partials(left, right, weight):
    lines_here, seg_len, channels = left.shape
    bf16, f32 = jnp.bfloat16, jnp.float32
    stacked = ((weight.shape[0], 12 * channels, 2 * channels), bf16)
    part = ((2 * lines_here, seg_len), f32)
    return kernel_call(
        functools.partial(own_kernel, min(256, seg_len)),
        (left, right, weight),
        (stacked, part),
        ((left.shape, bf16), (right.shape, bf16), (weight.shape, bf16), stacked, part),
        (2 * lines_here, 3),
        "column_own",
        column_cost(*left.shape),
    )


def next_kernel(
    block,
    next_in,
    right_in,
    own_in,
    back_in,
    merged_out,
    first_out,
    second_out,
    following,
    right,
    merged,
    back,
    first_part,
    second_part,
    line_sems,
    sems,
):
    lines_here, half = following.shape[:2]
    pairs = ((next_in, following), (right_in.at[:, pl.ds(0, half)], right))
    fetches = copies_of(((own_in, merged), (back_in, back)), sems)
    sends = copies_of(
        ((first_part, first_out), (second_part, second_out), (merged, merged_out)),
        sems.at[pl.ds(2, 3)],
    )
    begin_copies(fetches)
    for line in range(lines_here):
        begin_copies(line_copies(pairs, line_sems, line, lines_here))
    wait(fetches)
    last = lax.axis_index("seg") == lax.axis_size("seg") - 1

    def one_line(line, carry):
        wait(line_copies(pairs, line_sems, line, lines_here))
        top, bottom = pl.ds(line, 1), pl.ds(lines_here + line, 1)
        for first in range(0, half, block):
            cols = slice(first, first + block)
            peak, total = column_block(following[line, : first + block], right[line, cols], False)
            peak = jnp.where(last, NEG, peak)
            total = jnp.where(last, 0.0, total)
            own_peak = merged[top, cols]
            joint = jnp.maximum(own_peak, peak)
            merged[bottom, cols] = merged[bottom, cols] * jnp.exp2(
                own_peak - joint
            ) + total * jnp.exp2(peak - joint)
            merged[top, cols] = joint
        return carry

    lax.fori_loop(0, lines_here, one_line, 0)
    first_part[...], second_part[...] = by_parity(merged[...], back[...])
    begin_copies(sends)
    wait(sends)


def next_partials(next_low, right, own, back):
    lines_here, half, channels = next_low.shape
    part = (own.shape, jnp.float32)
    features = (next_low.shape, jnp.bfloat16)
    return kernel_call(
        functools.partial(next_kernel, min(256, half)),
        (next_low, right, own, back),
        (part,) * 3,
        (features, features) + (part,) * 4,
        (2 * lines_here, 5),
        "column_next",
        column_cost(lines_here, half, channels),
    )


def cross_kernel(block, left_in, prev_in, back_out, left, prev, back, line_sems, sems):
    lines_here, seg_len = left.shape[:2]
    half = seg_len - prev.shape[1]
    pairs = ((left_in, left), (prev_in, prev))
    for line in range(lines_here):
        begin_copies(line_copies(pairs, line_sems, line, lines_here))
    (send,) = copies_of(((back, back_out),), sems)
    back[...] = jnp.zeros_like(back)

    def one_line(line, carry):
        wait(line_copies(pairs, line_sems, line, lines_here))
        top, bottom = pl.ds(line, 1), pl.ds(lines_here + line, 1)
        for first in range(0, prev.shape[1], block):
            cols = slice(first, first + block)
            peak, total = column_block(
                left[line, : half + first + block], prev[line, cols], False
            )
            back[top, cols] = peak
            back[bottom, cols] = total
        return carry

    lax.fori_loop(0, lines_here, one_line, 0)
    send.start()
    send.wait()


def cross_partials(left, prev_high):
    lines_here, seg_len, channels = left.shape
    part = ((2 * lines_here, seg_len), jnp.float32)
    return kernel_call(
        functools.partial(cross_kernel, min(256, prev_high.shape[1])),
        (left, prev_high),
        (part,),
        ((left.shape, jnp.bfloat16), (prev_high.shape, jnp.bfloat16), part),
        (2 * lines_here, 1),
        "column_cross",
        column_cost(*left.shape),
    )[0]


def potential(peak, total):
    return -(peak + jnp.log2(total))


def merged_potential(first, second):
    first_max = jnp.where(first[1] > 0, first[0], NEG)
    second_max = jnp.where(second[1] > 0, second[0], NEG)
    peak = jnp.maximum(first_max, second_max)
    total = first[1] * jnp.exp2(first_max - peak) + second[1] * jnp.exp2(second_max - peak)
    return potential(peak, total)


def split(values, parts):
    pieces = []
    for _ in range(parts):
        piece = values.astype(jnp.bfloat16).astype(jnp.float32)
        pieces.append(piece)
        values = values - piece
    return pieces


SHIFT = 2


def potential_lanes(pot, channels):
    lines_here, count = pot.shape
    parts = split(pot, 3)
    filler = jnp.zeros((channels - 3 * lines_here, count), jnp.float32)
    lanes = jnp.concatenate(parts + [filler], axis=0).T
    lane = lax.broadcasted_iota(jnp.int32, lanes.shape, 1)
    return jnp.where(lane >= channels - SHIFT, -1.0, lanes).astype(jnp.bfloat16)


def line_lanes(line, lines_here, shape):
    lane = lax.broadcasted_iota(jnp.int32, shape, 1)
    mine = jnp.zeros(shape, jnp.float32)
    for part in range(3):
        mine = jnp.where(lane == part * lines_here + line, 1.0, mine)
    return mine


def banded(values, row, block):
    rows, window = values.shape
    col_ids = lax.broadcasted_iota(jnp.int32, (rows, block), 1)
    row_ids = lax.broadcasted_iota(jnp.int32, (rows, block), 0) + row
    return jnp.concatenate(
        [
            jnp.where(col_ids > row_ids, values[:, :block], NEG),
            values[:, block : window - block],
            jnp.where(col_ids <= row_ids, values[:, window - block :], NEG),
        ],
        axis=1,
    )


def feature_pairs(left_in, right_in, prev_low_in, prev_high_in, left, ext):
    seg_len, half = left.shape[1], prev_low_in.shape[1]
    return (
        (left_in, left),
        (prev_low_in, ext.at[:, pl.ds(0, half)]),
        (prev_high_in, ext.at[:, pl.ds(half, seg_len - half)]),
        (right_in, ext.at[:, pl.ds(seg_len, seg_len)]),
    )


def row_kernel(
    block,
    left_in,
    right_in,
    prev_low_in,
    prev_high_in,
    own_in,
    back_in,
    first_in,
    second_in,
    pot_out,
    lanes_out,
    own_out,
    prev_out,
    first_out,
    second_out,
    left,
    ext,
    own,
    back,
    first_part,
    second_part,
    pot,
    lanes,
    own_sum,
    prev_sum,
    first_sum,
    second_sum,
    pot_lanes,
    sums,
    raw,
    line_sems,
    sems,
):
    lines_here, seg_len, channels = left.shape
    half = prev_low_in.shape[1]
    scale = log2_scale(channels)
    fetches = copies_of(
        ((own_in, own), (back_in, back), (first_in, first_part), (second_in, second_part)), sems
    )
    begin_copies(fetches)
    pairs = feature_pairs(left_in, right_in, prev_low_in, prev_high_in, left, ext)
    for line in range(lines_here):
        begin_copies(line_copies(pairs, line_sems, line, lines_here))
    wait(fetches)

    following, before = by_parity(first_part[...], second_part[...])

    def parts(part, first, stop):
        return part[:lines_here, first:stop], part[lines_here:, first:stop]

    rest = seg_len - half
    pot[:, seg_len : seg_len + half] = potential(*parts(own, 0, half))
    pot[:, seg_len + half :] = merged_potential(
        parts(own, half, seg_len), parts(following, 0, rest)
    )
    low = parts(before, 0, half)
    high = parts(before, half, seg_len)
    pot[:, :half] = jnp.where(low[1] > 0, potential(*low), NEG)
    pot[:, half:seg_len] = jnp.where(
        high[1] > 0, merged_potential(high, parts(back, 0, rest)), NEG
    )
    pot_lanes[...] = potential_lanes(pot[...] * (1.0 / scale), channels)
    window = seg_len + block
    big = 2 * block
    steps = seg_len // big
    strip = 16
    lane = lax.broadcasted_iota(jnp.int32, (strip, channels), 1)

    def one_line(line, carry):
        wait(line_copies(pairs, line_sems, line, lines_here))
        sums[...] = jnp.zeros_like(sums)
        mine = line_lanes(line, lines_here, (big, channels)).astype(jnp.bfloat16)
        strip_lanes = line_lanes(line, lines_here, (strip, channels))

        def score(index):
            first = index * big
            reach = slice(first, first + seg_len + big)
            raw[index % 2] = scores_of(
                jnp.concatenate([left[line, first : first + big], mine], axis=1),
                jnp.concatenate([ext[line, reach], pot_lanes[reach]], axis=1),
            )

        score(0)
        for index in range(steps):
            slot = index % 2
            if index + 1 < steps:
                score(index + 1)
            for side in range(2):
                shift = side * block
                first = index * big + shift
                column_sum = jnp.zeros((8, window), jnp.float32)
                for row in range(0, block, strip):
                    rows = slice(shift + row, shift + row + strip)
                    logits = banded(raw[slot, rows, shift : shift + window], row, block)
                    peak = jnp.max(logits, axis=1, keepdims=True)
                    terms = jnp.exp2((logits - peak) * scale)
                    plan = terms * (1.0 / jnp.sum(terms, axis=1, keepdims=True))
                    column_sum += plan[:8] + plan[8:]
                    marked = strip_lanes
                    for part, piece in enumerate(split(peak, SHIFT)):
                        marked = jnp.where(lane == channels - SHIFT + part, piece, marked)
                    lanes[line, first + row : first + row + strip] = marked.astype(jnp.bfloat16)
                sums[:, first : first + window] += column_sum
        totals = jnp.sum(sums[...], axis=0, keepdims=True)
        prev_sum[pl.ds(line, 1), :] = totals[:, :seg_len]
        own_sum[pl.ds(line, 1), :] = totals[:, seg_len:]
        return carry

    lax.fori_loop(0, lines_here, one_line, 0)
    first_sum[...], second_sum[...] = by_parity(own_sum[...], prev_sum[...])
    sends = copies_of(
        (
            (first_sum, first_out),
            (second_sum, second_out),
            (own_sum, own_out),
            (prev_sum, prev_out),
            (pot, pot_out),
            (lanes, lanes_out),
        ),
        sems,
    )
    begin_copies(sends)
    wait(sends)


def row_pass(left, right, prev_low, prev_high, own, back, first, second, block):
    lines_here, seg_len, channels = left.shape
    bf16, f32 = jnp.bfloat16, jnp.float32
    part = (own.shape, f32)
    marginal = ((lines_here, seg_len), f32)
    pot = ((lines_here, 2 * seg_len), f32)
    lanes = (left.shape, bf16)
    return kernel_call(
        functools.partial(row_kernel, block),
        (left, right, prev_low, prev_high, own, back, first, second),
        (pot, lanes) + (marginal,) * 4,
        ((left.shape, bf16), ((lines_here, 2 * seg_len, channels), bf16))
        + (part,) * 4
        + (pot, lanes)
        + (marginal,) * 4
        + (
            ((2 * seg_len, channels), bf16),
            ((8, 2 * seg_len), f32),
            ((2, 2 * block, seg_len + 2 * block), f32),
        ),
        (4 * lines_here, 6),
        "row_pass",
    )


def transport_kernel(block, targets, outs, earlier, *refs):
    pot_in, lanes_in, left_in, right_in, prev_low_in, prev_high_in = refs[:6]
    own_in, back_in, first_in, second_in = refs[6:10]
    earlier_in = refs[10 : 10 + earlier]
    refs = refs[10 + earlier :]
    state_outs = refs[:outs]
    disp_out, first_px_out, second_px_out = refs[outs : outs + 3]
    (
        pot,
        lanes,
        left,
        ext,
        own,
        back,
        first_part,
        second_part,
        state,
        disp,
        first_px,
        second_px,
        pot_lanes,
        marks,
        raw,
        weights,
        line_sems,
        sems,
        send_sems,
    ) = refs[outs + 3 :]
    lines_here, seg_len, channels = left.shape
    scale = log2_scale(channels)
    big = 2 * block
    window = seg_len + big
    fetches = copies_of(
        (
            (pot_in, pot),
            (own_in, own),
            (back_in, back),
            (first_in, first_part),
            (second_in, second_part),
        )
        + tuple(zip(earlier_in, (disp, first_px, second_px))),
        sems,
    )
    begin_copies(fetches)
    pairs = feature_pairs(left_in, right_in, prev_low_in, prev_high_in, left, ext) + (
        (lanes_in, lanes),
    )
    for line, _, _ in targets:
        begin_copies(line_copies(pairs, line_sems, line, lines_here))
    lane = lax.broadcasted_iota(jnp.int32, (window, channels), 1)
    distance = seg_len - lax.broadcasted_iota(jnp.int32, (window, channels), 0)
    fine = jnp.bitwise_and(distance, 15)
    values = jnp.where(
        lane == 0,
        1,
        jnp.where(lane == 1, distance - fine, jnp.where(lane == 2, fine, 0)),
    )
    marks[...] = values.astype(jnp.float32).astype(jnp.bfloat16)
    wait(fetches)
    following, before = by_parity(first_part[...], second_part[...])
    total = jnp.concatenate([before + back[...], own[...] + following], axis=1)
    final = jnp.where(total > 0, pot[...] - jnp.log2(total), NEG)
    pot_lanes[...] = potential_lanes(final * (1.0 / scale), channels)
    offsets = lax.broadcasted_iota(jnp.int32, (1, big), 1).astype(jnp.float32)
    corner = jnp.zeros((block, block), jnp.bfloat16)
    steps = seg_len // big
    sends = []

    def one_line(line):
        wait(line_copies(pairs, line_sems, line, lines_here))

        def score(index):
            first = index * big
            rows, reach = slice(first, first + big), slice(first, first + window)
            raw[index % 2] = scores_of(
                jnp.concatenate([left[line, rows], lanes[line, rows]], axis=1),
                jnp.concatenate([ext[line, reach], pot_lanes[reach]], axis=1),
            )

        def weigh(index):
            slot = index % 2
            upper = jnp.exp2(banded(raw[slot, :block, : window - block], 0, block) * scale)
            lower = jnp.exp2(banded(raw[slot, block:, block:], 0, block) * scale)
            weights[slot, :block, : window - block] = upper.astype(jnp.bfloat16)
            weights[slot, :block, window - block :] = corner
            weights[slot, block:, block:] = lower.astype(jnp.bfloat16)
            weights[slot, block:, :block] = corner

        def gather(index):
            first = index * big
            rows = slice(first, first + big)
            table = jnp.concatenate([ext[line, first : first + window], marks[...]], axis=1)
            result = jnp.dot(weights[index % 2], table, preferred_element_type=jnp.float32)
            matched = result[:, :channels] * (1.0 / result[:, channels : channels + 1])
            state[line, rows] = (matched - left[line, rows].astype(jnp.float32)).astype(
                state.dtype
            )
            moments = result[:, channels:].T
            return offsets + (moments[1:2] + moments[2:3]) / moments[0:1]

        disparity = []
        for index in range(steps + 2):
            if index < steps:
                score(index)
            if index >= 2:
                disparity.append(gather(index - 2))
            if 1 <= index <= steps:
                weigh(index - 1)
        disp[line : line + 1, :] = jnp.concatenate(disparity, axis=1)
        high = state[line, seg_len - EDGE :].astype(jnp.float32)
        first, second = by_parity(high, state[line, :EDGE].astype(jnp.float32))
        first_px[line] = first.astype(jnp.bfloat16)
        second_px[line] = second.astype(jnp.bfloat16)

    for index, (line, out, place) in enumerate(targets):
        one_line(line)
        sends.append(
            pltpu.make_async_copy(state.at[line], state_outs[out].at[place], send_sems.at[index])
        )
        sends[-1].start()
    last = copies_of(
        ((first_px, first_px_out), (second_px, second_px_out), (disp, disp_out)),
        send_sems.at[pl.ds(len(targets), 3)],
    )
    begin_copies(last)
    wait(sends + last)


def transport(groups, earlier, pot, lanes, left, right, prev_low, prev_high, own, back, first, second, block):
    lines_here, seg_len, channels = left.shape
    bf16, f32 = jnp.bfloat16, jnp.float32
    side = ((lines_here, EDGE, channels), bf16)
    state = (left.shape, bf16)
    marginal = ((lines_here, seg_len), f32)
    window = seg_len + 2 * block
    targets = tuple(
        (line, out, place) for out, group in enumerate(groups) for place, line in enumerate(group)
    )
    return kernel_call(
        functools.partial(transport_kernel, block, targets, len(groups), len(earlier)),
        (pot, lanes, left, right, prev_low, prev_high, own, back, first, second) + earlier,
        tuple(((len(group), seg_len, channels), bf16) for group in groups)
        + (marginal, side, side),
        ((pot.shape, f32), (lanes.shape, bf16), state)
        + (((lines_here, 2 * seg_len, channels), bf16),)
        + (marginal,) * 4
        + (state, marginal, side, side)
        + (
            ((2 * seg_len, channels), bf16),
            ((window, channels), bf16),
            ((2, 2 * block, window), f32),
            ((2, 2 * block, window), bf16),
        ),
        (5 * lines_here, 8, len(targets) + 3),
        "transport",
        pl.CostEstimate(
            flops=len(targets) * 4 * seg_len * seg_len * channels,
            bytes_accessed=len(targets) * 8 * seg_len * channels,
            transcendentals=len(targets) * seg_len * seg_len,
        ),
    )


def stack_weights(weight_ref, stacked_ref):
    layers, taps, _, channels, _ = weight_ref.shape
    zeros = jnp.zeros((channels, channels), stacked_ref.dtype)
    for layer in range(layers):
        for col_tap in range(taps):
            for line in range(taps + 1):
                row = (col_tap * (taps + 1) + line) * channels
                for out in range(2):
                    row_tap = line - out
                    stacked_ref[
                        layer, row : row + channels, out * channels : (out + 1) * channels
                    ] = weight_ref[layer, row_tap, col_tap] if 0 <= row_tap < taps else zeros


def conv_kernel(
    first_line_in,
    middle_in,
    last_line_in,
    top_middle_in,
    top_last_in,
    bottom_first_in,
    bottom_middle_in,
    first_in,
    second_in,
    corner_top_in,
    corner_bottom_in,
    weight_in,
    bias_in,
    result_out,
    first_line_ref,
    middle_ref,
    last_line_ref,
    top_middle_ref,
    top_last_ref,
    bottom_first_ref,
    bottom_middle_ref,
    first_ref,
    second_ref,
    corner_top_ref,
    corner_bottom_ref,
    weight_ref,
    bias_ref,
    out_ref,
    first_image,
    second_image,
    sems,
    send_sems,
):
    fetches = copies_of(
        (
            (first_line_in, first_line_ref),
            (middle_in, middle_ref),
            (last_line_in, last_line_ref),
            (first_in, first_ref),
            (second_in, second_ref),
            (corner_top_in, corner_top_ref),
            (corner_bottom_in, corner_bottom_ref),
            (top_middle_in, top_middle_ref),
            (top_last_in, top_last_ref),
            (bottom_first_in, bottom_first_ref),
            (bottom_middle_in, bottom_middle_ref),
            (weight_in, weight_ref),
            (bias_in, bias_ref),
        ),
        sems,
    )
    begin_copies(fetches)
    lines_here, seg_len, channels = out_ref.shape
    layers = weight_ref.shape[0]
    after = layers + lines_here
    right = EDGE + seg_len
    f32 = jnp.float32
    wait(fetches)
    line = 0
    for part in (
        top_middle_ref,
        top_last_ref,
        first_line_ref,
        middle_ref,
        last_line_ref,
        bottom_first_ref,
        bottom_middle_ref,
    ):
        first_image[line : line + part.shape[0], EDGE:right] = part[...].astype(f32)
        line += part.shape[0]
    for rows, first_px, second_px in (
        (slice(layers, after), first_ref[...], second_ref[...]),
        (slice(0, layers), corner_top_ref[:, :EDGE], corner_top_ref[:, EDGE:]),
        (slice(after, None), corner_bottom_ref[:, :EDGE], corner_bottom_ref[:, EDGE:]),
    ):
        following, before = by_parity(first_px.astype(f32), second_px.astype(f32))
        first_image[rows, :EDGE] = before
        first_image[rows, right:] = following
    line0 = lax.axis_index("lines") * lines_here - layers
    all_lines = lax.axis_size("lines") * lines_here
    px0 = lax.axis_index("seg") * seg_len - EDGE
    all_px = lax.axis_size("seg") * seg_len
    source, target = first_image, second_image
    for layer in range(layers):
        reach = layers - 1 - layer
        begin, end = (EDGE // 2, right + EDGE // 2) if reach else (EDGE, right)
        middle = begin + seg_len // 2
        pieces = ((begin, middle), (middle, end))

        def pair(index, carry, layer=layer, reach=reach, pieces=pieces, source=source, target=target):
            base = layer + 2 * index
            for start, stop in pieces:
                size = stop - start
                taps = [
                    source[base + line, start + col_tap - 1 : start + col_tap - 1 + size].astype(jnp.bfloat16)
                    for col_tap in range(3)
                    for line in range(4)
                ]
                total = jnp.dot(
                    jnp.concatenate(taps, axis=1), weight_ref[layer], preferred_element_type=f32
                )
                for out in range(2):
                    line = base + 1 + out
                    part = total[:, out * channels : (out + 1) * channels] + bias_ref[layer : layer + 1]
                    updated = source[line, start : start + size] + jnp.maximum(part, 0.0)
                    if not reach:
                        out_ref[line - layers, start - EDGE : start - EDGE + size] = updated.astype(out_ref.dtype)
                        continue
                    image_line = line0 + line
                    inside = (image_line >= 0) & (image_line < all_lines)
                    if reach:
                        px = px0 + start + lax.broadcasted_iota(jnp.int32, updated.shape, 0)
                        inside = inside & (px >= 0) & (px < all_px)
                    updated = jnp.where(inside, updated, 0.0)
                    target[line, start : start + size] = updated.astype(jnp.bfloat16).astype(f32)
            if not reach:
                for line in (base + 1, base + 2):
                    begin_copies(line_copies(((out_ref, result_out),), send_sems, line - layers, lines_here))
            return carry

        lax.fori_loop(0, (lines_here + 2 * reach) // 2, pair, 0, unroll=True)
        source, target = target, source
    for line in range(lines_here):
        wait(line_copies(((out_ref, result_out),), send_sems, line, lines_here))


def conv_layers(lines_here, lines, edges, weight, bias):
    layers = weight.shape[0]
    seg_len, channels = lines[0].shape[1:]
    image = ((lines_here + 2 * layers, seg_len + 2 * EDGE, channels), jnp.float32)
    operands = lines + edges + (weight, bias)
    result = ((lines_here, seg_len, channels), jnp.bfloat16)
    return kernel_call(
        conv_kernel,
        operands,
        (result,),
        tuple((operand.shape, operand.dtype) for operand in operands) + (result, image, image),
        (len(operands), lines_here),
        "conv_layers",
    )[0]


def shards(left_features, right_features, conv_weight, conv_bias):
    seg_len = left_features.shape[1]
    half = seg_len // 2
    prev_high = shifted(right_features[:, half:], "seg", 1)
    next_low = shifted(left_features[:, :half], "seg", -1)
    stacked, own = own_partials(left_features, right_features, conv_weight)
    right_low, own = lax.optimization_barrier((right_features[:, :half], own))
    prev_low = shifted(right_low, "seg", 1)
    back = cross_partials(left_features, prev_high)
    own, first, second = next_partials(next_low, right_features, own, back)
    first = exchanged(first, "seg", 0)
    second = exchanged(second, "seg", 1)
    block = min(128, half)
    pot, lanes, own, back, first, second = row_pass(
        left_features, right_features, prev_low, prev_high, own, back, first, second, block
    )
    first = exchanged(first, "seg", 0)
    second = exchanged(second, "seg", 1)
    lines_here, layers = left_features.shape[0], conv_weight.shape[0]
    low, high = tuple(range(lines_here - layers)), tuple(range(layers, lines_here))
    shared = tuple(range(lines_here - layers, layers))
    given = (
        pot, lanes, left_features, right_features, prev_low, prev_high, own, back, first, second, block
    )
    middle, *earlier = transport((shared,), (), *given)
    bottom_middle = shifted(middle, "lines", -1)
    top_middle = shifted(middle, "lines", 1)
    first_line, last_line, disparity, first, second = transport((low, high), tuple(earlier), *given)
    bottom_first = shifted(first_line, "lines", -1)
    top_last = shifted(last_line, "lines", 1)
    first = exchanged(first, "seg", 0)
    second = exchanged(second, "seg", 1)
    edges = jnp.concatenate([first, second], axis=1)
    corners_bottom = shifted(edges[:layers], "lines", -1)
    corners_top = shifted(edges[-layers:], "lines", 1)
    refined = conv_layers(
        lines_here,
        (first_line, middle, last_line, top_middle, top_last, bottom_first, bottom_middle),
        (first, second, corners_top, corners_bottom),
        stacked,
        conv_bias,
    )
    return (refined, disparity)


def solution(mesh):
    return jax.shard_map(
        shards,
        mesh=mesh,
        in_specs=(P("lines", "seg", None), P("lines", "seg", None), P(), P()),
        out_specs=(P("lines", "seg", None), P("lines", "seg")),
        check_vma=False,
    )
```

```python
import functools
import math

import jax
import jax.numpy as jnp
from jax import lax
from jax.experimental import pallas as pl
from jax.experimental.pallas import tpu as pltpu
from jax.sharding import PartitionSpec as P

DISP = 1024
NEG = -1e30
EDGE = 16
VMEM_BYTES = 32 * 1024 * 1024


def shifted(block, axis, step):
    count = lax.axis_size(axis)
    route = [(i, i + step) for i in range(count) if 0 <= i + step < count]
    return lax.ppermute(block, axis, route)


def exchanged(block, axis, odd):
    route = []
    for low in range(odd, lax.axis_size(axis) - 1, 2):
        route += [(low, low + 1), (low + 1, low)]
    return lax.ppermute(block, axis, route)


def even_segment():
    return lax.rem(lax.axis_index("seg"), 2) == 0


def by_parity(following, previous):
    even = even_segment()
    return jnp.where(even, following, previous), jnp.where(even, previous, following)


def params():
    return pltpu.CompilerParams(vmem_limit_bytes=VMEM_BYTES)


ANYWHERE = pl.BlockSpec(memory_space=pl.ANY)


def kernel_call(kernel, operands, results, scratch, copies, name, cost=None):
    return pl.pallas_call(
        kernel,
        in_specs=[ANYWHERE] * len(operands),
        out_specs=[ANYWHERE] * len(results),
        out_shape=[jax.ShapeDtypeStruct(shape, dtype) for shape, dtype in results],
        scratch_shapes=[pltpu.VMEM(shape, dtype) for shape, dtype in scratch]
        + [pltpu.SemaphoreType.DMA((count,)) for count in copies],
        compiler_params=params(),
        cost_estimate=cost,
        name=name,
    )(*operands)


def copies_of(pairs, sems):
    return [
        pltpu.make_async_copy(source, target, sems.at[index])
        for index, (source, target) in enumerate(pairs)
    ]


def line_copies(pairs, sems, line, lines_here):
    return [
        pltpu.make_async_copy(source.at[line], target.at[line], sems.at[index * lines_here + line])
        for index, (source, target) in enumerate(pairs)
    ]


def begin_copies(copies):
    for copy in copies:
        copy.start()


def wait(copies):
    for copy in copies:
        copy.wait()


def scores_of(left, right):
    return lax.dot_general(
        left, right, (((1,), (1,)), ((), ())), preferred_element_type=jnp.float32
    )


def log2_scale(channels):
    return math.log2(math.e) / math.sqrt(channels)


def over_rows(reduce, values, chains=64):
    count, width = values.shape
    while count > chains >= 8 and count % chains == 0:
        values = reduce(values.reshape(count // chains, chains, width), axis=0)
        count, chains = chains, chains // 8
    return reduce(values, axis=0, keepdims=True)


def column_block(left, right, diagonal_first):
    block, channels = right.shape
    scale = log2_scale(channels)
    raw = scores_of(left, right)
    row_ids = lax.broadcasted_iota(jnp.int32, (block, block), 0)
    col_ids = lax.broadcasted_iota(jnp.int32, (block, block), 1)
    if diagonal_first:
        parts = [jnp.where(col_ids <= row_ids, raw[:block], NEG), raw[block:]]
    else:
        parts = [raw[:-block], jnp.where(col_ids > row_ids, raw[-block:], NEG)]
    parts = [part for part in parts if part.shape[0]]
    peak = functools.reduce(jnp.maximum, [over_rows(jnp.max, part) for part in parts])
    total = sum(over_rows(jnp.sum, jnp.exp2((part - peak) * scale)) for part in parts)
    return (peak * scale, total)


def own_kernel(
    block,
    left_in,
    right_in,
    weight_in,
    stacked_out,
    part_out,
    left,
    right,
    weight,
    stacked,
    part,
    line_sems,
    sems,
):
    lines_here, seg_len = left.shape[:2]
    pairs = ((left_in, left), (right_in, right))
    for line in range(lines_here):
        begin_copies(line_copies(pairs, line_sems, line, lines_here))
    fetch, send_stacked, send_part = copies_of(
        ((weight_in, weight), (stacked, stacked_out), (part, part_out)), sems
    )
    fetch.start()

    def one_line(line, carry):
        wait(line_copies(pairs, line_sems, line, lines_here))
        for first in range(0, seg_len, block):
            cols = slice(first, first + block)
            peak, total = column_block(left[line, first:], right[line, cols], True)
            part[pl.ds(line, 1), cols] = peak
            part[pl.ds(lines_here + line, 1), cols] = total
        return carry

    lax.fori_loop(0, lines_here, one_line, 0)
    send_part.start()
    fetch.wait()
    stack_weights(weight, stacked)
    send_stacked.start()
    send_part.wait()
    send_stacked.wait()


def column_cost(lines_here, seg_len, channels):
    return pl.CostEstimate(
        flops=2 * lines_here * seg_len * seg_len * channels,
        bytes_accessed=8 * lines_here * seg_len * channels,
        transcendentals=lines_here * seg_len * seg_len // 2,
    )


def own_partials(left, right, weight):
    lines_here, seg_len, channels = left.shape
    bf16, f32 = jnp.bfloat16, jnp.float32
    stacked = ((weight.shape[0], 12 * channels, 2 * channels), bf16)
    part = ((2 * lines_here, seg_len), f32)
    return kernel_call(
        functools.partial(own_kernel, min(256, seg_len)),
        (left, right, weight),
        (stacked, part),
        ((left.shape, bf16), (right.shape, bf16), (weight.shape, bf16), stacked, part),
        (2 * lines_here, 3),
        "column_own",
        column_cost(*left.shape),
    )


def next_kernel(
    block,
    next_in,
    right_in,
    own_in,
    back_in,
    merged_out,
    first_out,
    second_out,
    following,
    right,
    merged,
    back,
    first_part,
    second_part,
    line_sems,
    sems,
):
    lines_here, half = following.shape[:2]
    pairs = ((next_in, following), (right_in.at[:, pl.ds(0, half)], right))
    fetches = copies_of(((own_in, merged), (back_in, back)), sems)
    sends = copies_of(
        ((first_part, first_out), (second_part, second_out), (merged, merged_out)),
        sems.at[pl.ds(2, 3)],
    )
    begin_copies(fetches)
    for line in range(lines_here):
        begin_copies(line_copies(pairs, line_sems, line, lines_here))
    wait(fetches)
    last = lax.axis_index("seg") == lax.axis_size("seg") - 1

    def one_line(line, carry):
        wait(line_copies(pairs, line_sems, line, lines_here))
        top, bottom = pl.ds(line, 1), pl.ds(lines_here + line, 1)
        for first in range(0, half, block):
            cols = slice(first, first + block)
            peak, total = column_block(following[line, : first + block], right[line, cols], False)
            peak = jnp.where(last, NEG, peak)
            total = jnp.where(last, 0.0, total)
            own_peak = merged[top, cols]
            joint = jnp.maximum(own_peak, peak)
            merged[bottom, cols] = merged[bottom, cols] * jnp.exp2(
                own_peak - joint
            ) + total * jnp.exp2(peak - joint)
            merged[top, cols] = joint
        return carry

    lax.fori_loop(0, lines_here, one_line, 0)
    first_part[...], second_part[...] = by_parity(merged[...], back[...])
    begin_copies(sends)
    wait(sends)


def next_partials(next_low, right, own, back):
    lines_here, half, channels = next_low.shape
    part = (own.shape, jnp.float32)
    features = (next_low.shape, jnp.bfloat16)
    return kernel_call(
        functools.partial(next_kernel, min(256, half)),
        (next_low, right, own, back),
        (part,) * 3,
        (features, features) + (part,) * 4,
        (2 * lines_here, 5),
        "column_next",
        column_cost(lines_here, half, channels),
    )


def cross_kernel(block, left_in, prev_in, back_out, left, prev, back, line_sems, sems):
    lines_here, seg_len = left.shape[:2]
    half = seg_len - prev.shape[1]
    pairs = ((left_in, left), (prev_in, prev))
    for line in range(lines_here):
        begin_copies(line_copies(pairs, line_sems, line, lines_here))
    (send,) = copies_of(((back, back_out),), sems)
    back[...] = jnp.zeros_like(back)

    def one_line(line, carry):
        wait(line_copies(pairs, line_sems, line, lines_here))
        top, bottom = pl.ds(line, 1), pl.ds(lines_here + line, 1)
        for first in range(0, prev.shape[1], block):
            cols = slice(first, first + block)
            peak, total = column_block(
                left[line, : half + first + block], prev[line, cols], False
            )
            back[top, cols] = peak
            back[bottom, cols] = total
        return carry

    lax.fori_loop(0, lines_here, one_line, 0)
    send.start()
    send.wait()


def cross_partials(left, prev_high):
    lines_here, seg_len, channels = left.shape
    part = ((2 * lines_here, seg_len), jnp.float32)
    return kernel_call(
        functools.partial(cross_kernel, min(256, prev_high.shape[1])),
        (left, prev_high),
        (part,),
        ((left.shape, jnp.bfloat16), (prev_high.shape, jnp.bfloat16), part),
        (2 * lines_here, 1),
        "column_cross",
        column_cost(*left.shape),
    )[0]


def potential(peak, total):
    return -(peak + jnp.log2(total))


def merged_potential(first, second):
    first_max = jnp.where(first[1] > 0, first[0], NEG)
    second_max = jnp.where(second[1] > 0, second[0], NEG)
    peak = jnp.maximum(first_max, second_max)
    total = first[1] * jnp.exp2(first_max - peak) + second[1] * jnp.exp2(second_max - peak)
    return potential(peak, total)


def split(values, parts):
    pieces = []
    for _ in range(parts):
        piece = values.astype(jnp.bfloat16).astype(jnp.float32)
        pieces.append(piece)
        values = values - piece
    return pieces


SHIFT = 2


def potential_lanes(pot, channels):
    lines_here, count = pot.shape
    parts = split(pot, 3)
    filler = jnp.zeros((channels - 3 * lines_here, count), jnp.float32)
    lanes = jnp.concatenate(parts + [filler], axis=0).T
    lane = lax.broadcasted_iota(jnp.int32, lanes.shape, 1)
    return jnp.where(lane >= channels - SHIFT, -1.0, lanes).astype(jnp.bfloat16)


def line_lanes(line, lines_here, shape):
    lane = lax.broadcasted_iota(jnp.int32, shape, 1)
    mine = jnp.zeros(shape, jnp.float32)
    for part in range(3):
        mine = jnp.where(lane == part * lines_here + line, 1.0, mine)
    return mine


def banded(values, row, block):
    rows, window = values.shape
    col_ids = lax.broadcasted_iota(jnp.int32, (rows, block), 1)
    row_ids = lax.broadcasted_iota(jnp.int32, (rows, block), 0) + row
    return jnp.concatenate(
        [
            jnp.where(col_ids > row_ids, values[:, :block], NEG),
            values[:, block : window - block],
            jnp.where(col_ids <= row_ids, values[:, window - block :], NEG),
        ],
        axis=1,
    )


def feature_pairs(left_in, right_in, prev_low_in, prev_high_in, left, ext):
    seg_len, half = left.shape[1], prev_low_in.shape[1]
    return (
        (left_in, left),
        (prev_low_in, ext.at[:, pl.ds(0, half)]),
        (prev_high_in, ext.at[:, pl.ds(half, seg_len - half)]),
        (right_in, ext.at[:, pl.ds(seg_len, seg_len)]),
    )


def row_kernel(
    block,
    left_in,
    right_in,
    prev_low_in,
    prev_high_in,
    own_in,
    back_in,
    first_in,
    second_in,
    pot_out,
    lanes_out,
    own_out,
    prev_out,
    first_out,
    second_out,
    left,
    ext,
    own,
    back,
    first_part,
    second_part,
    pot,
    lanes,
    own_sum,
    prev_sum,
    first_sum,
    second_sum,
    pot_lanes,
    sums,
    raw,
    line_sems,
    sems,
    lane_sems,
):
    lines_here, seg_len, channels = left.shape
    half = prev_low_in.shape[1]
    scale = log2_scale(channels)
    fetches = copies_of(
        ((own_in, own), (back_in, back), (first_in, first_part), (second_in, second_part)), sems
    )
    begin_copies(fetches)
    pairs = feature_pairs(left_in, right_in, prev_low_in, prev_high_in, left, ext)
    for line in range(lines_here):
        begin_copies(line_copies(pairs, line_sems, line, lines_here))
    wait(fetches)

    following, before = by_parity(first_part[...], second_part[...])

    def parts(part, first, stop):
        return part[:lines_here, first:stop], part[lines_here:, first:stop]

    rest = seg_len - half
    pot[:, seg_len : seg_len + half] = potential(*parts(own, 0, half))
    pot[:, seg_len + half :] = merged_potential(
        parts(own, half, seg_len), parts(following, 0, rest)
    )
    low = parts(before, 0, half)
    high = parts(before, half, seg_len)
    pot[:, :half] = jnp.where(low[1] > 0, potential(*low), NEG)
    pot[:, half:seg_len] = jnp.where(
        high[1] > 0, merged_potential(high, parts(back, 0, rest)), NEG
    )
    pot_lanes[...] = potential_lanes(pot[...] * (1.0 / scale), channels)
    window = seg_len + block
    big = 2 * block
    steps = seg_len // big
    strip = 16
    lane = lax.broadcasted_iota(jnp.int32, (strip, channels), 1)

    def one_line(line, carry):
        wait(line_copies(pairs, line_sems, line, lines_here))
        sums[...] = jnp.zeros_like(sums)
        mine = line_lanes(line, lines_here, (big, channels)).astype(jnp.bfloat16)
        strip_lanes = line_lanes(line, lines_here, (strip, channels))

        def score(index):
            first = index * big
            reach = slice(first, first + seg_len + big)
            raw[index % 2] = scores_of(
                jnp.concatenate([left[line, first : first + big], mine], axis=1),
                jnp.concatenate([ext[line, reach], pot_lanes[reach]], axis=1),
            )

        score(0)
        for index in range(steps):
            slot = index % 2
            if index + 1 < steps:
                score(index + 1)
            for side in range(2):
                shift = side * block
                first = index * big + shift
                column_sum = jnp.zeros((8, window), jnp.float32)
                for row in range(0, block, strip):
                    rows = slice(shift + row, shift + row + strip)
                    logits = banded(raw[slot, rows, shift : shift + window], row, block)
                    peak = jnp.max(logits, axis=1, keepdims=True)
                    terms = jnp.exp2((logits - peak) * scale)
                    plan = terms * (1.0 / jnp.sum(terms, axis=1, keepdims=True))
                    column_sum += plan[:8] + plan[8:]
                    marked = strip_lanes
                    for part, piece in enumerate(split(peak, SHIFT)):
                        marked = jnp.where(lane == channels - SHIFT + part, piece, marked)
                    lanes[line, first + row : first + row + strip] = marked.astype(jnp.bfloat16)
                sums[:, first : first + window] += column_sum
        totals = jnp.sum(sums[...], axis=0, keepdims=True)
        begin_copies(line_copies(((lanes, lanes_out),), lane_sems, line, lines_here))
        prev_sum[pl.ds(line, 1), :] = totals[:, :seg_len]
        own_sum[pl.ds(line, 1), :] = totals[:, seg_len:]
        return carry

    lax.fori_loop(0, lines_here, one_line, 0)
    first_sum[...], second_sum[...] = by_parity(own_sum[...], prev_sum[...])
    sends = copies_of(
        (
            (first_sum, first_out),
            (second_sum, second_out),
            (own_sum, own_out),
            (prev_sum, prev_out),
            (pot, pot_out),
        ),
        sems,
    )
    begin_copies(sends)
    wait(sends)
    for line in range(lines_here):
        wait(line_copies(((lanes, lanes_out),), lane_sems, line, lines_here))


def row_pass(left, right, prev_low, prev_high, own, back, first, second, block):
    lines_here, seg_len, channels = left.shape
    bf16, f32 = jnp.bfloat16, jnp.float32
    part = (own.shape, f32)
    marginal = ((lines_here, seg_len), f32)
    pot = ((lines_here, 2 * seg_len), f32)
    lanes = (left.shape, bf16)
    return kernel_call(
        functools.partial(row_kernel, block),
        (left, right, prev_low, prev_high, own, back, first, second),
        (pot, lanes) + (marginal,) * 4,
        ((left.shape, bf16), ((lines_here, 2 * seg_len, channels), bf16))
        + (part,) * 4
        + (pot, lanes)
        + (marginal,) * 4
        + (
            ((2 * seg_len, channels), bf16),
            ((8, 2 * seg_len), f32),
            ((2, 2 * block, seg_len + 2 * block), f32),
        ),
        (4 * lines_here, 5, lines_here),
        "row_pass",
    )


def transport_kernel(
    block,
    pot_in,
    lanes_in,
    left_in,
    right_in,
    prev_low_in,
    prev_high_in,
    own_in,
    back_in,
    first_in,
    second_in,
    state_out,
    disp_out,
    first_out,
    last_out,
    first_px_out,
    second_px_out,
    pot,
    lanes,
    left,
    ext,
    own,
    back,
    first_part,
    second_part,
    state,
    disp,
    first_px,
    second_px,
    pot_lanes,
    marks,
    raw,
    weights,
    line_sems,
    sems,
    send_sems,
):
    lines_here, seg_len, channels = left.shape
    layers = first_out.shape[0]
    scale = log2_scale(channels)
    big = 2 * block
    window = seg_len + big
    fetches = copies_of(
        (
            (pot_in, pot),
            (own_in, own),
            (back_in, back),
            (first_in, first_part),
            (second_in, second_part),
        ),
        sems,
    )
    begin_copies(fetches)
    pairs = feature_pairs(left_in, right_in, prev_low_in, prev_high_in, left, ext) + (
        (lanes_in, lanes),
    )
    for line in range(lines_here):
        begin_copies(line_copies(pairs, line_sems, line, lines_here))
    lane = lax.broadcasted_iota(jnp.int32, (window, channels), 1)
    distance = seg_len - lax.broadcasted_iota(jnp.int32, (window, channels), 0)
    fine = jnp.bitwise_and(distance, 15)
    values = jnp.where(
        lane == 0,
        1,
        jnp.where(lane == 1, distance - fine, jnp.where(lane == 2, fine, 0)),
    )
    marks[...] = values.astype(jnp.float32).astype(jnp.bfloat16)
    wait(fetches)
    following, before = by_parity(first_part[...], second_part[...])
    total = jnp.concatenate([before + back[...], own[...] + following], axis=1)
    final = jnp.where(total > 0, pot[...] - jnp.log2(total), NEG)
    pot_lanes[...] = potential_lanes(final * (1.0 / scale), channels)
    offsets = lax.broadcasted_iota(jnp.int32, (1, big), 1).astype(jnp.float32)
    corner = jnp.zeros((block, block), jnp.bfloat16)
    steps = seg_len // big

    def one_line(line, carry):
        wait(line_copies(pairs, line_sems, line, lines_here))

        def score(index):
            first = index * big
            rows, reach = slice(first, first + big), slice(first, first + window)
            raw[index % 2] = scores_of(
                jnp.concatenate([left[line, rows], lanes[line, rows]], axis=1),
                jnp.concatenate([ext[line, reach], pot_lanes[reach]], axis=1),
            )

        def weigh(index):
            slot = index % 2
            upper = jnp.exp2(banded(raw[slot, :block, : window - block], 0, block) * scale)
            lower = jnp.exp2(banded(raw[slot, block:, block:], 0, block) * scale)
            weights[slot, :block, : window - block] = upper.astype(jnp.bfloat16)
            weights[slot, :block, window - block :] = corner
            weights[slot, block:, block:] = lower.astype(jnp.bfloat16)
            weights[slot, block:, :block] = corner

        def gather(index):
            first = index * big
            rows = slice(first, first + big)
            table = jnp.concatenate([ext[line, first : first + window], marks[...]], axis=1)
            result = jnp.dot(weights[index % 2], table, preferred_element_type=jnp.float32)
            matched = result[:, :channels] * (1.0 / result[:, channels : channels + 1])
            state[line, rows] = (matched - left[line, rows].astype(jnp.float32)).astype(
                state.dtype
            )
            moments = result[:, channels:].T
            return offsets + (moments[1:2] + moments[2:3]) / moments[0:1]

        disparity = []
        for index in range(steps + 2):
            if index < steps:
                score(index)
            if index >= 2:
                disparity.append(gather(index - 2))
            if 1 <= index <= steps:
                weigh(index - 1)
        disp[pl.ds(line, 1), :] = jnp.concatenate(disparity, axis=1)
        begin_copies(line_copies(((state, state_out),), send_sems, line, lines_here))
        high = state[line, seg_len - EDGE :].astype(jnp.float32)
        first, second = by_parity(high, state[line, :EDGE].astype(jnp.float32))
        first_px[line] = first.astype(jnp.bfloat16)
        second_px[line] = second.astype(jnp.bfloat16)

        @pl.when(line < layers)
        def _():
            pltpu.make_async_copy(state.at[line], first_out.at[line], sems.at[line]).start()

        @pl.when(line >= lines_here - layers)
        def _():
            target = line - (lines_here - layers)
            pltpu.make_async_copy(
                state.at[line], last_out.at[target], sems.at[layers + target]
            ).start()

        return carry

    lax.fori_loop(0, lines_here, one_line, 0)
    sends = copies_of(
        ((first_px, first_px_out), (second_px, second_px_out), (disp, disp_out)),
        send_sems.at[pl.ds(lines_here, 3)],
    )
    begin_copies(sends)
    for line in range(layers):
        pltpu.make_async_copy(state.at[line], first_out.at[line], sems.at[line]).wait()
        source = line + lines_here - layers
        pltpu.make_async_copy(state.at[source], last_out.at[line], sems.at[layers + line]).wait()
    for line in range(lines_here):
        wait(line_copies(((state, state_out),), send_sems, line, lines_here))
    wait(sends)


def transport(pot, lanes, left, right, prev_low, prev_high, own, back, first, second, block, layers):
    lines_here, seg_len, channels = left.shape
    bf16, f32 = jnp.bfloat16, jnp.float32
    edge = ((layers, seg_len, channels), bf16)
    side = ((lines_here, EDGE, channels), bf16)
    state = (left.shape, bf16)
    marginal = ((lines_here, seg_len), f32)
    window = seg_len + 2 * block
    return kernel_call(
        functools.partial(transport_kernel, block),
        (pot, lanes, left, right, prev_low, prev_high, own, back, first, second),
        (state, marginal, edge, edge, side, side),
        ((pot.shape, f32), (lanes.shape, bf16), state)
        + (((lines_here, 2 * seg_len, channels), bf16),)
        + (marginal,) * 4
        + (state, marginal, side, side)
        + (
            ((2 * seg_len, channels), bf16),
            ((window, channels), bf16),
            ((2, 2 * block, window), f32),
            ((2, 2 * block, window), bf16),
        ),
        (5 * lines_here, max(5, 2 * layers), lines_here + 3),
        "transport",
    )


def stack_weights(weight_ref, stacked_ref):
    layers, taps, _, channels, _ = weight_ref.shape
    zeros = jnp.zeros((channels, channels), stacked_ref.dtype)
    for layer in range(layers):
        for col_tap in range(taps):
            for line in range(taps + 1):
                row = (col_tap * (taps + 1) + line) * channels
                for out in range(2):
                    row_tap = line - out
                    stacked_ref[
                        layer, row : row + channels, out * channels : (out + 1) * channels
                    ] = weight_ref[layer, row_tap, col_tap] if 0 <= row_tap < taps else zeros


def conv_kernel(
    state_in,
    top_in,
    bottom_in,
    first_in,
    second_in,
    corner_top_in,
    corner_bottom_in,
    weight_in,
    bias_in,
    result_out,
    state_ref,
    top_ref,
    bottom_ref,
    first_ref,
    second_ref,
    corner_top_ref,
    corner_bottom_ref,
    weight_ref,
    bias_ref,
    out_ref,
    first_image,
    second_image,
    sems,
    send_sems,
):
    fetches = copies_of(
        (
            (state_in, state_ref),
            (first_in, first_ref),
            (second_in, second_ref),
            (corner_top_in, corner_top_ref),
            (corner_bottom_in, corner_bottom_ref),
            (top_in, top_ref),
            (bottom_in, bottom_ref),
            (weight_in, weight_ref),
            (bias_in, bias_ref),
        ),
        sems,
    )
    begin_copies(fetches)
    lines_here, seg_len, channels = state_ref.shape
    layers = weight_ref.shape[0]
    after = layers + lines_here
    right = EDGE + seg_len
    f32 = jnp.float32
    wait(fetches[:1])
    first_image[layers:after, EDGE:right] = state_ref[...].astype(f32)
    wait(fetches[1:-2])
    first_image[:layers, EDGE:right] = top_ref[...].astype(f32)
    first_image[after:, EDGE:right] = bottom_ref[...].astype(f32)
    for rows, first_px, second_px in (
        (slice(layers, after), first_ref[...], second_ref[...]),
        (slice(0, layers), corner_top_ref[:, :EDGE], corner_top_ref[:, EDGE:]),
        (slice(after, None), corner_bottom_ref[:, :EDGE], corner_bottom_ref[:, EDGE:]),
    ):
        following, before = by_parity(first_px.astype(f32), second_px.astype(f32))
        first_image[rows, :EDGE] = before
        first_image[rows, right:] = following
    wait(fetches[-2:])
    line0 = lax.axis_index("lines") * lines_here - layers
    all_lines = lax.axis_size("lines") * lines_here
    px0 = lax.axis_index("seg") * seg_len - EDGE
    all_px = lax.axis_size("seg") * seg_len
    source, target = first_image, second_image
    for layer in range(layers):
        reach = layers - 1 - layer
        begin, end = (EDGE // 2, right + EDGE // 2) if reach else (EDGE, right)
        middle = begin + seg_len // 2
        pieces = ((begin, middle), (middle, end))

        def pair(index, carry, layer=layer, reach=reach, pieces=pieces, source=source, target=target):
            base = layer + 2 * index
            for start, stop in pieces:
                size = stop - start
                taps = [
                    source[base + line, start + col_tap - 1 : start + col_tap - 1 + size].astype(jnp.bfloat16)
                    for col_tap in range(3)
                    for line in range(4)
                ]
                total = jnp.dot(
                    jnp.concatenate(taps, axis=1), weight_ref[layer], preferred_element_type=f32
                )
                for out in range(2):
                    line = base + 1 + out
                    part = total[:, out * channels : (out + 1) * channels] + bias_ref[layer : layer + 1]
                    updated = source[line, start : start + size] + jnp.maximum(part, 0.0)
                    if not reach:
                        out_ref[line - layers, start - EDGE : start - EDGE + size] = updated.astype(out_ref.dtype)
                        continue
                    image_line = line0 + line
                    inside = (image_line >= 0) & (image_line < all_lines)
                    if reach:
                        px = px0 + start + lax.broadcasted_iota(jnp.int32, updated.shape, 0)
                        inside = inside & (px >= 0) & (px < all_px)
                    updated = jnp.where(inside, updated, 0.0)
                    target[line, start : start + size] = updated.astype(jnp.bfloat16).astype(f32)
            if not reach:
                for line in (base + 1, base + 2):
                    begin_copies(line_copies(((out_ref, result_out),), send_sems, line - layers, lines_here))
            return carry

        lax.fori_loop(0, (lines_here + 2 * reach) // 2, pair, 0, unroll=True)
        source, target = target, source
    for line in range(lines_here):
        wait(line_copies(((out_ref, result_out),), send_sems, line, lines_here))


def conv_layers(state, top, bottom, left_px, right_px, corners_top, corners_bottom, weight, bias):
    layers = weight.shape[0]
    lines_here, seg_len, channels = state.shape
    image = ((lines_here + 2 * layers, seg_len + 2 * EDGE, channels), jnp.float32)
    operands = (state, top, bottom, left_px, right_px, corners_top, corners_bottom, weight, bias)
    result = (state.shape, state.dtype)
    return kernel_call(
        conv_kernel,
        operands,
        (result,),
        tuple((operand.shape, operand.dtype) for operand in operands) + (result, image, image),
        (len(operands), lines_here),
        "conv_layers",
    )[0]


def shards(left_features, right_features, conv_weight, conv_bias):
    seg_len = left_features.shape[1]
    half = seg_len // 2
    layers = conv_weight.shape[0]
    prev_high = shifted(right_features[:, half:], "seg", 1)
    next_low = shifted(left_features[:, :half], "seg", -1)
    stacked, own = own_partials(left_features, right_features, conv_weight)
    right_low, own = lax.optimization_barrier((right_features[:, :half], own))
    prev_low = shifted(right_low, "seg", 1)
    back = cross_partials(left_features, prev_high)
    own, first, second = next_partials(next_low, right_features, own, back)
    first = exchanged(first, "seg", 0)
    second = exchanged(second, "seg", 1)
    block = min(128, half)
    pot, lanes, own, back, first, second = row_pass(
        left_features, right_features, prev_low, prev_high, own, back, first, second, block
    )
    first = exchanged(first, "seg", 0)
    second = exchanged(second, "seg", 1)
    state, disparity, first_lines, last_lines, first, second = transport(
        pot, lanes, left_features, right_features, prev_low, prev_high, own, back, first, second, block, layers
    )
    bottom = shifted(first_lines, "lines", -1)
    top = shifted(last_lines, "lines", 1)
    first = exchanged(first, "seg", 0)
    second = exchanged(second, "seg", 1)
    edges = jnp.concatenate([first, second], axis=1)
    corners_bottom = shifted(edges[:layers], "lines", -1)
    corners_top = shifted(edges[-layers:], "lines", 1)
    refined = conv_layers(
        state, top, bottom, first, second, corners_top, corners_bottom, stacked, conv_bias
    )
    return (refined, disparity)


def solution(mesh):
    return jax.shard_map(
        shards,
        mesh=mesh,
        in_specs=(P("lines", "seg", None), P("lines", "seg", None), P(), P()),
        out_specs=(P("lines", "seg", None), P("lines", "seg")),
        check_vma=False,
    )
```

```python
import functools
import math

import jax
import jax.numpy as jnp
from jax import lax
from jax.experimental import pallas as pl
from jax.experimental.pallas import tpu as pltpu
from jax.sharding import PartitionSpec as P

DISP = 1024
NEG = -1e30
EDGE = 16
VMEM_BYTES = 32 * 1024 * 1024


def shifted(block, axis, step):
    count = lax.axis_size(axis)
    route = [(i, i + step) for i in range(count) if 0 <= i + step < count]
    return lax.ppermute(block, axis, route)


def exchanged(block, axis, odd):
    route = []
    for low in range(odd, lax.axis_size(axis) - 1, 2):
        route += [(low, low + 1), (low + 1, low)]
    return lax.ppermute(block, axis, route)


def even_segment():
    return lax.rem(lax.axis_index("seg"), 2) == 0


def by_parity(following, previous):
    even = even_segment()
    return jnp.where(even, following, previous), jnp.where(even, previous, following)


def params():
    return pltpu.CompilerParams(vmem_limit_bytes=VMEM_BYTES)


ANYWHERE = pl.BlockSpec(memory_space=pl.ANY)


def kernel_call(kernel, operands, results, scratch, copies, name, cost=None):
    return pl.pallas_call(
        kernel,
        in_specs=[ANYWHERE] * len(operands),
        out_specs=[ANYWHERE] * len(results),
        out_shape=[jax.ShapeDtypeStruct(shape, dtype) for shape, dtype in results],
        scratch_shapes=[pltpu.VMEM(shape, dtype) for shape, dtype in scratch]
        + [pltpu.SemaphoreType.DMA((count,)) for count in copies],
        compiler_params=params(),
        cost_estimate=cost,
        name=name,
    )(*operands)


def copies_of(pairs, sems):
    return [
        pltpu.make_async_copy(source, target, sems.at[index])
        for index, (source, target) in enumerate(pairs)
    ]


def line_copies(pairs, sems, line, lines_here):
    return [
        pltpu.make_async_copy(source.at[line], target.at[line], sems.at[index * lines_here + line])
        for index, (source, target) in enumerate(pairs)
    ]


def begin_copies(copies):
    for copy in copies:
        copy.start()


def wait(copies):
    for copy in copies:
        copy.wait()


def scores_of(left, right):
    return lax.dot_general(
        left, right, (((1,), (1,)), ((), ())), preferred_element_type=jnp.float32
    )


def log2_scale(channels):
    return math.log2(math.e) / math.sqrt(channels)


def over_rows(reduce, values, chains=64):
    count, width = values.shape
    while count > chains >= 8 and count % chains == 0:
        values = reduce(values.reshape(count // chains, chains, width), axis=0)
        count, chains = chains, chains // 8
    return reduce(values, axis=0, keepdims=True)


def column_block(left, right, diagonal_first):
    block, channels = right.shape
    scale = log2_scale(channels)
    raw = scores_of(left, right)
    row_ids = lax.broadcasted_iota(jnp.int32, (block, block), 0)
    col_ids = lax.broadcasted_iota(jnp.int32, (block, block), 1)
    if diagonal_first:
        parts = [jnp.where(col_ids <= row_ids, raw[:block], NEG), raw[block:]]
    else:
        parts = [raw[:-block], jnp.where(col_ids > row_ids, raw[-block:], NEG)]
    parts = [part for part in parts if part.shape[0]]
    peak = functools.reduce(jnp.maximum, [over_rows(jnp.max, part) for part in parts])
    total = sum(over_rows(jnp.sum, jnp.exp2((part - peak) * scale)) for part in parts)
    return (peak * scale, total)


def own_kernel(
    block,
    left_in,
    right_in,
    weight_in,
    stacked_out,
    part_out,
    left,
    right,
    weight,
    stacked,
    part,
    line_sems,
    sems,
):
    lines_here, seg_len = left.shape[:2]
    pairs = ((left_in, left), (right_in, right))
    for line in range(lines_here):
        begin_copies(line_copies(pairs, line_sems, line, lines_here))
    fetch, send_stacked, send_part = copies_of(
        ((weight_in, weight), (stacked, stacked_out), (part, part_out)), sems
    )
    fetch.start()

    def one_line(line, carry):
        wait(line_copies(pairs, line_sems, line, lines_here))
        for first in range(0, seg_len, block):
            cols = slice(first, first + block)
            peak, total = column_block(left[line, first:], right[line, cols], True)
            part[pl.ds(line, 1), cols] = peak
            part[pl.ds(lines_here + line, 1), cols] = total
        return carry

    lax.fori_loop(0, lines_here, one_line, 0)
    send_part.start()
    fetch.wait()
    stack_weights(weight, stacked)
    send_stacked.start()
    send_part.wait()
    send_stacked.wait()


def column_cost(lines_here, seg_len, channels):
    return pl.CostEstimate(
        flops=2 * lines_here * seg_len * seg_len * channels,
        bytes_accessed=8 * lines_here * seg_len * channels,
        transcendentals=lines_here * seg_len * seg_len // 2,
    )


def own_partials(left, right, weight):
    lines_here, seg_len, channels = left.shape
    bf16, f32 = jnp.bfloat16, jnp.float32
    stacked = ((weight.shape[0], 12 * channels, 2 * channels), bf16)
    part = ((2 * lines_here, seg_len), f32)
    return kernel_call(
        functools.partial(own_kernel, min(256, seg_len)),
        (left, right, weight),
        (stacked, part),
        ((left.shape, bf16), (right.shape, bf16), (weight.shape, bf16), stacked, part),
        (2 * lines_here, 3),
        "column_own",
        column_cost(*left.shape),
    )


def next_kernel(
    block,
    next_in,
    right_in,
    own_in,
    back_in,
    merged_out,
    first_out,
    second_out,
    following,
    right,
    merged,
    back,
    first_part,
    second_part,
    line_sems,
    sems,
):
    lines_here, half = following.shape[:2]
    pairs = ((next_in, following), (right_in.at[:, pl.ds(0, half)], right))
    fetches = copies_of(((own_in, merged), (back_in, back)), sems)
    sends = copies_of(
        ((first_part, first_out), (second_part, second_out), (merged, merged_out)),
        sems.at[pl.ds(2, 3)],
    )
    begin_copies(fetches)
    for line in range(lines_here):
        begin_copies(line_copies(pairs, line_sems, line, lines_here))
    wait(fetches)
    last = lax.axis_index("seg") == lax.axis_size("seg") - 1

    def one_line(line, carry):
        wait(line_copies(pairs, line_sems, line, lines_here))
        top, bottom = pl.ds(line, 1), pl.ds(lines_here + line, 1)
        for first in range(0, half, block):
            cols = slice(first, first + block)
            peak, total = column_block(following[line, : first + block], right[line, cols], False)
            peak = jnp.where(last, NEG, peak)
            total = jnp.where(last, 0.0, total)
            own_peak = merged[top, cols]
            joint = jnp.maximum(own_peak, peak)
            merged[bottom, cols] = merged[bottom, cols] * jnp.exp2(
                own_peak - joint
            ) + total * jnp.exp2(peak - joint)
            merged[top, cols] = joint
        return carry

    lax.fori_loop(0, lines_here, one_line, 0)
    first_part[...], second_part[...] = by_parity(merged[...], back[...])
    begin_copies(sends)
    wait(sends)


def next_partials(next_low, right, own, back):
    lines_here, half, channels = next_low.shape
    part = (own.shape, jnp.float32)
    features = (next_low.shape, jnp.bfloat16)
    return kernel_call(
        functools.partial(next_kernel, min(256, half)),
        (next_low, right, own, back),
        (part,) * 3,
        (features, features) + (part,) * 4,
        (2 * lines_here, 5),
        "column_next",
        column_cost(lines_here, half, channels),
    )


def cross_kernel(block, left_in, prev_in, back_out, left, prev, back, line_sems, sems):
    lines_here, seg_len = left.shape[:2]
    half = seg_len - prev.shape[1]
    pairs = ((left_in, left), (prev_in, prev))
    for line in range(lines_here):
        begin_copies(line_copies(pairs, line_sems, line, lines_here))
    (send,) = copies_of(((back, back_out),), sems)
    back[...] = jnp.zeros_like(back)

    def one_line(line, carry):
        wait(line_copies(pairs, line_sems, line, lines_here))
        top, bottom = pl.ds(line, 1), pl.ds(lines_here + line, 1)
        for first in range(0, prev.shape[1], block):
            cols = slice(first, first + block)
            peak, total = column_block(
                left[line, : half + first + block], prev[line, cols], False
            )
            back[top, cols] = peak
            back[bottom, cols] = total
        return carry

    lax.fori_loop(0, lines_here, one_line, 0)
    send.start()
    send.wait()


def cross_partials(left, prev_high):
    lines_here, seg_len, channels = left.shape
    part = ((2 * lines_here, seg_len), jnp.float32)
    return kernel_call(
        functools.partial(cross_kernel, min(256, prev_high.shape[1])),
        (left, prev_high),
        (part,),
        ((left.shape, jnp.bfloat16), (prev_high.shape, jnp.bfloat16), part),
        (2 * lines_here, 1),
        "column_cross",
        column_cost(*left.shape),
    )[0]


def potential(peak, total):
    return -(peak + jnp.log2(total))


def merged_potential(first, second):
    first_max = jnp.where(first[1] > 0, first[0], NEG)
    second_max = jnp.where(second[1] > 0, second[0], NEG)
    peak = jnp.maximum(first_max, second_max)
    total = first[1] * jnp.exp2(first_max - peak) + second[1] * jnp.exp2(second_max - peak)
    return potential(peak, total)


def split(values, parts):
    pieces = []
    for _ in range(parts):
        piece = values.astype(jnp.bfloat16).astype(jnp.float32)
        pieces.append(piece)
        values = values - piece
    return pieces


SHIFT = 2


def potential_lanes(pot, channels):
    lines_here, count = pot.shape
    parts = split(pot, 3)
    filler = jnp.zeros((channels - 3 * lines_here, count), jnp.float32)
    lanes = jnp.concatenate(parts + [filler], axis=0).T
    lane = lax.broadcasted_iota(jnp.int32, lanes.shape, 1)
    return jnp.where(lane >= channels - SHIFT, -1.0, lanes).astype(jnp.bfloat16)


def line_lanes(line, lines_here, shape):
    lane = lax.broadcasted_iota(jnp.int32, shape, 1)
    mine = jnp.zeros(shape, jnp.float32)
    for part in range(3):
        mine = jnp.where(lane == part * lines_here + line, 1.0, mine)
    return mine


def banded(values, row, block):
    rows, window = values.shape
    col_ids = lax.broadcasted_iota(jnp.int32, (rows, block), 1)
    row_ids = lax.broadcasted_iota(jnp.int32, (rows, block), 0) + row
    return jnp.concatenate(
        [
            jnp.where(col_ids > row_ids, values[:, :block], NEG),
            values[:, block : window - block],
            jnp.where(col_ids <= row_ids, values[:, window - block :], NEG),
        ],
        axis=1,
    )


def feature_pairs(left_in, right_in, prev_low_in, prev_high_in, left, ext):
    seg_len, half = left.shape[1], prev_low_in.shape[1]
    return (
        (left_in, left),
        (prev_low_in, ext.at[:, pl.ds(0, half)]),
        (prev_high_in, ext.at[:, pl.ds(half, seg_len - half)]),
        (right_in, ext.at[:, pl.ds(seg_len, seg_len)]),
    )


def row_kernel(
    block,
    left_in,
    right_in,
    prev_low_in,
    prev_high_in,
    own_in,
    back_in,
    first_in,
    second_in,
    pot_out,
    lanes_out,
    own_out,
    prev_out,
    first_out,
    second_out,
    left,
    ext,
    own,
    back,
    first_part,
    second_part,
    pot,
    lanes,
    own_sum,
    prev_sum,
    first_sum,
    second_sum,
    pot_lanes,
    sums,
    raw,
    line_sems,
    sems,
    lane_sems,
):
    lines_here, seg_len, channels = left.shape
    half = prev_low_in.shape[1]
    scale = log2_scale(channels)
    fetches = copies_of(
        ((own_in, own), (back_in, back), (first_in, first_part), (second_in, second_part)), sems
    )
    begin_copies(fetches)
    pairs = feature_pairs(left_in, right_in, prev_low_in, prev_high_in, left, ext)
    for line in range(lines_here):
        begin_copies(line_copies(pairs, line_sems, line, lines_here))
    wait(fetches)

    following, before = by_parity(first_part[...], second_part[...])

    def parts(part, first, stop):
        return part[:lines_here, first:stop], part[lines_here:, first:stop]

    rest = seg_len - half
    pot[:, seg_len : seg_len + half] = potential(*parts(own, 0, half))
    pot[:, seg_len + half :] = merged_potential(
        parts(own, half, seg_len), parts(following, 0, rest)
    )
    low = parts(before, 0, half)
    high = parts(before, half, seg_len)
    pot[:, :half] = jnp.where(low[1] > 0, potential(*low), NEG)
    pot[:, half:seg_len] = jnp.where(
        high[1] > 0, merged_potential(high, parts(back, 0, rest)), NEG
    )
    pot_lanes[...] = potential_lanes(pot[...] * (1.0 / scale), channels)
    window = seg_len + block
    big = 2 * block
    steps = seg_len // big
    strip = 16
    lane = lax.broadcasted_iota(jnp.int32, (strip, channels), 1)

    def one_line(line, carry):
        wait(line_copies(pairs, line_sems, line, lines_here))
        sums[...] = jnp.zeros_like(sums)
        mine = line_lanes(line, lines_here, (big, channels)).astype(jnp.bfloat16)
        strip_lanes = line_lanes(line, lines_here, (strip, channels))

        def score(index):
            first = index * big
            reach = slice(first, first + seg_len + big)
            raw[index % 2] = scores_of(
                jnp.concatenate([left[line, first : first + big], mine], axis=1),
                jnp.concatenate([ext[line, reach], pot_lanes[reach]], axis=1),
            )

        score(0)
        for index in range(steps):
            slot = index % 2
            if index + 1 < steps:
                score(index + 1)
            for side in range(2):
                shift = side * block
                first = index * big + shift
                column_sum = jnp.zeros((8, window), jnp.float32)
                for row in range(0, block, strip):
                    rows = slice(shift + row, shift + row + strip)
                    logits = banded(raw[slot, rows, shift : shift + window], row, block)
                    peak = jnp.max(logits, axis=1, keepdims=True)
                    terms = jnp.exp2((logits - peak) * scale)
                    plan = terms * (1.0 / jnp.sum(terms, axis=1, keepdims=True))
                    column_sum += plan[:8] + plan[8:]
                    marked = strip_lanes
                    for part, piece in enumerate(split(peak, SHIFT)):
                        marked = jnp.where(lane == channels - SHIFT + part, piece, marked)
                    lanes[line, first + row : first + row + strip] = marked.astype(jnp.bfloat16)
                sums[:, first : first + window] += column_sum
        totals = jnp.sum(sums[...], axis=0, keepdims=True)
        begin_copies(line_copies(((lanes, lanes_out),), lane_sems, line, lines_here))
        prev_sum[pl.ds(line, 1), :] = totals[:, :seg_len]
        own_sum[pl.ds(line, 1), :] = totals[:, seg_len:]
        return carry

    lax.fori_loop(0, lines_here, one_line, 0)
    first_sum[...], second_sum[...] = by_parity(own_sum[...], prev_sum[...])
    sends = copies_of(
        (
            (first_sum, first_out),
            (second_sum, second_out),
            (own_sum, own_out),
            (prev_sum, prev_out),
            (pot, pot_out),
        ),
        sems,
    )
    begin_copies(sends)
    wait(sends)
    for line in range(lines_here):
        wait(line_copies(((lanes, lanes_out),), lane_sems, line, lines_here))


def row_pass(left, right, prev_low, prev_high, own, back, first, second, block):
    lines_here, seg_len, channels = left.shape
    bf16, f32 = jnp.bfloat16, jnp.float32
    part = (own.shape, f32)
    marginal = ((lines_here, seg_len), f32)
    pot = ((lines_here, 2 * seg_len), f32)
    lanes = (left.shape, bf16)
    return kernel_call(
        functools.partial(row_kernel, block),
        (left, right, prev_low, prev_high, own, back, first, second),
        (pot, lanes) + (marginal,) * 4,
        ((left.shape, bf16), ((lines_here, 2 * seg_len, channels), bf16))
        + (part,) * 4
        + (pot, lanes)
        + (marginal,) * 4
        + (
            ((2 * seg_len, channels), bf16),
            ((8, 2 * seg_len), f32),
            ((2, 2 * block, seg_len + 2 * block), f32),
        ),
        (4 * lines_here, 5, lines_here),
        "row_pass",
    )


def transport_kernel(
    block,
    pot_in,
    lanes_in,
    left_in,
    right_in,
    prev_low_in,
    prev_high_in,
    own_in,
    back_in,
    first_in,
    second_in,
    state_out,
    disp_out,
    first_out,
    last_out,
    first_px_out,
    second_px_out,
    pot,
    lanes,
    left,
    ext,
    own,
    back,
    first_part,
    second_part,
    state,
    disp,
    first_px,
    second_px,
    pot_lanes,
    marks,
    raw,
    weights,
    line_sems,
    sems,
    send_sems,
):
    lines_here, seg_len, channels = left.shape
    layers = first_out.shape[0]
    scale = log2_scale(channels)
    big = 2 * block
    window = seg_len + big
    fetches = copies_of(
        (
            (pot_in, pot),
            (own_in, own),
            (back_in, back),
            (first_in, first_part),
            (second_in, second_part),
        ),
        sems,
    )
    begin_copies(fetches)
    pairs = feature_pairs(left_in, right_in, prev_low_in, prev_high_in, left, ext) + (
        (lanes_in, lanes),
    )
    for line in range(lines_here):
        begin_copies(line_copies(pairs, line_sems, line, lines_here))
    lane = lax.broadcasted_iota(jnp.int32, (window, channels), 1)
    distance = seg_len - lax.broadcasted_iota(jnp.int32, (window, channels), 0)
    fine = jnp.bitwise_and(distance, 15)
    values = jnp.where(
        lane == 0,
        1,
        jnp.where(lane == 1, distance - fine, jnp.where(lane == 2, fine, 0)),
    )
    marks[...] = values.astype(jnp.float32).astype(jnp.bfloat16)
    wait(fetches)
    following, before = by_parity(first_part[...], second_part[...])
    total = jnp.concatenate([before + back[...], own[...] + following], axis=1)
    final = jnp.where(total > 0, pot[...] - jnp.log2(total), NEG)
    pot_lanes[...] = potential_lanes(final * (1.0 / scale), channels)
    offsets = lax.broadcasted_iota(jnp.int32, (1, big), 1).astype(jnp.float32)
    corner = jnp.zeros((block, block), jnp.bfloat16)
    steps = seg_len // big

    def one_line(line, carry):
        wait(line_copies(pairs, line_sems, line, lines_here))

        def score(index):
            first = index * big
            rows, reach = slice(first, first + big), slice(first, first + window)
            raw[index % 2] = scores_of(
                jnp.concatenate([left[line, rows], lanes[line, rows]], axis=1),
                jnp.concatenate([ext[line, reach], pot_lanes[reach]], axis=1),
            )

        def weigh(index):
            slot = index % 2
            upper = jnp.exp2(banded(raw[slot, :block, : window - block], 0, block) * scale)
            lower = jnp.exp2(banded(raw[slot, block:, block:], 0, block) * scale)
            weights[slot, :block, : window - block] = upper.astype(jnp.bfloat16)
            weights[slot, :block, window - block :] = corner
            weights[slot, block:, block:] = lower.astype(jnp.bfloat16)
            weights[slot, block:, :block] = corner

        def gather(index):
            first = index * big
            rows = slice(first, first + big)
            table = jnp.concatenate([ext[line, first : first + window], marks[...]], axis=1)
            result = jnp.dot(weights[index % 2], table, preferred_element_type=jnp.float32)
            matched = result[:, :channels] * (1.0 / result[:, channels : channels + 1])
            state[line, rows] = (matched - left[line, rows].astype(jnp.float32)).astype(
                state.dtype
            )
            moments = result[:, channels:].T
            return offsets + (moments[1:2] + moments[2:3]) / moments[0:1]

        disparity = []
        for index in range(steps + 2):
            if index < steps:
                score(index)
            if index >= 2:
                disparity.append(gather(index - 2))
            if 1 <= index <= steps:
                weigh(index - 1)
        disp[pl.ds(line, 1), :] = jnp.concatenate(disparity, axis=1)
        begin_copies(line_copies(((state, state_out),), send_sems, line, lines_here))
        high = state[line, seg_len - EDGE :].astype(jnp.float32)
        first, second = by_parity(high, state[line, :EDGE].astype(jnp.float32))
        first_px[line] = first.astype(jnp.bfloat16)
        second_px[line] = second.astype(jnp.bfloat16)

        @pl.when(line < layers)
        def _():
            pltpu.make_async_copy(state.at[line], first_out.at[line], sems.at[line]).start()

        @pl.when(line >= lines_here - layers)
        def _():
            target = line - (lines_here - layers)
            pltpu.make_async_copy(
                state.at[line], last_out.at[target], sems.at[layers + target]
            ).start()

        return carry

    lax.fori_loop(0, lines_here, one_line, 0)
    sends = copies_of(
        ((first_px, first_px_out), (second_px, second_px_out), (disp, disp_out)),
        send_sems.at[pl.ds(lines_here, 3)],
    )
    begin_copies(sends)
    for line in range(layers):
        pltpu.make_async_copy(state.at[line], first_out.at[line], sems.at[line]).wait()
        source = line + lines_here - layers
        pltpu.make_async_copy(state.at[source], last_out.at[line], sems.at[layers + line]).wait()
    for line in range(lines_here):
        wait(line_copies(((state, state_out),), send_sems, line, lines_here))
    wait(sends)


def transport(pot, lanes, left, right, prev_low, prev_high, own, back, first, second, block, layers):
    lines_here, seg_len, channels = left.shape
    bf16, f32 = jnp.bfloat16, jnp.float32
    edge = ((layers, seg_len, channels), bf16)
    side = ((lines_here, EDGE, channels), bf16)
    state = (left.shape, bf16)
    marginal = ((lines_here, seg_len), f32)
    window = seg_len + 2 * block
    return kernel_call(
        functools.partial(transport_kernel, block),
        (pot, lanes, left, right, prev_low, prev_high, own, back, first, second),
        (state, marginal, edge, edge, side, side),
        ((pot.shape, f32), (lanes.shape, bf16), state)
        + (((lines_here, 2 * seg_len, channels), bf16),)
        + (marginal,) * 4
        + (state, marginal, side, side)
        + (
            ((2 * seg_len, channels), bf16),
            ((window, channels), bf16),
            ((2, 2 * block, window), f32),
            ((2, 2 * block, window), bf16),
        ),
        (5 * lines_here, max(5, 2 * layers), lines_here + 3),
        "transport",
    )


def stack_weights(weight_ref, stacked_ref):
    layers, taps, _, channels, _ = weight_ref.shape
    zeros = jnp.zeros((channels, channels), stacked_ref.dtype)
    for layer in range(layers):
        for col_tap in range(taps):
            for line in range(taps + 1):
                row = (col_tap * (taps + 1) + line) * channels
                for out in range(2):
                    row_tap = line - out
                    stacked_ref[
                        layer, row : row + channels, out * channels : (out + 1) * channels
                    ] = weight_ref[layer, row_tap, col_tap] if 0 <= row_tap < taps else zeros


def conv_kernel(
    state_in,
    top_in,
    bottom_in,
    first_in,
    second_in,
    corner_top_in,
    corner_bottom_in,
    weight_in,
    bias_in,
    result_out,
    state_ref,
    top_ref,
    bottom_ref,
    first_ref,
    second_ref,
    corner_top_ref,
    corner_bottom_ref,
    weight_ref,
    bias_ref,
    out_ref,
    first_image,
    second_image,
    sems,
    send_sems,
):
    fetches = copies_of(
        (
            (state_in, state_ref),
            (first_in, first_ref),
            (second_in, second_ref),
            (corner_top_in, corner_top_ref),
            (corner_bottom_in, corner_bottom_ref),
            (top_in, top_ref),
            (bottom_in, bottom_ref),
            (weight_in, weight_ref),
            (bias_in, bias_ref),
        ),
        sems,
    )
    begin_copies(fetches)
    lines_here, seg_len, channels = state_ref.shape
    layers = weight_ref.shape[0]
    after = layers + lines_here
    right = EDGE + seg_len
    f32 = jnp.float32
    wait(fetches[:1])
    first_image[layers:after, EDGE:right] = state_ref[...].astype(f32)
    wait(fetches[1:-2])
    first_image[:layers, EDGE:right] = top_ref[...].astype(f32)
    first_image[after:, EDGE:right] = bottom_ref[...].astype(f32)
    for rows, first_px, second_px in (
        (slice(layers, after), first_ref[...], second_ref[...]),
        (slice(0, layers), corner_top_ref[:, :EDGE], corner_top_ref[:, EDGE:]),
        (slice(after, None), corner_bottom_ref[:, :EDGE], corner_bottom_ref[:, EDGE:]),
    ):
        following, before = by_parity(first_px.astype(f32), second_px.astype(f32))
        first_image[rows, :EDGE] = before
        first_image[rows, right:] = following
    wait(fetches[-2:])
    line0 = lax.axis_index("lines") * lines_here - layers
    all_lines = lax.axis_size("lines") * lines_here
    px0 = lax.axis_index("seg") * seg_len - EDGE
    all_px = lax.axis_size("seg") * seg_len
    source, target = first_image, second_image
    for layer in range(layers):
        reach = layers - 1 - layer
        begin, end = (EDGE // 2, right + EDGE // 2) if reach else (EDGE, right)
        middle = begin + seg_len // 2
        pieces = ((begin, middle), (middle, end))

        def pair(index, carry, layer=layer, reach=reach, pieces=pieces, source=source, target=target):
            base = layer + 2 * index
            for start, stop in pieces:
                size = stop - start
                taps = [
                    source[base + line, start + col_tap - 1 : start + col_tap - 1 + size].astype(jnp.bfloat16)
                    for col_tap in range(3)
                    for line in range(4)
                ]
                total = jnp.dot(
                    jnp.concatenate(taps, axis=1), weight_ref[layer], preferred_element_type=f32
                )
                for out in range(2):
                    line = base + 1 + out
                    part = total[:, out * channels : (out + 1) * channels] + bias_ref[layer : layer + 1]
                    updated = source[line, start : start + size] + jnp.maximum(part, 0.0)
                    if not reach:
                        out_ref[line - layers, start - EDGE : start - EDGE + size] = updated.astype(out_ref.dtype)
                        continue
                    image_line = line0 + line
                    inside = (image_line >= 0) & (image_line < all_lines)
                    if reach:
                        px = px0 + start + lax.broadcasted_iota(jnp.int32, updated.shape, 0)
                        inside = inside & (px >= 0) & (px < all_px)
                    updated = jnp.where(inside, updated, 0.0)
                    target[line, start : start + size] = updated.astype(jnp.bfloat16).astype(f32)
            if not reach:
                for line in (base + 1, base + 2):
                    begin_copies(line_copies(((out_ref, result_out),), send_sems, line - layers, lines_here))
            return carry

        lax.fori_loop(0, (lines_here + 2 * reach) // 2, pair, 0, unroll=True)
        source, target = target, source
    for line in range(lines_here):
        wait(line_copies(((out_ref, result_out),), send_sems, line, lines_here))


def conv_layers(state, top, bottom, left_px, right_px, corners_top, corners_bottom, weight, bias):
    layers = weight.shape[0]
    lines_here, seg_len, channels = state.shape
    image = ((lines_here + 2 * layers, seg_len + 2 * EDGE, channels), jnp.float32)
    operands = (state, top, bottom, left_px, right_px, corners_top, corners_bottom, weight, bias)
    result = (state.shape, state.dtype)
    return kernel_call(
        conv_kernel,
        operands,
        (result,),
        tuple((operand.shape, operand.dtype) for operand in operands) + (result, image, image),
        (len(operands), lines_here),
        "conv_layers",
    )[0]


def shards(left_features, right_features, conv_weight, conv_bias):
    seg_len = left_features.shape[1]
    half = seg_len // 2
    layers = conv_weight.shape[0]
    prev_high = shifted(right_features[:, half:], "seg", 1)
    next_low = shifted(left_features[:, :half], "seg", -1)
    stacked, own = own_partials(left_features, right_features, conv_weight)
    right_later, own = lax.optimization_barrier((right_features, own))
    prev_low = shifted(right_later[:, :half], "seg", 1)
    back = cross_partials(left_features, prev_high)
    own, first, second = next_partials(next_low, right_features, own, back)
    first = exchanged(first, "seg", 0)
    second = exchanged(second, "seg", 1)
    block = min(128, half)
    pot, lanes, own, back, first, second = row_pass(
        left_features, right_features, prev_low, prev_high, own, back, first, second, block
    )
    first = exchanged(first, "seg", 0)
    second = exchanged(second, "seg", 1)
    state, disparity, first_lines, last_lines, first, second = transport(
        pot, lanes, left_features, right_features, prev_low, prev_high, own, back, first, second, block, layers
    )
    bottom = shifted(first_lines, "lines", -1)
    top = shifted(last_lines, "lines", 1)
    first = exchanged(first, "seg", 0)
    second = exchanged(second, "seg", 1)
    edges = jnp.concatenate([first, second], axis=1)
    corners_bottom = shifted(edges[:layers], "lines", -1)
    corners_top = shifted(edges[-layers:], "lines", 1)
    refined = conv_layers(
        state, top, bottom, first, second, corners_top, corners_bottom, stacked, conv_bias
    )
    return (refined, disparity)


def solution(mesh):
    return jax.shard_map(
        shards,
        mesh=mesh,
        in_specs=(P("lines", "seg", None), P("lines", "seg", None), P(), P()),
        out_specs=(P("lines", "seg", None), P("lines", "seg")),
        check_vma=False,
    )
```

```python
import functools
import math

import jax
import jax.numpy as jnp
from jax import lax
from jax.experimental import pallas as pl
from jax.experimental.pallas import tpu as pltpu
from jax.sharding import PartitionSpec as P

DISP = 1024
NEG = -1e30
EDGE = 16
VMEM_BYTES = 32 * 1024 * 1024


def shifted(block, axis, step):
    count = lax.axis_size(axis)
    route = [(i, i + step) for i in range(count) if 0 <= i + step < count]
    return lax.ppermute(block, axis, route)


def exchanged(block, axis, odd):
    route = []
    for low in range(odd, lax.axis_size(axis) - 1, 2):
        route += [(low, low + 1), (low + 1, low)]
    return lax.ppermute(block, axis, route)


def even_segment():
    return lax.rem(lax.axis_index("seg"), 2) == 0


def by_parity(following, previous):
    even = even_segment()
    return jnp.where(even, following, previous), jnp.where(even, previous, following)


def params():
    return pltpu.CompilerParams(vmem_limit_bytes=VMEM_BYTES)


ANYWHERE = pl.BlockSpec(memory_space=pl.ANY)


def kernel_call(kernel, operands, results, scratch, copies, name, cost=None):
    return pl.pallas_call(
        kernel,
        in_specs=[ANYWHERE] * len(operands),
        out_specs=[ANYWHERE] * len(results),
        out_shape=[jax.ShapeDtypeStruct(shape, dtype) for shape, dtype in results],
        scratch_shapes=[pltpu.VMEM(shape, dtype) for shape, dtype in scratch]
        + [pltpu.SemaphoreType.DMA((count,)) for count in copies],
        compiler_params=params(),
        cost_estimate=cost,
        name=name,
    )(*operands)


def copies_of(pairs, sems):
    return [
        pltpu.make_async_copy(source, target, sems.at[index])
        for index, (source, target) in enumerate(pairs)
    ]


def line_copies(pairs, sems, line, lines_here):
    return [
        pltpu.make_async_copy(source.at[line], target.at[line], sems.at[index * lines_here + line])
        for index, (source, target) in enumerate(pairs)
    ]


def begin_copies(copies):
    for copy in copies:
        copy.start()


def wait(copies):
    for copy in copies:
        copy.wait()


def scores_of(left, right):
    return lax.dot_general(
        left, right, (((1,), (1,)), ((), ())), preferred_element_type=jnp.float32
    )


def log2_scale(channels):
    return math.log2(math.e) / math.sqrt(channels)


def over_rows(reduce, values, chains=64):
    count, width = values.shape
    while count > chains >= 8 and count % chains == 0:
        values = reduce(values.reshape(count // chains, chains, width), axis=0)
        count, chains = chains, chains // 8
    return reduce(values, axis=0, keepdims=True)


def column_block(left, right, diagonal_first):
    block, channels = right.shape
    scale = log2_scale(channels)
    raw = scores_of(left, right)
    row_ids = lax.broadcasted_iota(jnp.int32, (block, block), 0)
    col_ids = lax.broadcasted_iota(jnp.int32, (block, block), 1)
    if diagonal_first:
        parts = [jnp.where(col_ids <= row_ids, raw[:block], NEG), raw[block:]]
    else:
        parts = [raw[:-block], jnp.where(col_ids > row_ids, raw[-block:], NEG)]
    parts = [part for part in parts if part.shape[0]]
    peak = functools.reduce(jnp.maximum, [over_rows(jnp.max, part) for part in parts])
    total = sum(over_rows(jnp.sum, jnp.exp2((part - peak) * scale)) for part in parts)
    return (peak * scale, total)


def own_kernel(
    block,
    left_in,
    right_in,
    weight_in,
    stacked_out,
    part_out,
    left,
    right,
    weight,
    stacked,
    part,
    line_sems,
    sems,
):
    lines_here, seg_len = left.shape[:2]
    pairs = ((left_in, left), (right_in, right))
    for line in range(lines_here):
        begin_copies(line_copies(pairs, line_sems, line, lines_here))
    fetch, send_stacked, send_part = copies_of(
        ((weight_in, weight), (stacked, stacked_out), (part, part_out)), sems
    )
    fetch.start()

    def one_line(line, carry):
        wait(line_copies(pairs, line_sems, line, lines_here))
        for first in range(0, seg_len, block):
            cols = slice(first, first + block)
            peak, total = column_block(left[line, first:], right[line, cols], True)
            part[pl.ds(line, 1), cols] = peak
            part[pl.ds(lines_here + line, 1), cols] = total
        return carry

    lax.fori_loop(0, lines_here, one_line, 0)
    send_part.start()
    fetch.wait()
    stack_weights(weight, stacked)
    send_stacked.start()
    send_part.wait()
    send_stacked.wait()


def column_cost(lines_here, seg_len, channels):
    return pl.CostEstimate(
        flops=2 * lines_here * seg_len * seg_len * channels,
        bytes_accessed=8 * lines_here * seg_len * channels,
        transcendentals=lines_here * seg_len * seg_len // 2,
    )


def own_partials(left, right, weight):
    lines_here, seg_len, channels = left.shape
    bf16, f32 = jnp.bfloat16, jnp.float32
    stacked = ((weight.shape[0], 12 * channels, 2 * channels), bf16)
    part = ((2 * lines_here, seg_len), f32)
    return kernel_call(
        functools.partial(own_kernel, min(256, seg_len)),
        (left, right, weight),
        (stacked, part),
        ((left.shape, bf16), (right.shape, bf16), (weight.shape, bf16), stacked, part),
        (2 * lines_here, 3),
        "column_own",
        column_cost(*left.shape),
    )


def next_kernel(
    block,
    next_in,
    right_in,
    own_in,
    back_in,
    merged_out,
    first_out,
    second_out,
    following,
    right,
    merged,
    back,
    first_part,
    second_part,
    line_sems,
    sems,
):
    lines_here, half = following.shape[:2]
    pairs = ((next_in, following), (right_in.at[:, pl.ds(0, half)], right))
    fetches = copies_of(((own_in, merged), (back_in, back)), sems)
    sends = copies_of(
        ((first_part, first_out), (second_part, second_out), (merged, merged_out)),
        sems.at[pl.ds(2, 3)],
    )
    begin_copies(fetches)
    for line in range(lines_here):
        begin_copies(line_copies(pairs, line_sems, line, lines_here))
    wait(fetches)
    last = lax.axis_index("seg") == lax.axis_size("seg") - 1

    def one_line(line, carry):
        wait(line_copies(pairs, line_sems, line, lines_here))
        top, bottom = pl.ds(line, 1), pl.ds(lines_here + line, 1)
        for first in range(0, half, block):
            cols = slice(first, first + block)
            peak, total = column_block(following[line, : first + block], right[line, cols], False)
            peak = jnp.where(last, NEG, peak)
            total = jnp.where(last, 0.0, total)
            own_peak = merged[top, cols]
            joint = jnp.maximum(own_peak, peak)
            merged[bottom, cols] = merged[bottom, cols] * jnp.exp2(
                own_peak - joint
            ) + total * jnp.exp2(peak - joint)
            merged[top, cols] = joint
        return carry

    lax.fori_loop(0, lines_here, one_line, 0, unroll=True)
    first_part[...], second_part[...] = by_parity(merged[...], back[...])
    begin_copies(sends)
    wait(sends)


def next_partials(next_low, right, own, back):
    lines_here, half, channels = next_low.shape
    part = (own.shape, jnp.float32)
    features = (next_low.shape, jnp.bfloat16)
    return kernel_call(
        functools.partial(next_kernel, min(256, half)),
        (next_low, right, own, back),
        (part,) * 3,
        (features, features) + (part,) * 4,
        (2 * lines_here, 5),
        "column_next",
        column_cost(lines_here, half, channels),
    )


def cross_kernel(block, left_in, prev_in, back_out, left, prev, back, line_sems, sems):
    lines_here, seg_len = left.shape[:2]
    half = seg_len - prev.shape[1]
    pairs = ((left_in, left), (prev_in, prev))
    for line in range(lines_here):
        begin_copies(line_copies(pairs, line_sems, line, lines_here))
    (send,) = copies_of(((back, back_out),), sems)
    back[...] = jnp.zeros_like(back)

    def one_line(line, carry):
        wait(line_copies(pairs, line_sems, line, lines_here))
        top, bottom = pl.ds(line, 1), pl.ds(lines_here + line, 1)
        for first in range(0, prev.shape[1], block):
            cols = slice(first, first + block)
            peak, total = column_block(
                left[line, : half + first + block], prev[line, cols], False
            )
            back[top, cols] = peak
            back[bottom, cols] = total
        return carry

    lax.fori_loop(0, lines_here, one_line, 0, unroll=True)
    send.start()
    send.wait()


def cross_partials(left, prev_high):
    lines_here, seg_len, channels = left.shape
    part = ((2 * lines_here, seg_len), jnp.float32)
    return kernel_call(
        functools.partial(cross_kernel, min(256, prev_high.shape[1])),
        (left, prev_high),
        (part,),
        ((left.shape, jnp.bfloat16), (prev_high.shape, jnp.bfloat16), part),
        (2 * lines_here, 1),
        "column_cross",
        column_cost(*left.shape),
    )[0]


def potential(peak, total):
    return -(peak + jnp.log2(total))


def merged_potential(first, second):
    first_max = jnp.where(first[1] > 0, first[0], NEG)
    second_max = jnp.where(second[1] > 0, second[0], NEG)
    peak = jnp.maximum(first_max, second_max)
    total = first[1] * jnp.exp2(first_max - peak) + second[1] * jnp.exp2(second_max - peak)
    return potential(peak, total)


def split(values, parts):
    pieces = []
    for _ in range(parts):
        piece = values.astype(jnp.bfloat16).astype(jnp.float32)
        pieces.append(piece)
        values = values - piece
    return pieces


SHIFT = 2


def potential_lanes(pot, channels):
    lines_here, count = pot.shape
    parts = split(pot, 3)
    filler = jnp.zeros((channels - 3 * lines_here, count), jnp.float32)
    lanes = jnp.concatenate(parts + [filler], axis=0).T
    lane = lax.broadcasted_iota(jnp.int32, lanes.shape, 1)
    return jnp.where(lane >= channels - SHIFT, -1.0, lanes).astype(jnp.bfloat16)


def line_lanes(line, lines_here, shape):
    lane = lax.broadcasted_iota(jnp.int32, shape, 1)
    mine = jnp.zeros(shape, jnp.float32)
    for part in range(3):
        mine = jnp.where(lane == part * lines_here + line, 1.0, mine)
    return mine


def banded(values, row, block):
    rows, window = values.shape
    col_ids = lax.broadcasted_iota(jnp.int32, (rows, block), 1)
    row_ids = lax.broadcasted_iota(jnp.int32, (rows, block), 0) + row
    return jnp.concatenate(
        [
            jnp.where(col_ids > row_ids, values[:, :block], NEG),
            values[:, block : window - block],
            jnp.where(col_ids <= row_ids, values[:, window - block :], NEG),
        ],
        axis=1,
    )


def feature_pairs(left_in, right_in, prev_low_in, prev_high_in, left, ext):
    seg_len, half = left.shape[1], prev_low_in.shape[1]
    return (
        (left_in, left),
        (prev_low_in, ext.at[:, pl.ds(0, half)]),
        (prev_high_in, ext.at[:, pl.ds(half, seg_len - half)]),
        (right_in, ext.at[:, pl.ds(seg_len, seg_len)]),
    )


def row_kernel(
    block,
    left_in,
    right_in,
    prev_low_in,
    prev_high_in,
    own_in,
    back_in,
    first_in,
    second_in,
    pot_out,
    lanes_out,
    own_out,
    prev_out,
    first_out,
    second_out,
    left,
    ext,
    own,
    back,
    first_part,
    second_part,
    pot,
    lanes,
    own_sum,
    prev_sum,
    first_sum,
    second_sum,
    pot_lanes,
    sums,
    raw,
    line_sems,
    sems,
    lane_sems,
):
    lines_here, seg_len, channels = left.shape
    half = prev_low_in.shape[1]
    scale = log2_scale(channels)
    fetches = copies_of(
        ((own_in, own), (back_in, back), (first_in, first_part), (second_in, second_part)), sems
    )
    begin_copies(fetches)
    pairs = feature_pairs(left_in, right_in, prev_low_in, prev_high_in, left, ext)
    for line in range(lines_here):
        begin_copies(line_copies(pairs, line_sems, line, lines_here))
    wait(fetches)

    following, before = by_parity(first_part[...], second_part[...])

    def parts(part, first, stop):
        return part[:lines_here, first:stop], part[lines_here:, first:stop]

    rest = seg_len - half
    pot[:, seg_len : seg_len + half] = potential(*parts(own, 0, half))
    pot[:, seg_len + half :] = merged_potential(
        parts(own, half, seg_len), parts(following, 0, rest)
    )
    low = parts(before, 0, half)
    high = parts(before, half, seg_len)
    pot[:, :half] = jnp.where(low[1] > 0, potential(*low), NEG)
    pot[:, half:seg_len] = jnp.where(
        high[1] > 0, merged_potential(high, parts(back, 0, rest)), NEG
    )
    pot_lanes[...] = potential_lanes(pot[...] * (1.0 / scale), channels)
    window = seg_len + block
    big = 2 * block
    steps = seg_len // big
    strip = 16
    lane = lax.broadcasted_iota(jnp.int32, (strip, channels), 1)

    def one_line(line, carry):
        wait(line_copies(pairs, line_sems, line, lines_here))
        sums[...] = jnp.zeros_like(sums)
        mine = line_lanes(line, lines_here, (big, channels)).astype(jnp.bfloat16)
        strip_lanes = line_lanes(line, lines_here, (strip, channels))

        def score(index):
            first = index * big
            reach = slice(first, first + seg_len + big)
            raw[index % 2] = scores_of(
                jnp.concatenate([left[line, first : first + big], mine], axis=1),
                jnp.concatenate([ext[line, reach], pot_lanes[reach]], axis=1),
            )

        score(0)
        for index in range(steps):
            slot = index % 2
            if index + 1 < steps:
                score(index + 1)
            for side in range(2):
                shift = side * block
                first = index * big + shift
                column_sum = jnp.zeros((8, window), jnp.float32)
                for row in range(0, block, strip):
                    rows = slice(shift + row, shift + row + strip)
                    logits = banded(raw[slot, rows, shift : shift + window], row, block)
                    peak = jnp.max(logits, axis=1, keepdims=True)
                    terms = jnp.exp2((logits - peak) * scale)
                    plan = terms * (1.0 / jnp.sum(terms, axis=1, keepdims=True))
                    column_sum += plan[:8] + plan[8:]
                    marked = strip_lanes
                    for part, piece in enumerate(split(peak, SHIFT)):
                        marked = jnp.where(lane == channels - SHIFT + part, piece, marked)
                    lanes[line, first + row : first + row + strip] = marked.astype(jnp.bfloat16)
                sums[:, first : first + window] += column_sum
        totals = jnp.sum(sums[...], axis=0, keepdims=True)
        begin_copies(line_copies(((lanes, lanes_out),), lane_sems, line, lines_here))
        prev_sum[pl.ds(line, 1), :] = totals[:, :seg_len]
        own_sum[pl.ds(line, 1), :] = totals[:, seg_len:]
        return carry

    lax.fori_loop(0, lines_here, one_line, 0)
    first_sum[...], second_sum[...] = by_parity(own_sum[...], prev_sum[...])
    sends = copies_of(
        (
            (first_sum, first_out),
            (second_sum, second_out),
            (own_sum, own_out),
            (prev_sum, prev_out),
            (pot, pot_out),
        ),
        sems,
    )
    begin_copies(sends)
    wait(sends)
    for line in range(lines_here):
        wait(line_copies(((lanes, lanes_out),), lane_sems, line, lines_here))


def row_pass(left, right, prev_low, prev_high, own, back, first, second, block):
    lines_here, seg_len, channels = left.shape
    bf16, f32 = jnp.bfloat16, jnp.float32
    part = (own.shape, f32)
    marginal = ((lines_here, seg_len), f32)
    pot = ((lines_here, 2 * seg_len), f32)
    lanes = (left.shape, bf16)
    return kernel_call(
        functools.partial(row_kernel, block),
        (left, right, prev_low, prev_high, own, back, first, second),
        (pot, lanes) + (marginal,) * 4,
        ((left.shape, bf16), ((lines_here, 2 * seg_len, channels), bf16))
        + (part,) * 4
        + (pot, lanes)
        + (marginal,) * 4
        + (
            ((2 * seg_len, channels), bf16),
            ((8, 2 * seg_len), f32),
            ((2, 2 * block, seg_len + 2 * block), f32),
        ),
        (4 * lines_here, 5, lines_here),
        "row_pass",
    )


def transport_kernel(
    block,
    pot_in,
    lanes_in,
    left_in,
    right_in,
    prev_low_in,
    prev_high_in,
    own_in,
    back_in,
    first_in,
    second_in,
    state_out,
    disp_out,
    first_out,
    last_out,
    first_px_out,
    second_px_out,
    pot,
    lanes,
    left,
    ext,
    own,
    back,
    first_part,
    second_part,
    state,
    disp,
    first_px,
    second_px,
    pot_lanes,
    marks,
    raw,
    weights,
    line_sems,
    sems,
    send_sems,
):
    lines_here, seg_len, channels = left.shape
    layers = first_out.shape[0]
    scale = log2_scale(channels)
    big = 2 * block
    window = seg_len + big
    fetches = copies_of(
        (
            (pot_in, pot),
            (own_in, own),
            (back_in, back),
            (first_in, first_part),
            (second_in, second_part),
        ),
        sems,
    )
    begin_copies(fetches)
    pairs = feature_pairs(left_in, right_in, prev_low_in, prev_high_in, left, ext) + (
        (lanes_in, lanes),
    )
    for line in range(lines_here):
        begin_copies(line_copies(pairs, line_sems, line, lines_here))
    lane = lax.broadcasted_iota(jnp.int32, (window, channels), 1)
    distance = seg_len - lax.broadcasted_iota(jnp.int32, (window, channels), 0)
    fine = jnp.bitwise_and(distance, 15)
    values = jnp.where(
        lane == 0,
        1,
        jnp.where(lane == 1, distance - fine, jnp.where(lane == 2, fine, 0)),
    )
    marks[...] = values.astype(jnp.float32).astype(jnp.bfloat16)
    wait(fetches)
    following, before = by_parity(first_part[...], second_part[...])
    total = jnp.concatenate([before + back[...], own[...] + following], axis=1)
    final = jnp.where(total > 0, pot[...] - jnp.log2(total), NEG)
    pot_lanes[...] = potential_lanes(final * (1.0 / scale), channels)
    offsets = lax.broadcasted_iota(jnp.int32, (1, big), 1).astype(jnp.float32)
    corner = jnp.zeros((block, block), jnp.bfloat16)
    steps = seg_len // big

    def one_line(line, carry):
        wait(line_copies(pairs, line_sems, line, lines_here))

        def score(index):
            first = index * big
            rows, reach = slice(first, first + big), slice(first, first + window)
            raw[index % 2] = scores_of(
                jnp.concatenate([left[line, rows], lanes[line, rows]], axis=1),
                jnp.concatenate([ext[line, reach], pot_lanes[reach]], axis=1),
            )

        def weigh(index):
            slot = index % 2
            upper = jnp.exp2(banded(raw[slot, :block, : window - block], 0, block) * scale)
            lower = jnp.exp2(banded(raw[slot, block:, block:], 0, block) * scale)
            weights[slot, :block, : window - block] = upper.astype(jnp.bfloat16)
            weights[slot, :block, window - block :] = corner
            weights[slot, block:, block:] = lower.astype(jnp.bfloat16)
            weights[slot, block:, :block] = corner

        def gather(index):
            first = index * big
            rows = slice(first, first + big)
            table = jnp.concatenate([ext[line, first : first + window], marks[...]], axis=1)
            result = jnp.dot(weights[index % 2], table, preferred_element_type=jnp.float32)
            matched = result[:, :channels] * (1.0 / result[:, channels : channels + 1])
            state[line, rows] = (matched - left[line, rows].astype(jnp.float32)).astype(
                state.dtype
            )
            moments = result[:, channels:].T
            return offsets + (moments[1:2] + moments[2:3]) / moments[0:1]

        disparity = []
        for index in range(steps + 2):
            if index < steps:
                score(index)
            if index >= 2:
                disparity.append(gather(index - 2))
            if 1 <= index <= steps:
                weigh(index - 1)
        disp[pl.ds(line, 1), :] = jnp.concatenate(disparity, axis=1)
        begin_copies(line_copies(((state, state_out),), send_sems, line, lines_here))
        high = state[line, seg_len - EDGE :].astype(jnp.float32)
        first, second = by_parity(high, state[line, :EDGE].astype(jnp.float32))
        first_px[line] = first.astype(jnp.bfloat16)
        second_px[line] = second.astype(jnp.bfloat16)

        @pl.when(line < layers)
        def _():
            pltpu.make_async_copy(state.at[line], first_out.at[line], sems.at[line]).start()

        @pl.when(line >= lines_here - layers)
        def _():
            target = line - (lines_here - layers)
            pltpu.make_async_copy(
                state.at[line], last_out.at[target], sems.at[layers + target]
            ).start()

        return carry

    lax.fori_loop(0, lines_here, one_line, 0)
    sends = copies_of(
        ((first_px, first_px_out), (second_px, second_px_out), (disp, disp_out)),
        send_sems.at[pl.ds(lines_here, 3)],
    )
    begin_copies(sends)
    for line in range(layers):
        pltpu.make_async_copy(state.at[line], first_out.at[line], sems.at[line]).wait()
        source = line + lines_here - layers
        pltpu.make_async_copy(state.at[source], last_out.at[line], sems.at[layers + line]).wait()
    for line in range(lines_here):
        wait(line_copies(((state, state_out),), send_sems, line, lines_here))
    wait(sends)


def transport(pot, lanes, left, right, prev_low, prev_high, own, back, first, second, block, layers):
    lines_here, seg_len, channels = left.shape
    bf16, f32 = jnp.bfloat16, jnp.float32
    edge = ((layers, seg_len, channels), bf16)
    side = ((lines_here, EDGE, channels), bf16)
    state = (left.shape, bf16)
    marginal = ((lines_here, seg_len), f32)
    window = seg_len + 2 * block
    return kernel_call(
        functools.partial(transport_kernel, block),
        (pot, lanes, left, right, prev_low, prev_high, own, back, first, second),
        (state, marginal, edge, edge, side, side),
        ((pot.shape, f32), (lanes.shape, bf16), state)
        + (((lines_here, 2 * seg_len, channels), bf16),)
        + (marginal,) * 4
        + (state, marginal, side, side)
        + (
            ((2 * seg_len, channels), bf16),
            ((window, channels), bf16),
            ((2, 2 * block, window), f32),
            ((2, 2 * block, window), bf16),
        ),
        (5 * lines_here, max(5, 2 * layers), lines_here + 3),
        "transport",
    )


def stack_weights(weight_ref, stacked_ref):
    layers, taps, _, channels, _ = weight_ref.shape
    zeros = jnp.zeros((channels, channels), stacked_ref.dtype)
    for layer in range(layers):
        for col_tap in range(taps):
            for line in range(taps + 1):
                row = (col_tap * (taps + 1) + line) * channels
                for out in range(2):
                    row_tap = line - out
                    stacked_ref[
                        layer, row : row + channels, out * channels : (out + 1) * channels
                    ] = weight_ref[layer, row_tap, col_tap] if 0 <= row_tap < taps else zeros


def conv_kernel(
    state_in,
    top_in,
    bottom_in,
    first_in,
    second_in,
    corner_top_in,
    corner_bottom_in,
    weight_in,
    bias_in,
    result_out,
    state_ref,
    top_ref,
    bottom_ref,
    first_ref,
    second_ref,
    corner_top_ref,
    corner_bottom_ref,
    weight_ref,
    bias_ref,
    out_ref,
    first_image,
    second_image,
    sems,
    send_sems,
):
    fetches = copies_of(
        (
            (state_in, state_ref),
            (first_in, first_ref),
            (second_in, second_ref),
            (corner_top_in, corner_top_ref),
            (corner_bottom_in, corner_bottom_ref),
            (top_in, top_ref),
            (bottom_in, bottom_ref),
            (weight_in, weight_ref),
            (bias_in, bias_ref),
        ),
        sems,
    )
    begin_copies(fetches)
    lines_here, seg_len, channels = state_ref.shape
    layers = weight_ref.shape[0]
    after = layers + lines_here
    right = EDGE + seg_len
    f32 = jnp.float32
    wait(fetches[:1])
    first_image[layers:after, EDGE:right] = state_ref[...].astype(f32)
    wait(fetches[1:-2])
    first_image[:layers, EDGE:right] = top_ref[...].astype(f32)
    first_image[after:, EDGE:right] = bottom_ref[...].astype(f32)
    for rows, first_px, second_px in (
        (slice(layers, after), first_ref[...], second_ref[...]),
        (slice(0, layers), corner_top_ref[:, :EDGE], corner_top_ref[:, EDGE:]),
        (slice(after, None), corner_bottom_ref[:, :EDGE], corner_bottom_ref[:, EDGE:]),
    ):
        following, before = by_parity(first_px.astype(f32), second_px.astype(f32))
        first_image[rows, :EDGE] = before
        first_image[rows, right:] = following
    wait(fetches[-2:])
    line0 = lax.axis_index("lines") * lines_here - layers
    all_lines = lax.axis_size("lines") * lines_here
    px0 = lax.axis_index("seg") * seg_len - EDGE
    all_px = lax.axis_size("seg") * seg_len
    source, target = first_image, second_image
    for layer in range(layers):
        reach = layers - 1 - layer
        begin, end = (EDGE // 2, right + EDGE // 2) if reach else (EDGE, right)
        middle = begin + seg_len // 2
        pieces = ((begin, middle), (middle, end))

        def pair(index, carry, layer=layer, reach=reach, pieces=pieces, source=source, target=target):
            base = layer + 2 * index
            for start, stop in pieces:
                size = stop - start
                taps = [
                    source[base + line, start + col_tap - 1 : start + col_tap - 1 + size].astype(jnp.bfloat16)
                    for col_tap in range(3)
                    for line in range(4)
                ]
                total = jnp.dot(
                    jnp.concatenate(taps, axis=1), weight_ref[layer], preferred_element_type=f32
                )
                for out in range(2):
                    line = base + 1 + out
                    part = total[:, out * channels : (out + 1) * channels] + bias_ref[layer : layer + 1]
                    updated = source[line, start : start + size] + jnp.maximum(part, 0.0)
                    if not reach:
                        out_ref[line - layers, start - EDGE : start - EDGE + size] = updated.astype(out_ref.dtype)
                        continue
                    image_line = line0 + line
                    inside = (image_line >= 0) & (image_line < all_lines)
                    if reach:
                        px = px0 + start + lax.broadcasted_iota(jnp.int32, updated.shape, 0)
                        inside = inside & (px >= 0) & (px < all_px)
                    updated = jnp.where(inside, updated, 0.0)
                    target[line, start : start + size] = updated.astype(jnp.bfloat16).astype(f32)
            if not reach:
                for line in (base + 1, base + 2):
                    begin_copies(line_copies(((out_ref, result_out),), send_sems, line - layers, lines_here))
            return carry

        lax.fori_loop(0, (lines_here + 2 * reach) // 2, pair, 0, unroll=True)
        source, target = target, source
    for line in range(lines_here):
        wait(line_copies(((out_ref, result_out),), send_sems, line, lines_here))


def conv_layers(state, top, bottom, left_px, right_px, corners_top, corners_bottom, weight, bias):
    layers = weight.shape[0]
    lines_here, seg_len, channels = state.shape
    image = ((lines_here + 2 * layers, seg_len + 2 * EDGE, channels), jnp.float32)
    operands = (state, top, bottom, left_px, right_px, corners_top, corners_bottom, weight, bias)
    result = (state.shape, state.dtype)
    return kernel_call(
        conv_kernel,
        operands,
        (result,),
        tuple((operand.shape, operand.dtype) for operand in operands) + (result, image, image),
        (len(operands), lines_here),
        "conv_layers",
    )[0]


def shards(left_features, right_features, conv_weight, conv_bias):
    seg_len = left_features.shape[1]
    half = seg_len // 2
    layers = conv_weight.shape[0]
    prev_high = shifted(right_features[:, half:], "seg", 1)
    next_low = shifted(left_features[:, :half], "seg", -1)
    stacked, own = own_partials(left_features, right_features, conv_weight)
    right_low, own = lax.optimization_barrier((right_features[:, :half], own))
    prev_low = shifted(right_low, "seg", 1)
    back = cross_partials(left_features, prev_high)
    own, first, second = next_partials(next_low, right_features, own, back)
    first = exchanged(first, "seg", 0)
    second = exchanged(second, "seg", 1)
    block = min(128, half)
    pot, lanes, own, back, first, second = row_pass(
        left_features, right_features, prev_low, prev_high, own, back, first, second, block
    )
    first = exchanged(first, "seg", 0)
    second = exchanged(second, "seg", 1)
    state, disparity, first_lines, last_lines, first, second = transport(
        pot, lanes, left_features, right_features, prev_low, prev_high, own, back, first, second, block, layers
    )
    bottom = shifted(first_lines, "lines", -1)
    top = shifted(last_lines, "lines", 1)
    first = exchanged(first, "seg", 0)
    second = exchanged(second, "seg", 1)
    edges = jnp.concatenate([first, second], axis=1)
    corners_bottom = shifted(edges[:layers], "lines", -1)
    corners_top = shifted(edges[-layers:], "lines", 1)
    refined = conv_layers(
        state, top, bottom, first, second, corners_top, corners_bottom, stacked, conv_bias
    )
    return (refined, disparity)


def solution(mesh):
    return jax.shard_map(
        shards,
        mesh=mesh,
        in_specs=(P("lines", "seg", None), P("lines", "seg", None), P(), P()),
        out_specs=(P("lines", "seg", None), P("lines", "seg")),
        check_vma=False,
    )
```
